128 devices in a mesh: tensor: 8 (over x, core), dp: 16 (over y, z).
Axes of the slice: x: 4, y: 4, z: 4, core: 2. Of those that a mesh axis runs over, the one named last changes fastest.
Arguments:
- tokens: bfloat16 [16384, 2048], P('dp'), may hold values from -6 to 6
- cotangent: bfloat16 [16384, 2048], P('dp'), may hold values from -6 to 6
- lengths: int32 [16, 4], P('dp'), may hold values from 1 to 512, 1024 in all within a row
- exits: int32 [16384], P('dp'), may hold values from 0 to 23, as said below
- w_query: bfloat16 [2048, 2048], P(None, 'tensor'), may hold values from -0.125 to 0.125
- b_query: bfloat16 [2048], P('tensor'), may hold values from -3 to 3
- w_key: bfloat16 [2048, 2048], P(None, 'tensor'), may hold values from -0.125 to 0.125
- w_value: bfloat16 [2048, 2048], P(None, 'tensor'), may hold values from -0.125 to 0.125
- b_value: bfloat16 [2048], P('tensor'), may hold values from -3 to 3
- w_out: bfloat16 [2048, 2048], P('tensor'), may hold values from -0.5 to 0.5
- b_out: bfloat16 [2048], replicated, may hold values from -2 to 2
- gain_one: bfloat16 [2048], replicated, may hold values from 0.5 to 1.5
- shift_one: bfloat16 [2048], replicated, may hold values from -2 to 2
- gain_two: bfloat16 [2048], replicated, may hold values from 0.5 to 1.5
- shift_two: bfloat16 [2048], replicated, may hold values from -2 to 2
- w_up: bfloat16 [2048, 8192], P(None, 'tensor'), may hold values from -0.125 to 0.125
- b_up: bfloat16 [8192], P('tensor'), may hold values from -3 to 3
- w_down: bfloat16 [8192, 2048], P('tensor'), may hold values from -0.0625 to 0.0625
- b_down: bfloat16 [2048], replicated, may hold values from -2 to 2
Outputs:
- output: bfloat16 [16384, 2048], P('dp')
- input_grad: bfloat16 [16384, 2048], P('dp')
- grad_w_query: float32 [2048, 2048], P('dp', 'tensor')
- grad_b_query: float32 [2048], P(('tensor', 'dp'))
- grad_w_key: float32 [2048, 2048], P('dp', 'tensor')
- grad_w_value: float32 [2048, 2048], P('dp', 'tensor')
- grad_b_value: float32 [2048], P(('tensor', 'dp'))
- grad_w_out: float32 [2048, 2048], P('tensor', 'dp')
- grad_b_out: float32 [2048], P('dp')
- grad_gain_one: float32 [2048], P('dp')
- grad_shift_one: float32 [2048], P('dp')
- grad_gain_two: float32 [2048], P('dp')
- grad_shift_two: float32 [2048], P('dp')
- grad_w_up: float32 [2048, 8192], P('dp', 'tensor')
- grad_b_up: float32 [8192], P(('tensor', 'dp'))
- grad_w_down: float32 [8192, 2048], P('tensor', 'dp')
- grad_b_down: float32 [2048], P('dp')
The draws below stay inside these ranges and needn't reach their ends.
Inputs may be any that keep to these rules, and one draw needn't show every extreme that they name: Each bucket's 4 lengths sum to 1024; the longest is exactly 512. In every bucket exactly 512 tokens have exits above 12.
All inputs are finite; a program needn't handle non-finite values.
Results may differ from the reference program's by a relative error of at most 0.014.
Values sent between devices are 32-bit elements; how exact they have to be, the bound alone decides.
No kernel may reach another device: no remote copies, remote signals or barrier semaphores. Data moves between devices by JAX's collectives and lax.ppermute only.
A program may use at most 256 MiB of HBM per device.

```python
import math
import jax
import jax.numpy as jnp
import numpy as np
from jax import lax

D = 2048
HEADS = 32
HEAD = 64
FF = 8192
BUCKET = 1024
SEQS = 4
LAYER = 12
LONGEST = 512
LIVE = 512
TOKENS = 16384
N_DP = 16


def draw_exits(key, part):
    key = jax.random.fold_in(key, 7)
    bucket_keys = jax.random.split(jax.random.fold_in(key, 1), TOKENS // BUCKET)
    ranks = jax.vmap(lambda k: jax.random.permutation(k, BUCKET))(bucket_keys).reshape(TOKENS)
    high = jax.random.randint(jax.random.fold_in(key, 2), (TOKENS,), LAYER + 1, 2 * LAYER)
    lower = jax.random.randint(jax.random.fold_in(key, 3), (TOKENS,), 0, LAYER + 1)
    return jnp.where(ranks < LIVE, high, lower).astype(jnp.int32)


def steps_of(own_key, extent, cuts, smallest, high):
    def one(dim, blocks):
        heights = jax.random.uniform(jax.random.fold_in(jax.random.fold_in(own_key, 6), dim), (blocks,), jnp.float32, smallest / len(cuts), high / len(cuts))
        return jnp.repeat(jnp.exp(heights), extent[dim] // blocks).reshape((-1,) + (1,) * (len(extent) - dim - 1))

    factor_of = one(*cuts[0])
    for cut in cuts[1:]:
        factor_of = factor_of * one(*cut)
    return factor_of


def split_up(amount, total, reach, skew):
    loads = [(1 << 20) // math.isqrt(grade ** skew) + 1 for grade in range(2, amount + 1)]
    surplus, given = total - reach - (amount - 1), [1] * (amount - 1)
    while surplus > 0:
        candidates = [i for i in range(amount - 1) if given[i] < reach]
        whole, left = sum([loads[i] for i in candidates]), surplus
        for i in candidates:
            addition = min(reach - given[i], max(1, left * loads[i] // whole), surplus)
            given[i] = given[i] + addition
            surplus = surplus - addition
    return np.array([reach] + given)


def ragged_sizes(own_key, number_of, total, reach, skew):
    if number_of == 2:
        one = jax.random.randint(own_key, (), max(1, total - reach), min(reach, total - 1) + 1)
        return jnp.stack([one, total - one])
    tallies = jnp.asarray(split_up(number_of, total, reach, skew), jnp.int32)
    pairs = (number_of - 1) // 2
    giver, receiver = tallies[1:1 + 2 * pairs:2], tallies[2:2 + 2 * pairs:2]
    slack = jnp.minimum(giver - 1, reach - receiver)
    moved = jax.random.randint(jax.random.fold_in(own_key, 1), (pairs,), 0, 1 << 20) % (slack + 1)
    tallies = tallies.at[1:1 + 2 * pairs:2].set(giver - moved).at[2:2 + 2 * pairs:2].set(receiver + moved)
    return tallies[jax.random.permutation(jax.random.fold_in(own_key, 2), number_of)]


def noise(rng, dims, width, limit, shards=(), kind=jnp.bfloat16):
    array = jax.random.normal(rng, dims, jnp.float32) * width
    if len(shards) > 0:
        array = steps_of(rng, dims, shards, -0.22, 0.18) * array
    return jnp.clip(array, min=-limit, max=limit).astype(kind)


def setup_inputs(seed: int = 0) -> dict:
    splits = jax.random.split(jax.random.key(seed), 20)
    return {
        "tokens": noise(splits[0], (TOKENS, D), 1.0, 6.0, ((0, 16),)),
        "cotangent": noise(splits[1], (TOKENS, D), 1.0, 6.0, ((0, 16),)),
        "lengths": jax.vmap(lambda own: ragged_sizes(own, SEQS, BUCKET, LONGEST, 2))(jax.random.split(splits[2], N_DP)).reshape((N_DP, SEQS)).astype(jnp.int32),
        "exits": draw_exits(jax.random.fold_in(splits[19], 71), 0),
        "w_query": noise(splits[4], (D, D), D ** -0.5, 0.125, ((1, 8),)),
        "b_query": noise(splits[5], (D,), 0.5, 3.0, ((0, 8),)),
        "w_key": noise(splits[6], (D, D), D ** -0.5, 0.125, ((1, 8),)),
        "w_value": noise(splits[7], (D, D), D ** -0.5, 0.125, ((1, 8),)),
        "b_value": noise(splits[8], (D,), 0.5, 3.0, ((0, 8),)),
        "w_out": noise(splits[9], (D, D), (D // 16) ** -0.5, 0.5, ((0, 8),)),
        "b_out": noise(splits[10], (D,), 0.3, 2.0),
        "gain_one": jnp.clip(1.0 + 0.1 * jax.random.normal(splits[11], (D,), jnp.float32), 0.5, 1.5).astype(jnp.bfloat16),
        "shift_one": noise(splits[12], (D,), 0.3, 2.0),
        "gain_two": jnp.clip(1.0 + 0.1 * jax.random.normal(splits[13], (D,), jnp.float32), 0.5, 1.5).astype(jnp.bfloat16),
        "shift_two": noise(splits[14], (D,), 0.3, 2.0),
        "w_up": noise(splits[15], (D, FF), D ** -0.5, 0.125, ((1, 8),)),
        "b_up": noise(splits[16], (FF,), 0.5, 3.0, ((0, 8),)),
        "w_down": noise(splits[17], (FF, D), FF ** -0.5, 0.0625, ((0, 8),)),
        "b_down": noise(splits[18], (D,), 0.3, 2.0),
    }


@jax.custom_vjp
def low(v):
    return lax.optimization_barrier(v.astype(jnp.bfloat16)).astype(jnp.float32)

@jax.custom_vjp
def low_back(v):
    return v

def low_keep(v):
    return (low(v), None)

def low_pass(kept, grad):
    return (grad,)

def back_keep(v):
    return (v, None)

def back_low(kept, grad):
    return (low(grad),)
low.defvjp(low_keep, low_pass)
low_back.defvjp(back_keep, back_low)

def matmul(left, right):
    return jnp.dot(left, right, precision=lax.Precision.HIGHEST, preferred_element_type=jnp.float32)

def layer_norm(values, gain, shift):
    average = lax.optimization_barrier(jnp.mean(values, axis=-1, keepdims=True))
    centred = values - average
    spread = lax.optimization_barrier(jnp.mean(centred * centred, axis=-1, keepdims=True))
    return centred * lax.rsqrt(spread + 1e-05) * gain + shift

def bucket_mask(bucket_lengths, bucket_exits):
    position = jnp.arange(BUCKET, dtype=jnp.int32)
    bounds = jnp.cumsum(bucket_lengths).astype(jnp.int32)
    segment = lax.optimization_barrier(jnp.sum((position[:, None] >= bounds[None, :]).astype(jnp.int32), axis=1))
    living = bucket_exits > LAYER
    allowed = (segment[:, None] == segment[None, :]) & (position[None, :] <= position[:, None])
    allowed = allowed & (living[None, :] | (position[None, :] == position[:, None]))
    return (allowed, living.astype(jnp.float32)[:, None])

def bucket_forward(params, source, bucket_lengths, bucket_exits):
    w_query, b_query, w_key, w_value, b_value, w_out, b_out, gain_one, shift_one, gain_two, shift_two, w_up, b_up, w_down, b_down = params
    allowed, live_col = bucket_mask(bucket_lengths, bucket_exits)
    act_one = low(layer_norm(source, gain_one, shift_one))
    query = low(low_back((matmul(act_one, w_query) + b_query) * 0.125))
    keys = low(low_back(matmul(act_one, w_key)))
    values = low(low_back(matmul(act_one, w_value) + b_value))
    query_h = query.reshape(BUCKET, HEADS, HEAD)
    key_h = keys.reshape(BUCKET, HEADS, HEAD)
    value_h = values.reshape(BUCKET, HEADS, HEAD)
    scores = low_back(jnp.einsum('qhd,khd->hqk', query_h, key_h, precision=lax.Precision.HIGHEST))
    scores = jnp.where(allowed[None], scores, -1e+30)
    prob = low(jax.nn.softmax(scores, axis=-1))
    attended = jnp.einsum('hqk,khd->qhd', prob, value_h, precision=lax.Precision.HIGHEST).reshape(BUCKET, D)
    attended = low(low_back(attended))
    hidden_one = source + live_col * (low_back(matmul(attended, w_out)) + b_out)
    act_two = low(layer_norm(hidden_one, gain_two, shift_two))
    pre_gelu = low_back(matmul(act_two, w_up) + b_up)
    inner = low(jax.nn.gelu(pre_gelu, approximate=True))
    return hidden_one + live_col * (low_back(matmul(inner, w_down)) + b_down)

def forward(source, params, lengths, exits):
    buckets = TOKENS // BUCKET
    step = jax.checkpoint(bucket_forward)

    def one(item):
        return step(params, item[0], item[1], item[2])
    result = lax.map(one, (source.reshape(buckets, BUCKET, D), lengths, exits.reshape(buckets, BUCKET)))
    return result.reshape(TOKENS, D)

def reference(tokens, cotangent, lengths, exits, w_query, b_query, w_key, w_value, b_value, w_out, b_out, gain_one, shift_one, gain_two, shift_two, w_up, b_up, w_down, b_down):
    params = tuple((p.astype(jnp.float32) for p in (w_query, b_query, w_key, w_value, b_value, w_out, b_out, gain_one, shift_one, gain_two, shift_two, w_up, b_up, w_down, b_down)))
    source = tokens.astype(jnp.float32)

    def run(src, prm):
        return forward(src, prm, lengths, exits)
    output, pullback = jax.vjp(run, source, params)
    grad_source, grads = pullback(cotangent.astype(jnp.float32))
    return (output.astype(jnp.bfloat16), grad_source.astype(jnp.bfloat16), grads[0], grads[1], grads[2], grads[3], grads[4], grads[5], grads[6], grads[7], grads[8], grads[9], grads[10], grads[11], grads[12], grads[13], grads[14])
```

```python
import jax
import jax.numpy as jnp
from jax import lax
from jax.experimental import pallas as pl
from jax.experimental.pallas import tpu as pltpu
from jax.sharding import PartitionSpec as P

HEAD = 64
LAYER = 12
LIVE = 512
COLS = 256
NEG_BIG = -1e30
EPSILON = 1e-05
GELU_A = 0.7978845608028654
GELU_B = 0.044715

CORE = [(i, i ^ 1) for i in range(8)]
X_NEAR = [(2 * x + c, 2 * (x ^ 1) + c) for x in range(4) for c in range(2)]
X_FAR = [(2 * x + c, 2 * (3 - x) + c) for x in range(4) for c in range(2)]
Y_NEAR = [(4 * y + z, 4 * (y ^ 1) + z) for y in range(4) for z in range(4)]
Y_FAR = [(4 * y + z, 4 * (3 - y) + z) for y in range(4) for z in range(4)]
Z_NEAR = [(4 * y + z, 4 * y + (z ^ 1)) for y in range(4) for z in range(4)]
Z_FAR = [(4 * y + z, 4 * y + (3 - z)) for y in range(4) for z in range(4)]
ORDERS = (
    ((Y_NEAR, 0), (Y_FAR, 1), (Z_NEAR, 2), (Z_FAR, 3)),
    ((Y_FAR, 1), (Y_NEAR, 0), (Z_FAR, 3), (Z_NEAR, 2)),
    ((Z_NEAR, 2), (Z_FAR, 3), (Y_NEAR, 0), (Y_FAR, 1)),
    ((Z_FAR, 3), (Z_NEAR, 2), (Y_FAR, 1), (Y_NEAR, 0)),
)


def over_tensor(value, pairs):
    return lax.ppermute(value, "tensor", pairs)


def over_dp(value, pairs):
    return lax.ppermute(value, "dp", pairs)


def dot(left, right):
    return jnp.dot(left, right, preferred_element_type=jnp.float32)


def back_dot(left, right):
    return lax.dot_general(
        left, right, (((1,), (1,)), ((), ())), preferred_element_type=jnp.float32
    )


def outer_sum(left, right):
    return lax.dot_general(
        left, right, (((0,), (0,)), ((), ())), preferred_element_type=jnp.float32
    )


def normed(values):
    average = jnp.mean(values, axis=-1, keepdims=True)
    centred = values - average
    spread = jnp.mean(centred * centred, axis=-1, keepdims=True)
    scale = lax.rsqrt(spread + EPSILON)
    return centred * scale, scale


def norm_back(grad, normal, scale, gain):
    scaled = grad * gain
    first = jnp.mean(scaled, axis=-1, keepdims=True)
    second = jnp.mean(scaled * normal, axis=-1, keepdims=True)
    return scale * (scaled - first - normal * second)


def scatter_rows(part):
    sent = part(384, 512)
    core_one = over_tensor(sent, CORE)
    core_two = over_tensor(part(256, 384), CORE)
    far = part(128, 256) + core_one
    got_a11 = over_tensor(far[32:64], X_NEAR)
    got_b11 = over_tensor(far[96:128], X_FAR)
    got_a10 = over_tensor(far[0:32], X_NEAR)
    got_b10 = over_tensor(far[64:96], X_FAR)
    near = part(0, 128) + core_two
    got_a01 = over_tensor(near[32:64] + got_a11, X_FAR)
    got_b01 = over_tensor(near[96:128] + got_b11, X_NEAR)
    mine_a = near[0:32] + got_a10 + got_a01
    mine_b = near[64:96] + got_b10 + got_b01
    return jnp.concatenate([mine_a, mine_b], axis=0), sent


def gather_rows(mine):
    mine_a, mine_b = mine[0:32], mine[32:64]
    a01 = over_tensor(mine_a, X_FAR)
    b01 = over_tensor(mine_b, X_NEAR)
    a10 = over_tensor(mine_a, X_NEAR)
    b10 = over_tensor(mine_b, X_FAR)
    a11 = over_tensor(a01, X_NEAR)
    b11 = over_tensor(b01, X_FAR)
    first = jnp.concatenate([mine_a, a01, mine_b, b01], axis=0)
    second = jnp.concatenate([a10, a11, b10, b11], axis=0)
    return first, second, over_tensor(first, CORE), over_tensor(second, CORE)


def own_rows(values):
    return jnp.concatenate([values[0:32], values[64:96]], axis=0)


def attend_kernel(q_ref, k_ref, v_ref, bias_ref, out_ref, lse_ref):
    rows = 256
    lane = lax.broadcasted_iota(jnp.int32, (1, 128), 1)
    for step in range(LIVE // rows):
        here = pl.ds(step * rows, rows)
        bias = bias_ref[here, :]
        total = jnp.zeros((rows, 128), jnp.float32)
        logs = jnp.zeros((rows, 128), jnp.float32)
        for head in range(2):
            inside = (lane // HEAD) == head
            query = jnp.where(inside, q_ref[here, :], 0)
            scores = back_dot(query, k_ref[...]) + bias
            peak = jnp.max(scores, axis=-1, keepdims=True)
            expo = jnp.exp(scores - peak)
            summed = jnp.sum(expo, axis=-1, keepdims=True)
            prob = (expo * (1.0 / summed)).astype(jnp.bfloat16)
            total = jnp.where(inside, dot(prob, v_ref[...]), total)
            logs = jnp.where(inside, peak + jnp.log(summed), logs)
        out_ref[here, :] = total.astype(jnp.bfloat16)
        lse_ref[here, :] = logs


def attend(query, keys, values, bias):
    cols = query.shape[1]
    block = pl.BlockSpec((LIVE, 128), lambda i: (0, i))
    return pl.pallas_call(
        attend_kernel,
        grid=(cols // 128,),
        in_specs=[block, block, block, pl.BlockSpec((LIVE, LIVE), lambda i: (0, 0))],
        out_specs=[block, block],
        out_shape=[
            jax.ShapeDtypeStruct((LIVE, cols), jnp.bfloat16),
            jax.ShapeDtypeStruct((LIVE, cols), jnp.float32),
        ],
        compiler_params=pltpu.CompilerParams(vmem_limit_bytes=32 << 20),
        cost_estimate=pl.CostEstimate(
            flops=4 * 4 * LIVE * LIVE * 128, bytes_accessed=4 << 20, transcendentals=4 * LIVE * LIVE
        ),
        name="attend",
    )(query, keys, values, bias)


def piece_specs():
    return [pl.BlockSpec((128, COLS), lambda i: (0, i))] * 4


def together(pieces):
    return jnp.concatenate([piece[...] for piece in pieces], axis=0)


def ffn_kernel(
    p0, p1, p2, p3, gain_ref, shift_ref, up_ref, bias_ref, grad_ref,
    act_ref, inner_ref, pre_ref, sum_ref, total,
):
    step = pl.program_id(0)
    act = (together((p0, p1, p2, p3)) * gain_ref[...] + shift_ref[...]).astype(jnp.bfloat16)
    act_ref[...] = act
    product = dot(act, up_ref[...])

    @pl.when(step == 0)
    def _():
        total[...] = product

    @pl.when(step > 0)
    def _():
        total[...] += product

    @pl.when(step == pl.num_programs(0) - 1)
    def _():
        sum_ref[...] = jnp.zeros_like(sum_ref)

        def some(i, carry):
            here = pl.ds(pl.multiple_of(i * 32, 32), 32)
            pre = total[here, :] + bias_ref[...]
            square = pre * pre
            bent = jnp.tanh(GELU_A * pre * (1.0 + GELU_B * square))
            half = 0.5 * (1.0 + bent)
            inner_ref[here, :] = (pre * half).astype(jnp.bfloat16)
            slope = half + 0.5 * GELU_A * pre * (1.0 - bent * bent) * (
                1.0 + 3.0 * GELU_B * square
            )
            grad = (slope * grad_ref[here, :]).astype(jnp.bfloat16)
            pre_ref[here, :] = grad
            sum_ref[...] += jnp.sum(grad.astype(jnp.float32).reshape(4, 8, -1), axis=0)
            return carry

        lax.fori_loop(0, LIVE // 32, some, 0)


def ffn(pieces, gain, shift, w_up, b_up, grad_inner):
    features, width = w_up.shape
    whole = pl.BlockSpec((LIVE, width), lambda i: (0, 0))
    row = pl.BlockSpec((1, COLS), lambda i: (0, i))
    low = jax.ShapeDtypeStruct((LIVE, width), jnp.bfloat16)
    return pl.pallas_call(
        ffn_kernel,
        grid=(features // COLS,),
        in_specs=piece_specs()
        + [row, row, pl.BlockSpec((COLS, width), lambda i: (i, 0))]
        + [pl.BlockSpec((1, width), lambda i: (0, 0)), whole],
        out_specs=[pl.BlockSpec((LIVE, COLS), lambda i: (0, i)), whole, whole]
        + [pl.BlockSpec((8, width), lambda i: (0, 0))],
        out_shape=[
            jax.ShapeDtypeStruct((LIVE, features), jnp.bfloat16),
            low,
            low,
            jax.ShapeDtypeStruct((8, width), jnp.float32),
        ],
        scratch_shapes=[pltpu.VMEM((LIVE, width), jnp.float32)],
        compiler_params=pltpu.CompilerParams(vmem_limit_bytes=40 << 20),
        cost_estimate=pl.CostEstimate(
            flops=2 * LIVE * features * width, bytes_accessed=16 << 20, transcendentals=LIVE * width
        ),
        name="ffn",
    )(*pieces, gain, shift, w_up, b_up, grad_inner)


def ffn_out_kernel(rows_ref, inner_ref, down_ref, extra_ref, out_ref, ordered):
    @pl.when(pl.program_id(0) == 0)
    def _():
        for i in range(16):
            here = pl.ds(pl.multiple_of(rows_ref[i] * 32, 32), 32)
            ordered[32 * i : 32 * i + 32, :] = inner_ref[here, :]

    out_ref[...] = dot(ordered[...], down_ref[...])
    for i in range(2):
        here = pl.ds(pl.multiple_of(rows_ref[2 * i] * 32, 32), 32)
        out_ref[here, :] += extra_ref[32 * i : 32 * i + 32, :]


def ffn_out(rows, inner, w_down, extra):
    width, features = w_down.shape
    return pl.pallas_call(
        ffn_out_kernel,
        grid_spec=pltpu.PrefetchScalarGridSpec(
            num_scalar_prefetch=1,
            grid=(features // COLS,),
            in_specs=[
                pl.BlockSpec((LIVE, width), lambda i, rows: (0, 0)),
                pl.BlockSpec((width, COLS), lambda i, rows: (0, i)),
                pl.BlockSpec((64, COLS), lambda i, rows: (0, i)),
            ],
            out_specs=pl.BlockSpec((LIVE, COLS), lambda i, rows: (0, i)),
            scratch_shapes=[pltpu.VMEM((LIVE, width), jnp.bfloat16)],
        ),
        out_shape=jax.ShapeDtypeStruct((LIVE, features), jnp.float32),
        compiler_params=pltpu.CompilerParams(vmem_limit_bytes=32 << 20),
        cost_estimate=pl.CostEstimate(
            flops=2 * LIVE * features * width, bytes_accessed=9 << 20, transcendentals=0
        ),
        name="ffn_out",
    )(rows, inner, w_down, extra)


def spread_kernel(place_ref, whole_ref, live_ref, *refs):
    rows, out_ref = refs[:-1], refs[-1]
    if len(rows) == 1:
        low = rows[0][...]
    else:
        low = together(rows[:4]) + rows[4][...]
    wide = dot(place_ref[...], low.astype(jnp.bfloat16)).astype(jnp.bfloat16)
    out_ref[...] = jnp.where(live_ref[...] > 0, wide, whole_ref[...])


def spread(place, whole, live, rows, after=()):
    tokens, features = whole.shape
    pieces = len(rows) > 1
    wide = pl.BlockSpec((LIVE, COLS), lambda i: (0, i))
    block = pl.BlockSpec((tokens, COLS), lambda i: (0, i))
    body = spread_kernel
    if after:

        def body(*refs):
            spread_kernel(*refs[: -1 - len(after)], refs[-1])

    return pl.pallas_call(
        body,
        grid=(features // COLS,),
        in_specs=[
            pl.BlockSpec((tokens, LIVE), lambda i: (0, 0)),
            block,
            pl.BlockSpec((tokens, 1), lambda i: (0, 0)),
        ]
        + (piece_specs() if pieces else [])
        + [wide]
        + [pl.BlockSpec(memory_space=pl.ANY)] * len(after),
        out_specs=block,
        out_shape=jax.ShapeDtypeStruct(whole.shape, jnp.bfloat16),
        compiler_params=pltpu.CompilerParams(vmem_limit_bytes=32 << 20),
        cost_estimate=pl.CostEstimate(
            flops=2 * tokens * LIVE * features, bytes_accessed=14 << 20, transcendentals=0
        ),
        name="spread",
    )(place, whole, live, *rows, *after)


def attend_back_kernel(
    p0, p1, p2, p3, out_grad_ref, w_ref, q_ref, k_ref, v_ref, bias_ref, lse_ref,
    hidden_ref, low_ref, gq_ref, gk_ref, gv_ref, mixed, key_sum, value_sum,
):
    step = pl.program_id(0)
    hidden = together((p0, p1, p2, p3)) + out_grad_ref[...].astype(jnp.float32)
    low = hidden.astype(jnp.bfloat16)
    hidden_ref[...] = hidden
    low_ref[...] = low
    product = back_dot(low, w_ref[...])

    @pl.when(step == 0)
    def _():
        mixed[...] = product

    @pl.when(step > 0)
    def _():
        mixed[...] += product

    @pl.when(step == pl.num_programs(0) - 1)
    def _():
        rows = 256
        lane = lax.broadcasted_iota(jnp.int32, (1, 128), 1)
        for pair in range(q_ref.shape[1] // 128):
            cols = slice(128 * pair, 128 * pair + 128)
            key_sum[...] = jnp.zeros_like(key_sum)
            value_sum[...] = jnp.zeros_like(value_sum)
            for part in range(LIVE // rows):
                here = slice(part * rows, part * rows + rows)
                bias = bias_ref[here, :]
                total = jnp.zeros((rows, 128), jnp.float32)
                for head in range(2):
                    inside = (lane // HEAD) == head
                    query = jnp.where(inside, q_ref[here, cols], 0)
                    grad = jnp.where(inside, mixed[here, cols], 0.0).astype(jnp.bfloat16)
                    first = 128 * pair + head * HEAD
                    logs = lse_ref[here, first : first + 1]
                    prob = jnp.exp(back_dot(query, k_ref[:, cols]) + bias - logs)
                    grad_prob = back_dot(grad, v_ref[:, cols])
                    inner = jnp.sum(prob * grad_prob, axis=-1, keepdims=True)
                    grad_scores = (prob * (grad_prob - inner)).astype(jnp.bfloat16)
                    total = jnp.where(inside, dot(grad_scores, k_ref[:, cols]), total)
                    key_sum[...] += outer_sum(grad_scores, query)
                    value_sum[...] += outer_sum(prob.astype(jnp.bfloat16), grad)
                gq_ref[here, cols] = total.astype(jnp.bfloat16) * jnp.bfloat16(0.125)
            gk_ref[:, cols] = key_sum[...].astype(jnp.bfloat16)
            gv_ref[:, cols] = value_sum[...].astype(jnp.bfloat16)


def attend_back(pieces, out_grad, w_out, query, keys, values, bias, logs):
    cols, features = w_out.shape
    wide = pl.BlockSpec((LIVE, COLS), lambda i: (0, i))
    block = pl.BlockSpec((LIVE, cols), lambda i: (0, 0))
    shape = jax.ShapeDtypeStruct((LIVE, cols), jnp.bfloat16)
    return pl.pallas_call(
        attend_back_kernel,
        grid=(features // COLS,),
        in_specs=piece_specs()
        + [wide, pl.BlockSpec((cols, COLS), lambda i: (0, i))]
        + [block] * 3
        + [pl.BlockSpec((LIVE, LIVE), lambda i: (0, 0)), block],
        out_specs=[wide, wide] + [block] * 3,
        out_shape=[
            jax.ShapeDtypeStruct((LIVE, features), jnp.float32),
            jax.ShapeDtypeStruct((LIVE, features), jnp.bfloat16),
        ]
        + [shape] * 3,
        scratch_shapes=[pltpu.VMEM((LIVE, cols), jnp.float32)]
        + [pltpu.VMEM((LIVE, 128), jnp.float32)] * 2,
        compiler_params=pltpu.CompilerParams(vmem_limit_bytes=40 << 20),
        cost_estimate=pl.CostEstimate(
            flops=10 * 4 * LIVE * LIVE * 128 + 2 * LIVE * features * cols,
            bytes_accessed=15 << 20,
            transcendentals=4 * LIVE * LIVE,
        ),
        name="attend_back",
    )(*pieces, out_grad, w_out, query, keys, values, bias, logs)


def ffn_grads_kernel(act_ref, pre_ref, out_grad_ref, inner_ref, after_ref, out_ref):
    width = pre_ref.shape[1]
    out_ref[:, 0:width] = outer_sum(act_ref[...], pre_ref[...])
    out_ref[:, width : 2 * width] = outer_sum(out_grad_ref[...], inner_ref[...])


def ffn_grads(act, grad_pre, out_grad, inner, after):
    features, width = act.shape[1], grad_pre.shape[1]
    rows = 256
    left = pl.BlockSpec((LIVE, rows), lambda i: (0, i))
    right = pl.BlockSpec((LIVE, width), lambda i: (0, 0))
    return pl.pallas_call(
        ffn_grads_kernel,
        grid=(features // rows,),
        in_specs=[left, right, left, right, pl.BlockSpec(memory_space=pl.ANY)],
        out_specs=pl.BlockSpec((rows, 2 * width), lambda i: (i, 0)),
        out_shape=jax.ShapeDtypeStruct((features, 2 * width), jnp.float32),
        compiler_params=pltpu.CompilerParams(vmem_limit_bytes=32 << 20),
        cost_estimate=pl.CostEstimate(
            flops=4 * LIVE * features * width, bytes_accessed=24 << 20, transcendentals=0
        ),
        name="ffn_grads",
    )(act, grad_pre, out_grad, inner, after)


def attn_grads_kernel(perm_ref, *refs):
    for i in range(4):
        refs[9 + i][...] = outer_sum(refs[i][...], refs[4 + i][...])


def attn_grads(perm, lefts, rights, base, after):
    cols = rights[0].shape[1]

    def left_at(i):
        return pl.BlockSpec((LIVE, 128), lambda j, perm: (0, perm[i, base + j]))

    return pl.pallas_call(
        attn_grads_kernel,
        grid_spec=pltpu.PrefetchScalarGridSpec(
            num_scalar_prefetch=1,
            grid=(8,),
            in_specs=[left_at(i) for i in range(4)]
            + [pl.BlockSpec((LIVE, cols), lambda j, perm: (0, 0))] * 4
            + [pl.BlockSpec(memory_space=pl.ANY)],
            out_specs=[pl.BlockSpec((128, cols), lambda j, perm: (j, 0))] * 4,
        ),
        out_shape=[jax.ShapeDtypeStruct((1024, cols), jnp.float32)] * 4,
        compiler_params=pltpu.CompilerParams(vmem_limit_bytes=32 << 20),
        cost_estimate=pl.CostEstimate(
            flops=8 * LIVE * 1024 * cols, bytes_accessed=8 << 20, transcendentals=0
        ),
        name="attn_grads",
    )(perm, *lefts, *rights, after)


def halve(order, keep, send):
    got = over_dp(send, order[0][0])
    two = over_dp(keep[512:1024] + got[512:1024], order[1][0])
    three = over_dp(keep[256:512] + got[256:512] + two[256:512], order[2][0])
    four = over_dp(
        keep[128:256] + got[128:256] + two[128:256] + three[128:256], order[3][0]
    )
    return keep[0:128] + got[0:128] + two[0:128] + three[0:128] + four


def local(
    tokens,
    cotangent,
    lengths,
    exits,
    w_query,
    b_query,
    w_key,
    w_value,
    b_value,
    w_out,
    b_out,
    gain_one,
    shift_one,
    gain_two,
    shift_two,
    w_up,
    b_up,
    w_down,
    b_down,
):
    f32, bf16 = jnp.float32, jnp.bfloat16
    at_tensor = lax.axis_index("tensor")
    core, x_high = at_tensor & 1, at_tensor >> 2
    x_gray = ((at_tensor >> 1) & 1) ^ x_high
    at_dp = lax.axis_index("dp")
    y_high, z_high = at_dp >> 3, (at_dp >> 1) & 1
    y_gray, z_gray = ((at_dp >> 2) & 1) ^ y_high, (at_dp & 1) ^ z_high
    dp_bits = (y_gray, y_high, z_gray, z_high)

    def own_place(rank):
        side = (rank >> 6) & 1
        one = jnp.where(side == 1, x_high, x_gray)
        two = jnp.where(side == 1, x_gray, x_high)
        return rank ^ (core << 8) ^ (one << 7) ^ (two << 5)

    def dp_blocks(order):
        own = jnp.arange(16, dtype=jnp.int32)
        bits = [None] * 4
        for place, (_, bit) in enumerate(order):
            bits[bit] = ((own >> (3 - place)) & 1) ^ dp_bits[bit]
        return 4 * (2 * bits[1] + (bits[0] ^ bits[1])) + 2 * bits[3] + (bits[2] ^ bits[3])

    perm = jnp.stack([dp_blocks(order) for order in ORDERS])

    bucket_rows = tokens.shape[0]
    place_all = jnp.arange(bucket_rows, dtype=jnp.int32)
    bounds = jnp.cumsum(lengths[0])
    segment_all = jnp.sum((place_all[:, None] >= bounds[None, :]).astype(jnp.int32), axis=1)
    living = exits > LAYER
    rank = (
        jnp.sum(
            jnp.where((place_all[None, :] <= place_all[:, None]) & living[None, :], 1, 0), axis=1
        )
        - 1
    )
    row_of = jnp.where(living, own_place(rank), -1)
    own_index = jnp.arange(LIVE, dtype=jnp.int32)
    pick = (own_index[:, None] == row_of[None, :]).astype(bf16)
    place = (row_of[:, None] == own_index[None, :]).astype(bf16)
    place_ranked = (jnp.where(living, rank, -1)[:, None] == own_index[None, :]).astype(bf16)
    living_column = living.astype(jnp.int32)[:, None]
    rows_of = own_place(32 * jnp.arange(16, dtype=jnp.int32)) >> 5
    rank_own = own_place(own_index)
    segment_own = jnp.sum(
        jnp.where(own_index[:, None] == row_of[None, :], segment_all[None, :], 0), axis=1
    )
    allowed = (segment_own[:, None] == segment_own[None, :]) & (
        rank_own[None, :] <= rank_own[:, None]
    )
    bias = jnp.where(allowed, 0.0, NEG_BIG).astype(f32)

    source_low = dot(pick, tokens).astype(bf16)
    grad_out_low = dot(pick, cotangent).astype(bf16)
    source = source_low.astype(f32)
    grad_out = grad_out_low.astype(f32)

    gain_one_f, shift_one_f = gain_one.astype(f32), shift_one.astype(f32)
    gain_two_f, shift_two_f = gain_two.astype(f32), shift_two.astype(f32)

    normal_one, scale_one = normed(source)
    act_one = (normal_one * gain_one_f + shift_one_f).astype(bf16)
    query = ((dot(act_one, w_query) + b_query) * 0.125).astype(bf16)
    keys = dot(act_one, w_key).astype(bf16)
    values = (dot(act_one, w_value) + b_value).astype(bf16)
    attended, logs = attend(query, keys, values, bias)
    attn_mine, _ = scatter_rows(lambda low, high: dot(attended[low:high], w_out))

    hidden_mine = own_rows(source) + (attn_mine + b_out.astype(f32))
    normal_two, scale_two = normed(hidden_mine)

    act_two, inner, grad_pre, sum_up = ffn(
        gather_rows(normal_two),
        gain_two_f[None],
        shift_two_f[None],
        w_up,
        b_up.astype(f32)[None],
        back_dot(grad_out_low, w_down),
    )
    grad_two_mine, sent = scatter_rows(lambda low, high: back_dot(grad_pre[low:high], w_up))
    ffn_both = ffn_grads(act_two, grad_pre, grad_out_low, inner, sent)
    ffn_share = lax.psum_scatter(ffn_both, "dp", scatter_dimension=0, tiled=True)
    output_live = lax.psum(
        ffn_out(rows_of, inner, w_down, hidden_mine + b_down.astype(f32)), "tensor"
    )

    norm_two_mine = norm_back(grad_two_mine, normal_two, scale_two, gain_two_f)
    grad_hidden, grad_attn_low, grad_query, grad_key, grad_value = attend_back(
        gather_rows(norm_two_mine), grad_out_low, w_out, query, keys, values, bias, logs
    )
    w_qkv = jnp.concatenate([w_query, w_key, w_value], axis=1)
    grad_qkv = jnp.concatenate([grad_query, grad_key, grad_value], axis=1)
    grad_one_mine, sent = scatter_rows(lambda low, high: back_dot(grad_qkv[low:high], w_qkv))
    rights = (grad_query, grad_key, grad_value, attended)
    lefts = (act_one, act_one, act_one, grad_attn_low)
    sends = attn_grads(perm, lefts, rights, 8, sent)
    keeps = attn_grads(perm, lefts, rights, 0, sends[0])
    attn_shares = [halve(order, keep, send) for order, keep, send in zip(ORDERS, keeps, sends)]
    output_rows = spread(place_ranked, tokens, living_column, (output_live,), (grad_one_mine,))

    normal_one_mine, scale_one_mine = own_rows(normal_one), own_rows(scale_one)
    norm_one_mine = norm_back(grad_one_mine, normal_one_mine, scale_one_mine, gain_one_f)
    input_rows = spread(
        place, cotangent, living_column, (*gather_rows(norm_one_mine), grad_hidden)
    )

    grad_out_mine = own_rows(grad_out)
    common = jnp.stack(
        [
            jnp.sum(grad_one_mine * normal_one_mine, axis=0),
            jnp.sum(grad_one_mine, axis=0),
            jnp.sum(grad_two_mine * normal_two, axis=0),
            jnp.sum(grad_two_mine, axis=0),
            jnp.sum(grad_out_mine + norm_two_mine, axis=0),
            jnp.sum(grad_out_mine, axis=0),
        ]
    )
    sum_query = jnp.sum(grad_query.astype(f32), axis=0).reshape(16, 16)
    sum_value = jnp.sum(grad_value.astype(f32), axis=0).reshape(16, 16)
    sum_up = jnp.sum(sum_up, axis=0).reshape(16, 64)
    own_vectors = jnp.concatenate(
        [sum_query, sum_value, sum_up, jnp.zeros((16, 32), f32)], axis=1
    ).reshape(16, 1, 128)
    vectors = jnp.concatenate(
        [common.reshape(6, 16, 128).transpose(1, 0, 2), own_vectors, jnp.zeros((16, 1, 128), f32)],
        axis=1,
    )[perm[0]]
    for count, (pairs, _) in zip((8, 4, 2, 1), ORDERS[0]):
        vectors = vectors[0:count] + over_dp(vectors[count : 2 * count], pairs)
    own_share = vectors[0, 6]
    common_share = vectors[0]
    for pairs in (CORE, X_NEAR, X_FAR):
        common_share = common_share + over_tensor(common_share, pairs)

    return (
        output_rows,
        input_rows,
        attn_shares[0],
        own_share[0:16],
        attn_shares[1],
        attn_shares[2],
        own_share[16:32],
        attn_shares[3].T,
        common_share[4],
        common_share[0],
        common_share[1],
        common_share[2],
        common_share[3],
        ffn_share[:, 0:1024],
        own_share[32:96],
        ffn_share[:, 1024:2048].T,
        common_share[5],
    )


def solution(mesh):
    in_specs = (
        P("dp", None),
        P("dp", None),
        P("dp", None),
        P("dp"),
        P(None, "tensor"),
        P("tensor"),
        P(None, "tensor"),
        P(None, "tensor"),
        P("tensor"),
        P("tensor", None),
        P(),
        P(),
        P(),
        P(),
        P(),
        P(None, "tensor"),
        P("tensor"),
        P("tensor", None),
        P(),
    )
    out_specs = (
        P("dp", None),
        P("dp", None),
        P("dp", "tensor"),
        P(("tensor", "dp")),
        P("dp", "tensor"),
        P("dp", "tensor"),
        P(("tensor", "dp")),
        P("tensor", "dp"),
        P("dp"),
        P("dp"),
        P("dp"),
        P("dp"),
        P("dp"),
        P("dp", "tensor"),
        P(("tensor", "dp")),
        P("tensor", "dp"),
        P("dp"),
    )
    return jax.shard_map(local, mesh=mesh, in_specs=in_specs, out_specs=out_specs, check_vma=False)
```

```python
import functools

import jax
import jax.numpy as jnp
from jax import lax
from jax.experimental import pallas as pl
from jax.experimental.pallas import tpu as pltpu
from jax.sharding import PartitionSpec as P

HEAD = 64
LAYER = 12
LIVE = 512
FFN_COLS = 1024
NEG_BIG = -1e30
EPSILON = 1e-05
GELU_A = 0.7978845608028654
GELU_B = 0.044715

CORE = [(i, i ^ 1) for i in range(8)]
X_NEAR = [(2 * x + c, 2 * (x ^ 1) + c) for x in range(4) for c in range(2)]
X_FAR = [(2 * x + c, 2 * (3 - x) + c) for x in range(4) for c in range(2)]
Y_NEAR = [(4 * y + z, 4 * (y ^ 1) + z) for y in range(4) for z in range(4)]
Y_FAR = [(4 * y + z, 4 * (3 - y) + z) for y in range(4) for z in range(4)]
Z_NEAR = [(4 * y + z, 4 * y + (z ^ 1)) for y in range(4) for z in range(4)]
Z_FAR = [(4 * y + z, 4 * y + (3 - z)) for y in range(4) for z in range(4)]
ORDERS = (
    ((Y_NEAR, 0), (Y_FAR, 1), (Z_NEAR, 2), (Z_FAR, 3)),
    ((Y_FAR, 1), (Y_NEAR, 0), (Z_FAR, 3), (Z_NEAR, 2)),
    ((Z_NEAR, 2), (Z_FAR, 3), (Y_NEAR, 0), (Y_FAR, 1)),
    ((Z_FAR, 3), (Z_NEAR, 2), (Y_FAR, 1), (Y_NEAR, 0)),
)


def over_tensor(value, pairs):
    return lax.ppermute(value, "tensor", pairs)


def over_dp(value, pairs):
    return lax.ppermute(value, "dp", pairs)


def dot(left, right):
    return jnp.dot(left, right, preferred_element_type=jnp.float32)


def back_dot(left, right):
    return lax.dot_general(
        left, right, (((1,), (1,)), ((), ())), preferred_element_type=jnp.float32
    )


def outer_sum(left, right):
    return lax.dot_general(
        left, right, (((0,), (0,)), ((), ())), preferred_element_type=jnp.float32
    )


def normed(values):
    average = jnp.mean(values, axis=-1, keepdims=True)
    centred = values - average
    spread = jnp.mean(centred * centred, axis=-1, keepdims=True)
    scale = lax.rsqrt(spread + EPSILON)
    return centred * scale, scale


def grant(mib, **more):
    return pltpu.CompilerParams(vmem_limit_bytes=mib << 20, **more)


def cost(flops, mib, transcendentals=0):
    return pl.CostEstimate(
        flops=flops, bytes_accessed=int(mib * 1048576), transcendentals=transcendentals
    )


ANYWHERE = pl.BlockSpec(memory_space=pl.ANY)


def far_away(*values):
    return [pltpu.with_memory_space_constraint(value, pltpu.HBM) for value in values]


def in_hbm(shape, dtype):
    return pltpu.HBM(shape, dtype)


DONE = jax.ShapeDtypeStruct((8, 128), jnp.float32)


def whole(shape):
    return pl.BlockSpec(shape, lambda *i: (0,) * len(shape))


def parts_kernel(count, transposed, sums, *refs):
    total = None
    for left, right in zip(refs[:count], refs[count : 2 * count]):
        product = (back_dot if transposed else dot)(left[...], right[...])
        total = product if total is None else total + product
    if sums:
        normal_ref, sum_ref = refs[2 * count], refs[-1]
        normal = normal_ref[...].astype(jnp.float32)
        sum_ref[...] = jnp.zeros_like(sum_ref)
        sum_ref[0:1, :] = jnp.sum(total * normal, axis=0, keepdims=True)
        sum_ref[1:2, :] = jnp.sum(total, axis=0, keepdims=True)
        refs = refs[:-1]
    first, second = refs[-2:]
    first[...] = total[0:128]
    second[...] = total[128:256]


def parts(lefts, rights, transposed, half, after=(), normal=None):
    count, depth = len(lefts), lefts[0].shape[1]
    features = rights[0].shape[0 if transposed else 1]
    cols = 512
    right = (
        pl.BlockSpec((cols, depth), lambda i: (i, 0))
        if transposed
        else pl.BlockSpec((depth, cols), lambda i: (0, i))
    )
    shape = jax.ShapeDtypeStruct((128, features), jnp.float32)
    sums = normal is not None
    extra = far_away(normal) if sums else []
    return pl.pallas_call(
        functools.partial(parts_kernel, count, transposed, sums),
        grid=(features // cols,),
        in_specs=[pl.BlockSpec((256, depth), lambda i: (half, 0))] * count
        + [right] * count
        + [pl.BlockSpec((256, cols), lambda i: (half, i))] * len(extra)
        + [ANYWHERE] * len(after),
        out_specs=[pl.BlockSpec((128, cols), lambda i: (0, i))] * 2
        + [pl.BlockSpec((8, cols), lambda i: (0, i))] * len(extra),
        out_shape=[shape] * 2 + [jax.ShapeDtypeStruct((8, features), jnp.float32)] * len(extra),
        compiler_params=grant(24),
        cost_estimate=cost(2 * 256 * depth * count * features, 6),
        name="parts",
    )(*lefts, *rights, *extra, *after)


def add_kernel(counts, *refs):
    outs = refs[-len(counts) :]
    first = 0
    for out_ref, count in zip(outs, counts):
        out_ref[...] = summed(refs[first : first + count])
        first += count


def add(sums, rows, after=()):
    features = sums[0][0][0].shape[1]
    cols = 1024
    return pl.pallas_call(
        functools.partial(add_kernel, [len(terms) for terms in sums]),
        grid=(features // cols,),
        in_specs=[
            pl.BlockSpec((rows, cols), lambda i, block=block: (block, i))
            for terms in sums
            for _, block in terms
        ]
        + [ANYWHERE] * len(after),
        out_specs=[pl.BlockSpec((rows, cols), lambda i: (0, i))] * len(sums),
        out_shape=[jax.ShapeDtypeStruct((rows, features), jnp.float32)] * len(sums),
        compiler_params=grant(8),
        cost_estimate=cost(0, 2),
        name="add",
    )(*[array for terms in sums for array, _ in terms], *after)


def scatter_rows(lefts, rights, transposed, early=None, beside=None, normal=None):
    sent = parts(lefts, rights, transposed, 1, (), normal)
    core_far = over_tensor(sent[1], CORE)
    core_near = over_tensor(sent[0], CORE)
    own = parts(lefts, rights, transposed, 0, sent[0:1], normal)
    near, far = own[0:2]
    done = early(sent, own) if early else ()
    far_a, far_b = add([[(far, i), (core_far, i)] for i in range(2)], 64, (*done, core_near))
    got_a = over_tensor(far_a, X_NEAR)
    got_b = over_tensor(far_b, X_FAR)
    done = beside(far_a) if beside else ()
    sends = [
        add([[(near, block), (core_near, block), (got, 1)]], 32, done)[0]
        for got, block in ((got_a, 1), (got_b, 3))
    ]
    last_a, last_b = [
        over_tensor(send, pairs) for send, pairs in zip(sends, (X_FAR, X_NEAR))
    ]
    return (
        [(near, 0), (core_near, 0), (got_a, 0), (last_a, 0)],
        [(near, 2), (core_near, 2), (got_b, 0), (last_b, 0)],
        sends,
    )


def join_kernel(*refs):
    for i in range(4):
        refs[4][32 * i : 32 * i + 32, :] = refs[i][...]


def join(pieces):
    features = pieces[0].shape[1]
    cols = 512
    return pl.pallas_call(
        join_kernel,
        grid=(features // cols,),
        in_specs=[pl.BlockSpec((32, cols), lambda i: (0, i))] * 4,
        out_specs=pl.BlockSpec((128, cols), lambda i: (0, i)),
        out_shape=jax.ShapeDtypeStruct((128, features), jnp.float32),
        compiler_params=grant(6),
        cost_estimate=cost(0, 2),
        name="join",
    )(*pieces)


def gather_rows(mine_a, mine_b):
    a01 = over_tensor(mine_a, X_FAR)
    b01 = over_tensor(mine_b, X_NEAR)
    a10 = over_tensor(mine_a, X_NEAR)
    b10 = over_tensor(mine_b, X_FAR)
    a11 = over_tensor(a01, X_NEAR)
    b11 = over_tensor(b01, X_FAR)
    first = join((mine_a, a01, mine_b, b01))
    second = join((a10, a11, b10, b11))
    return first, second, over_tensor(first, CORE), over_tensor(second, CORE)


def row_block(pair, features):
    return pl.BlockSpec((32, features), lambda i, block=pair[1]: (block, 0))


def summed(refs):
    return sum(ref[...].astype(jnp.float32) for ref in refs[1:]) + refs[0][...]


def norm_two_kernel(*refs):
    bias_ref, hidden_ref, scale_ref = refs[10], refs[11], refs[14]
    for i in range(2):
        here = slice(32 * i, 32 * i + 32)
        hidden = summed(refs[5 * i : 5 * i + 5]) + bias_ref[...]
        normal, scale = normed(hidden)
        hidden_ref[here, :] = hidden
        refs[12 + i][...] = normal
        scale_ref[here, :] = jnp.broadcast_to(scale, (32, 128))


def norm_two(terms_a, terms_b, bias):
    features = bias.shape[1]
    terms = terms_a + terms_b
    piece = jax.ShapeDtypeStruct((32, features), jnp.float32)
    return pl.pallas_call(
        norm_two_kernel,
        grid=(1,),
        in_specs=[row_block(term, features) for term in terms] + [whole((1, features))],
        out_specs=[whole((64, features)), whole((32, features)), whole((32, features)), whole((64, 128))],
        out_shape=[
            jax.ShapeDtypeStruct((64, features), jnp.float32),
            piece,
            piece,
            jax.ShapeDtypeStruct((64, 128), jnp.float32),
        ],
        compiler_params=grant(12),
        cost_estimate=cost(20 * 64 * features, 4),
        name="norm_two",
    )(*[term[0] for term in terms], bias)


def norm_back_kernel(*refs):
    scale_ref, gain_ref = refs[12:14]
    pieces, total_ref, sums_ref = refs[-4:-2], refs[-2], refs[-1]
    sums_ref[...] = jnp.zeros_like(sums_ref)
    for i in range(2):
        here = slice(32 * i, 32 * i + 32)
        grad = summed(refs[4 * i : 4 * i + 4])
        normal = refs[8 + 2 * i][...]
        base = refs[9 + 2 * i][...].astype(jnp.float32)
        scaled = grad * gain_ref[...]
        first = jnp.mean(scaled, axis=-1, keepdims=True)
        second = jnp.mean(scaled * normal, axis=-1, keepdims=True)
        norm = scale_ref[here, 0:1] * (scaled - first - normal * second)
        total = base + norm
        pieces[i][...] = norm
        total_ref[here, :] = total
        sums_ref[0:1, :] += jnp.sum(grad * normal, axis=0, keepdims=True)
        sums_ref[1:2, :] += jnp.sum(grad, axis=0, keepdims=True)
        sums_ref[2:3, :] += jnp.sum(total, axis=0, keepdims=True)
        sums_ref[3:4, :] += jnp.sum(base, axis=0, keepdims=True)


def norm_back(terms_a, terms_b, normals, bases, scale, gain, after=()):
    features = gain.shape[1]
    terms = terms_a + terms_b + [normals[0], bases[0], normals[1], bases[1]]
    piece = jax.ShapeDtypeStruct((32, features), jnp.float32)
    return pl.pallas_call(
        norm_back_kernel,
        grid=(1,),
        in_specs=[row_block(term, features) for term in terms]
        + [whole((64, 128)), whole((1, features))]
        + [ANYWHERE] * len(after),
        out_specs=[whole((32, features))] * 2 + [whole((64, features)), whole((8, features))],
        out_shape=[
            piece,
            piece,
            jax.ShapeDtypeStruct((64, features), jnp.float32),
            jax.ShapeDtypeStruct((8, features), jnp.float32),
        ],
        compiler_params=grant(12),
        cost_estimate=cost(20 * 64 * features, 4),
        name="norm_back",
    )(*[term[0] for term in terms], scale, gain, *after)


def own_bits():
    at = lax.axis_index("tensor")
    high = at >> 2
    return at & 1, ((at >> 1) & 1) ^ high, high


def own_place(rank, bits):
    core, gray, high = bits
    side = (rank >> 6) & 1
    one = side * high + (1 - side) * gray
    two = side * gray + (1 - side) * high
    return rank ^ (core << 8) ^ (one << 7) ^ (two << 5)


def iota(shape, axis):
    return lax.broadcasted_iota(jnp.int32, shape, axis)


def live_ranks(exits):
    living = exits > LAYER
    ones = jnp.where(living, 1.0, 0.0)
    up_to = (iota((128, 128), 0) <= iota((128, 128), 1)).astype(jnp.bfloat16)
    within = dot(ones.astype(jnp.bfloat16), up_to)
    totals = jnp.broadcast_to(jnp.sum(ones, axis=1, keepdims=True), (8, 128))
    before = jnp.zeros((8, 128), jnp.float32)
    for i in range(7):
        before += jnp.where(iota((8, 128), 0) > i, totals[i : i + 1, :], 0.0)
    return living, (within + before).astype(jnp.int32) - 1


def front_kernel(
    lengths_ref, exits_ref, tokens_ref, gain_ref, shift_ref, wq_hbm, wk_hbm, wv_hbm, bq_ref, bv_ref,
    pick_hbm, bias_hbm, source_ref, act_hbm, normal_hbm, q_ref, k_ref, v_ref, out_ref, lse_ref,
    rows_ref, w_ref, pick_ref, bias_ref, act_ref, normal_ref, sems, out_sems,
):
    step = pl.program_id(0)
    copies = [
        pltpu.make_async_copy(
            weight, w_ref.at[:, pl.ds(i * weight.shape[1], weight.shape[1])], sems.at[i]
        )
        for i, weight in enumerate((wq_hbm, wk_hbm, wv_hbm))
    ]
    outs = [
        pltpu.make_async_copy(here, there, out_sems.at[i])
        for i, (here, there) in enumerate(
            (
                (pick_ref, pick_hbm),
                (bias_ref, bias_hbm),
                (act_ref, act_hbm),
                (normal_ref, normal_hbm),
            )
        )
    ]

    @pl.when(step == 0)
    def _():
        for copy in copies:
            copy.start()
        bits = own_bits()
        living, rank = live_ranks(exits_ref[...])
        row_of = jnp.where(living, own_place(rank, bits), -1)
        for i in range(8):
            pick_ref[:, 128 * i : 128 * i + 128] = jnp.where(
                iota((LIVE, 128), 0) == row_of[i : i + 1, :], 1.0, 0.0
            ).astype(jnp.bfloat16)
        token = 128 * iota((8, 128), 0) + iota((8, 128), 1)
        rank_row = own_place(iota((1, LIVE), 1), bits)
        rank_column = own_place(iota((LIVE, 1), 0), bits)
        segment_row, segment_column = jnp.zeros_like(rank_row), jnp.zeros_like(rank_column)
        bound = 0
        for i in range(lengths_ref.shape[1] - 1):
            bound = bound + lengths_ref[0, i]
            count = jnp.sum(jnp.where(living & (token < bound), 1, 0))
            segment_row += (rank_row >= count).astype(jnp.int32)
            segment_column += (rank_column >= count).astype(jnp.int32)
        allowed = (segment_column == segment_row) & (rank_row <= rank_column)
        bias_ref[...] = jnp.where(allowed, 0.0, NEG_BIG)
        for out in outs[:2]:
            out.start()

    cols = tokens_ref.shape[1]
    found = dot(pick_ref[...], tokens_ref[...]).astype(jnp.bfloat16)
    source_ref[...] = found
    for i in range(2):

        @pl.when(step == i)
        def _(i=i):
            rows_ref[:, cols * i : cols * i + cols] = found

    @pl.when(step == pl.num_programs(0) - 1)
    def _():
        gain, shift = wide_row(gain_ref), wide_row(shift_ref)

        def some(i, carry):
            here = pl.ds(pl.multiple_of(i * 16, 16), 16)
            normal, _ = normed(rows_ref[here, :].astype(jnp.float32))
            normal_ref[here, :] = normal.astype(jnp.bfloat16)
            act_ref[here, :] = (normal * gain + shift).astype(jnp.bfloat16)
            return carry

        lax.fori_loop(0, LIVE // 16, some, 0, unroll=8)
        for out in outs[2:]:
            out.start()
        for copy in copies:
            copy.wait()
        width = q_ref.shape[1]
        product = dot(act_ref[...], w_ref[...])
        q_ref[...] = ((product[:, 0:width] + wide_row(bq_ref)) * 0.125).astype(jnp.bfloat16)
        k_ref[...] = product[:, width : 2 * width].astype(jnp.bfloat16)
        v_ref[...] = (product[:, 2 * width :] + wide_row(bv_ref)).astype(jnp.bfloat16)
        rows = LIVE
        lane = iota((1, 128), 1)
        for pair in range(q_ref.shape[1] // 128):
            at = slice(128 * pair, 128 * pair + 128)
            for part in range(LIVE // rows):
                here = slice(part * rows, part * rows + rows)
                bias = bias_ref[here, :]
                total = jnp.zeros((rows, 128), jnp.float32)
                logs = jnp.zeros((rows, 128), jnp.float32)
                for head in range(2):
                    inside = (lane // HEAD) == head
                    query = jnp.where(inside, q_ref[here, at], 0)
                    scores = back_dot(query, k_ref[:, at]) + bias
                    peak = jnp.max(scores, axis=-1, keepdims=True)
                    expo = jnp.exp(scores - peak)
                    total_expo = jnp.sum(expo, axis=-1, keepdims=True)
                    prob = (expo * (1.0 / total_expo)).astype(jnp.bfloat16)
                    total = jnp.where(inside, dot(prob, v_ref[:, at]), total)
                    logs = jnp.where(inside, peak + jnp.log(total_expo), logs)
                out_ref[here, at] = total.astype(jnp.bfloat16)
                lse_ref[here, at] = logs
        for out in outs:
            out.wait()


def wide_row(ref):
    return ref[...].astype(jnp.float32).reshape(1, -1)


def front(lengths, exits, tokens, gain, shift, weights, b_query, b_value):
    features, cols = weights[0].shape
    rows = tokens.shape[0]
    block = features // 2
    low = jax.ShapeDtypeStruct((LIVE, cols), jnp.bfloat16)
    row = whole((features,))
    heads = whole((LIVE, cols))
    return pl.pallas_call(
        front_kernel,
        grid=(2,),
        in_specs=[
            pl.BlockSpec(memory_space=pltpu.SMEM),
            whole((8, rows // 8)),
            pl.BlockSpec((rows, block), lambda i: (0, i)),
            row,
            row,
        ]
        + [ANYWHERE] * 3
        + [whole((cols,))] * 2,
        out_specs=[ANYWHERE] * 2
        + [pl.BlockSpec((LIVE, block), lambda i: (0, i))]
        + [ANYWHERE] * 2
        + [heads] * 5,
        out_shape=[
            in_hbm((LIVE, rows), jnp.bfloat16),
            in_hbm((LIVE, LIVE), jnp.float32),
        ]
        + [in_hbm((LIVE, features), jnp.bfloat16)] * 3
        + [in_hbm((LIVE, cols), jnp.bfloat16)] * 3
        + [low]
        + [in_hbm((LIVE, cols), jnp.float32)],
        scratch_shapes=[
            pltpu.VMEM((LIVE, features), jnp.bfloat16),
            pltpu.VMEM((features, 3 * cols), jnp.bfloat16),
            pltpu.VMEM((LIVE, rows), jnp.bfloat16),
            pltpu.VMEM((LIVE, LIVE), jnp.float32),
            pltpu.VMEM((LIVE, features), jnp.bfloat16),
            pltpu.VMEM((LIVE, features), jnp.bfloat16),
            pltpu.SemaphoreType.DMA((3,)),
            pltpu.SemaphoreType.DMA((4,)),
        ],
        compiler_params=grant(44),
        cost_estimate=cost(
            2 * LIVE * features * (rows + 3 * cols) + 16 * LIVE * LIVE * 128, 16, 4 * LIVE * LIVE
        ),
        name="front",
    )(
        lengths,
        *far_away(
            exits.reshape(8, rows // 8), tokens, gain, shift, *weights, b_query, b_value
        ),
    )


def pick_rows_kernel(pick_ref, full_ref, w_ref, *refs):
    rows_ref, product_ref = refs[-2:]
    rows = dot(pick_ref[...], full_ref[...]).astype(jnp.bfloat16)
    rows_ref[...] = rows
    product = back_dot(rows, w_ref[...])

    @pl.when(pl.program_id(0) == 0)
    def _():
        product_ref[...] = product

    @pl.when(pl.program_id(0) > 0)
    def _():
        product_ref[...] += product


def pick_rows(pick, full, weight, after):
    tokens, features = full.shape
    width = weight.shape[0]
    cols = 512
    return pl.pallas_call(
        pick_rows_kernel,
        grid=(features // cols,),
        in_specs=[
            whole((LIVE, tokens)),
            pl.BlockSpec((tokens, cols), lambda i: (0, i)),
            pl.BlockSpec((width, cols), lambda i: (0, i)),
        ]
        + [ANYWHERE] * len(after),
        out_specs=[pl.BlockSpec((LIVE, cols), lambda i: (0, i)), whole((LIVE, width))],
        out_shape=[
            in_hbm((LIVE, features), jnp.bfloat16),
            in_hbm((LIVE, width), jnp.float32),
        ],
        compiler_params=grant(24),
        cost_estimate=cost(2 * LIVE * features * (tokens + width), 12),
        name="pick_rows",
    )(*far_away(pick, full, weight), *after)


def piece_specs(cols):
    return [pl.BlockSpec((128, cols), lambda i: (0, i))] * 4


def together(pieces):
    return jnp.concatenate([piece[...] for piece in pieces], axis=0)


def attend_back_kernel(
    p0, p1, p2, p3, out_grad_ref, w_ref, q_ref, k_ref, v_ref, bias_ref, lse_ref,
    low_ref, gq_ref, gk_ref, gv_ref, sum_ref, mixed, key_sum, value_sum,
):
    step = pl.program_id(0)
    hidden = together((p0, p1, p2, p3)) + out_grad_ref[...].astype(jnp.float32)
    low = hidden.astype(jnp.bfloat16)
    low_ref[...] = low
    product = back_dot(low, w_ref[...])

    @pl.when(step == 0)
    def _():
        mixed[...] = product

    @pl.when(step > 0)
    def _():
        mixed[...] += product

    @pl.when(step == pl.num_programs(0) - 1)
    def _():
        rows = LIVE
        width = q_ref.shape[1]
        lane = lax.broadcasted_iota(jnp.int32, (1, 128), 1)
        sum_ref[...] = jnp.zeros_like(sum_ref)
        for pair in range(width // 128):
            cols = slice(128 * pair, 128 * pair + 128)
            key_sum[...] = jnp.zeros_like(key_sum)
            value_sum[...] = jnp.zeros_like(value_sum)
            for part in range(LIVE // rows):
                here = slice(part * rows, part * rows + rows)
                bias = bias_ref[here, :]
                total = jnp.zeros((rows, 128), jnp.float32)
                for head in range(2):
                    inside = (lane // HEAD) == head
                    query = jnp.where(inside, q_ref[here, cols], 0)
                    grad = jnp.where(inside, mixed[here, cols], 0.0).astype(jnp.bfloat16)
                    first = 128 * pair + head * HEAD
                    logs = lse_ref[here, first : first + 1]
                    prob = jnp.exp(back_dot(query, k_ref[:, cols]) + bias - logs)
                    grad_prob = back_dot(grad, v_ref[:, cols])
                    inner = jnp.sum(prob * grad_prob, axis=-1, keepdims=True)
                    grad_scores = (prob * (grad_prob - inner)).astype(jnp.bfloat16)
                    total = jnp.where(inside, dot(grad_scores, k_ref[:, cols]), total)
                    key_sum[...] += outer_sum(grad_scores, query)
                    value_sum[...] += outer_sum(prob.astype(jnp.bfloat16), grad)
                grad_query = total.astype(jnp.bfloat16) * jnp.bfloat16(0.125)
                gq_ref[here, cols] = grad_query
                sum_ref[0:1, cols] += jnp.sum(
                    grad_query.astype(jnp.float32), axis=0, keepdims=True
                )
            gk_ref[:, cols] = key_sum[...].astype(jnp.bfloat16)
            grad_value = value_sum[...].astype(jnp.bfloat16)
            gv_ref[:, cols] = grad_value
            sum_ref[1:2, cols] = jnp.sum(grad_value.astype(jnp.float32), axis=0, keepdims=True)


def attend_back(pieces, out_grad, w_out, query, keys, values, bias, logs):
    cols, features = w_out.shape
    block = 1024
    wide = pl.BlockSpec((LIVE, block), lambda i: (0, i))
    heads = whole((LIVE, cols))
    shape = jax.ShapeDtypeStruct((LIVE, cols), jnp.bfloat16)
    return pl.pallas_call(
        attend_back_kernel,
        grid=(features // block,),
        in_specs=piece_specs(block)
        + [wide, pl.BlockSpec((cols, block), lambda i: (0, i))]
        + [heads] * 3
        + [whole((LIVE, LIVE)), heads],
        out_specs=[wide] + [heads] * 3 + [whole((8, cols))],
        out_shape=[jax.ShapeDtypeStruct((LIVE, features), jnp.bfloat16)]
        + [shape] * 3
        + [jax.ShapeDtypeStruct((8, cols), jnp.float32)],
        scratch_shapes=[pltpu.VMEM((LIVE, cols), jnp.float32)]
        + [pltpu.VMEM((LIVE, 128), jnp.float32)] * 2,
        compiler_params=grant(36),
        cost_estimate=cost(40 * LIVE * LIVE * 128, 11, 4 * LIVE * LIVE),
        name="attend_back",
    )(*pieces, *far_away(out_grad, w_out, query, keys, values, bias, logs))


def ffn_kernel(
    p0, p1, p2, p3, gain_ref, shift_ref, up_ref, bias_ref, grad_ref,
    act_ref, inner_ref, pre_ref, sum_ref, total,
):
    step = pl.program_id(0)
    act = (together((p0, p1, p2, p3)) * gain_ref[...] + shift_ref[...]).astype(jnp.bfloat16)
    act_ref[...] = act
    product = dot(act, up_ref[...])

    @pl.when(step == 0)
    def _():
        total[...] = product

    @pl.when(step > 0)
    def _():
        total[...] += product

    @pl.when(step == pl.num_programs(0) - 1)
    def _():
        sum_ref[...] = jnp.zeros_like(sum_ref)

        def some(i, carry):
            here = pl.ds(pl.multiple_of(i * 32, 32), 32)
            pre = total[here, :] + bias_ref[...]
            square = pre * pre
            bent = jnp.tanh(GELU_A * pre * (1.0 + GELU_B * square))
            half = 0.5 * (1.0 + bent)
            inner_ref[here, :] = (pre * half).astype(jnp.bfloat16)
            slope = half + 0.5 * GELU_A * pre * (1.0 - bent * bent) * (
                1.0 + 3.0 * GELU_B * square
            )
            grad = (slope * grad_ref[here, :]).astype(jnp.bfloat16)
            pre_ref[here, :] = grad
            sum_ref[...] += jnp.sum(grad.astype(jnp.float32).reshape(4, 8, -1), axis=0)
            return carry

        lax.fori_loop(0, LIVE // 32, some, 0)


def ffn(pieces, gain, shift, w_up, b_up, grad_inner):
    features, width = w_up.shape
    full = whole((LIVE, width))
    row = pl.BlockSpec((1, FFN_COLS), lambda i: (0, i))
    low = jax.ShapeDtypeStruct((LIVE, width), jnp.bfloat16)
    return pl.pallas_call(
        ffn_kernel,
        grid=(features // FFN_COLS,),
        in_specs=piece_specs(FFN_COLS)
        + [row, row, pl.BlockSpec((FFN_COLS, width), lambda i: (i, 0))]
        + [pl.BlockSpec((1, width), lambda i: (0, 0)), full],
        out_specs=[pl.BlockSpec((LIVE, FFN_COLS), lambda i: (0, i)), full, full]
        + [pl.BlockSpec((8, width), lambda i: (0, 0))],
        out_shape=[
            jax.ShapeDtypeStruct((LIVE, features), jnp.bfloat16),
            low,
            low,
            jax.ShapeDtypeStruct((8, width), jnp.float32),
        ],
        scratch_shapes=[pltpu.VMEM((LIVE, width), jnp.float32)],
        compiler_params=grant(30),
        cost_estimate=pl.CostEstimate(
            flops=2 * LIVE * features * width, bytes_accessed=16 << 20, transcendentals=LIVE * width
        ),
        name="ffn",
    )(*pieces, gain, shift, *far_away(w_up), b_up, *far_away(grad_inner))


def ffn_out_kernel(rows_ref, inner_ref, down_ref, extra_ref, bias_ref, *refs):
    out_ref, done_ref, ordered = refs[-3:]

    @pl.when(pl.program_id(0) == 0)
    def _():
        done_ref[...] = jnp.zeros_like(done_ref)
        for i in range(16):
            here = pl.ds(pl.multiple_of(rows_ref[i] * 32, 32), 32)
            ordered[32 * i : 32 * i + 32, :] = inner_ref[here, :]

    out_ref[...] = dot(ordered[...], down_ref[...])
    for i in range(2):
        here = pl.ds(pl.multiple_of(rows_ref[2 * i] * 32, 32), 32)
        out_ref[here, :] += extra_ref[32 * i : 32 * i + 32, :] + bias_ref[...]


def ffn_out(rows, inner, w_down, extra, bias, after):
    width, features = w_down.shape
    cols = 512
    return pl.pallas_call(
        ffn_out_kernel,
        grid_spec=pltpu.PrefetchScalarGridSpec(
            num_scalar_prefetch=1,
            grid=(features // cols,),
            in_specs=[
                whole((LIVE, width)),
                pl.BlockSpec((width, cols), lambda i, rows: (0, i)),
                pl.BlockSpec((64, cols), lambda i, rows: (0, i)),
                pl.BlockSpec((1, cols), lambda i, rows: (0, i)),
            ]
            + [ANYWHERE] * len(after),
            out_specs=[pl.BlockSpec((LIVE, cols), lambda i, rows: (0, i)), whole((8, 128))],
            scratch_shapes=[pltpu.VMEM((LIVE, width), jnp.bfloat16)],
        ),
        out_shape=[in_hbm((LIVE, features), jnp.float32), DONE],
        compiler_params=grant(24),
        cost_estimate=cost(2 * LIVE * features * width, 9),
        name="ffn_out",
    )(rows, inner, *far_away(w_down), extra, bias, *after)


def ffn_grads_kernel(act_ref, pre_ref, out_grad_ref, inner_ref, *refs):
    width = pre_ref.shape[1]
    out_ref, done_ref = refs[-2:]
    done_ref[...] = jnp.zeros_like(done_ref)
    out_ref[:, 0:width] = outer_sum(act_ref[...], pre_ref[...])
    out_ref[:, width : 2 * width] = outer_sum(out_grad_ref[...], inner_ref[...])


def ffn_grads(act, grad_pre, out_grad, inner, after):
    features, width = act.shape[1], grad_pre.shape[1]
    rows = 512
    left = pl.BlockSpec((LIVE, rows), lambda i: (0, i))
    right = whole((LIVE, width))
    return pl.pallas_call(
        ffn_grads_kernel,
        grid=(features // rows,),
        in_specs=[left, right, left, right] + [ANYWHERE] * len(after),
        out_specs=[pl.BlockSpec((rows, 2 * width), lambda i: (i, 0)), whole((8, 128))],
        out_shape=[in_hbm((features, 2 * width), jnp.float32), DONE],
        compiler_params=grant(28),
        cost_estimate=cost(4 * LIVE * features * width, 24),
        name="ffn_grads",
    )(*far_away(act), grad_pre, *far_away(out_grad), inner, *after)


UNITS = (136, 128, 128, 128)


def attn_grads_kernel(base, perm_ref, *refs):
    outs, done_ref = refs[-5:-1], refs[-1]
    norm_two_ref, heads_ref, up_ref, norm_one_a, norm_one_b = refs[8:13]
    done_ref[...] = jnp.zeros_like(done_ref)
    for i in range(4):
        outs[i][0:128, :] = outer_sum(refs[i][...], refs[4 + i][...])
    share = perm_ref[0, base + pl.program_id(0)]
    lane = iota((8, 128), 1)
    heads = heads_ref[:, pl.ds(pl.multiple_of((share >> 3) * 128, 128), 128)]
    heads = pltpu.roll(heads, 128 - 16 * (share & 7), 1)
    up = up_ref[:, pl.ds(pl.multiple_of((share >> 1) * 128, 128), 128)]
    up = pltpu.roll(up, 64 * (1 - (share & 1)), 1)
    up = jnp.broadcast_to(jnp.sum(up, axis=0, keepdims=True), (8, 128))
    own = jnp.where(lane < 16, heads, jnp.where(lane < 64, 0.0, up))
    outs[0][128:136, 128:256] = jnp.zeros((8, 128), jnp.float32)
    outs[0][128:130, 0:128] = norm_one_a[0:2, :] + norm_one_b[0:2, :]
    outs[0][130:134, 0:128] = norm_two_ref[0:4, :]
    outs[0][134:136, 0:128] = own[0:2, :]


def attn_grads(perm, lefts, rights, vectors, base, after):
    cols = rights[0].shape[1]

    at_share = pl.BlockSpec((8, 128), lambda j, perm: (0, perm[0, base + j]))

    def left_at(i):
        return pl.BlockSpec((LIVE, 128), lambda j, perm: (0, perm[i, base + j]))

    return pl.pallas_call(
        functools.partial(attn_grads_kernel, base),
        grid_spec=pltpu.PrefetchScalarGridSpec(
            num_scalar_prefetch=1,
            grid=(8,),
            in_specs=[left_at(i) for i in range(4)]
            + [whole((LIVE, cols))] * 4
            + [at_share, whole(vectors[1].shape), whole(vectors[2].shape), at_share, at_share]
            + [ANYWHERE] * len(after),
            out_specs=[pl.BlockSpec((unit, cols), lambda j, perm: (j, 0)) for unit in UNITS]
            + [whole((8, 128))],
        ),
        out_shape=[in_hbm((8 * unit, cols), jnp.float32) for unit in UNITS] + [DONE],
        compiler_params=grant(16),
        cost_estimate=cost(8 * LIVE * 1024 * cols, 8),
        name="attn_grads",
    )(perm, *lefts, *rights, *vectors, *after)


def halve_kernel(*refs):
    for i in range(4):
        refs[-4 + i][...] = refs[2 * i][...] + refs[2 * i + 1][...]


def halve(keeps, gots, shares, place, after=(), far=False):
    cols = keeps[0].shape[1]
    return pl.pallas_call(
        halve_kernel,
        grid=(1,),
        in_specs=[
            pl.BlockSpec((shares * unit, cols), lambda i: (place, 0)) for unit in UNITS for _ in (0, 1)
        ]
        + [ANYWHERE] * len(after),
        out_specs=[whole((shares * unit, cols)) for unit in UNITS],
        out_shape=[jax.ShapeDtypeStruct((shares * unit, cols), jnp.float32) for unit in UNITS],
        compiler_params=grant(14),
        cost_estimate=cost(4 * shares * 128 * cols, 12 * shares / 8),
        name="halve",
    )(*[array for pair in zip(far_away(*keeps) if far else keeps, gots) for array in pair], *after)


def last_kernel(*refs):
    outs = refs[-5:]
    both = refs[0][...] + refs[1][...]
    outs[0][...] = both[0:128]
    outs[4][...] = both[128:136, 0:128]
    for i in (1, 2):
        outs[i][...] = refs[2 * i][...] + refs[2 * i + 1][...]
    outs[3][...] = (refs[6][...] + refs[7][...]).T


def last_step(keeps, gots):
    cols = keeps[0].shape[1]
    specs = [whole((unit, cols)) for unit in UNITS for _ in (0, 1)]
    shapes = [(128, cols)] * 3 + [(cols, 128), (8, 128)]
    return pl.pallas_call(
        last_kernel,
        grid=(1,),
        in_specs=specs,
        out_specs=[whole(shape) for shape in shapes],
        out_shape=[in_hbm(shape, jnp.float32) for shape in shapes[:4]] + [DONE],
        compiler_params=grant(14),
        cost_estimate=cost(4 * 128 * cols, 1.5),
        name="last_step",
    )(*[array for pair in zip(keeps, gots) for array in pair])


def split_kernel(both_ref, first_ref, second_ref):
    width = first_ref.shape[1]
    first_ref[...] = both_ref[:, 0:width]
    second_ref[...] = both_ref[:, width : 2 * width].T


def split(both):
    rows, width = both.shape[0], both.shape[1] // 2
    return pl.pallas_call(
        split_kernel,
        grid=(1,),
        in_specs=[whole(both.shape)],
        out_specs=[whole((rows, width)), whole((width, rows))],
        out_shape=[in_hbm((rows, width), jnp.float32), in_hbm((width, rows), jnp.float32)],
        compiler_params=grant(14),
        cost_estimate=cost(0, 2),
        name="split",
    )(*far_away(both))


def spread_kernel(place_ref, whole_ref, live_ref, rows_ref, *refs):
    wide = dot(place_ref[...], rows_ref[...].astype(jnp.bfloat16)).astype(jnp.bfloat16)
    for first in range(0, wide.shape[1], 128):
        here = slice(first, first + 128)
        refs[-2][:, here] = jnp.where(live_ref[...] > 0, wide[:, here], whole_ref[:, here])
    refs[-1][...] = jnp.zeros_like(refs[-1])


def spread(place, full, live, rows, after=()):
    tokens, features = full.shape
    cols = 1024
    block = pl.BlockSpec((tokens, cols), lambda i: (0, i))
    return pl.pallas_call(
        spread_kernel,
        grid=(features // cols,),
        in_specs=[
            whole((tokens, LIVE)),
            block,
            whole((tokens, 128)),
            pl.BlockSpec((LIVE, cols), lambda i: (0, i)),
        ]
        + [ANYWHERE] * len(after),
        out_specs=[block, whole((8, 128))],
        out_shape=[in_hbm(full.shape, jnp.bfloat16), DONE],
        compiler_params=grant(24),
        cost_estimate=cost(2 * tokens * LIVE * features, 14),
        name="spread",
    )(place, *far_away(full), live, *far_away(rows), *after)


def local(
    tokens,
    cotangent,
    lengths,
    exits,
    w_query,
    b_query,
    w_key,
    w_value,
    b_value,
    w_out,
    b_out,
    gain_one,
    shift_one,
    gain_two,
    shift_two,
    w_up,
    b_up,
    w_down,
    b_down,
):
    f32, bf16 = jnp.float32, jnp.bfloat16
    bits = own_bits()
    at_dp = lax.axis_index("dp")
    y_high, z_high = at_dp >> 3, (at_dp >> 1) & 1
    y_gray, z_gray = ((at_dp >> 2) & 1) ^ y_high, (at_dp & 1) ^ z_high
    dp_bits = (y_gray, y_high, z_gray, z_high)

    def gathered_place(rank):
        side, one, two = (rank >> 6) & 1, (rank >> 7) & 1, (rank >> 5) & 1
        gray, high = jnp.where(side == 1, two, one), jnp.where(side == 1, one, two)
        owner = 4 * high + 2 * (gray ^ high) + (rank >> 8)
        return 64 * owner + 32 * side + (rank & 31)

    def dp_blocks(order):
        own = jnp.arange(16, dtype=jnp.int32)
        bits = [None] * 4
        for place, (_, bit) in enumerate(order):
            bits[bit] = ((own >> (3 - place)) & 1) ^ dp_bits[bit]
        return 4 * (2 * bits[1] + (bits[0] ^ bits[1])) + 2 * bits[3] + (bits[2] ^ bits[3])

    perm = jnp.stack([dp_blocks(order) for order in ORDERS])

    gain_one_f, gain_two_f = gain_one.astype(f32)[None], gain_two.astype(f32)[None]
    pick, bias, source_low, act_one, normal_low, query, keys, values, attended, logs = front(
        lengths,
        exits,
        tokens,
        gain_one,
        shift_one,
        (w_query, w_key, w_value),
        b_query,
        b_value,
    )

    source_mine = jnp.concatenate([source_low[0:32], source_low[64:96]], axis=0).astype(f32)
    normal_one, scale_one = normed(source_mine)
    scale_one = jnp.broadcast_to(scale_one, (64, 128))
    picked = []

    def beside(far_a):
        picked.extend(pick_rows(pick, cotangent, w_down, (far_a,)))
        return picked[1:]

    terms_a, terms_b, _ = scatter_rows((attended,), (w_out,), False, None, beside)
    grad_out_low, grad_inner = picked
    hidden_mine, normal_a, normal_b, scale_two = norm_two(
        terms_a + [(source_low, 0)], terms_b + [(source_low, 2)], b_out.astype(f32)[None]
    )
    place_all = jnp.arange(tokens.shape[0], dtype=jnp.int32)
    living = exits > LAYER
    below = (place_all[None, :] <= place_all[:, None]) & living[None, :]
    rank = jnp.sum(jnp.where(below, 1, 0), axis=1) - 1
    own_index = jnp.arange(LIVE, dtype=jnp.int32)
    living_column = jnp.broadcast_to(living.astype(bf16)[:, None], (tokens.shape[0], 128))
    rows_of = own_place(32 * own_index[:16], bits) >> 5
    ranked = jnp.where(living, rank, -1)
    place_ranked = (ranked[:, None] == own_index[None, :]).astype(bf16)
    gathered = jnp.where(living, gathered_place(rank), -1)
    place_gathered = (gathered[:, None] == own_index[None, :]).astype(bf16)
    perm, living_column, rows_of, place_ranked, place_gathered, normal_b = (
        lax.optimization_barrier(
            (perm, living_column, rows_of, place_ranked, place_gathered, normal_b)
        )
    )

    act_two, inner, grad_pre, sum_up = ffn(
        gather_rows(normal_a, normal_b),
        gain_two_f,
        shift_two.astype(f32)[None],
        w_up,
        b_up.astype(f32)[None],
        grad_inner,
    )
    ffn_sums = []

    def early(sent, own):
        ffn_sums.extend(ffn_grads(act_two, grad_pre, grad_out_low, inner, own[0:1]))
        return ffn_sums[1:2]

    terms_a, terms_b, sent = scatter_rows((grad_pre,), (w_up,), True, early)
    ffn_both, _ = ffn_sums
    ffn_part, ffn_part_done = ffn_out(
        rows_of, inner, w_down, hidden_mine, b_down.astype(f32)[None], sent
    )
    ffn_share = lax.psum_scatter(ffn_both, "dp", scatter_dimension=0, tiled=True)
    output_live = lax.psum(ffn_part, "tensor")

    norm_a, norm_b, grad_hidden_mine, sums_two = norm_back(
        terms_a,
        terms_b,
        ((normal_a, 0), (normal_b, 0)),
        ((grad_out_low, 0), (grad_out_low, 2)),
        scale_two,
        gain_two_f,
        (ffn_part_done,),
    )
    grad_attn_low, grad_query, grad_key, grad_value, sums_heads = attend_back(
        gather_rows(norm_a, norm_b), grad_out_low, w_out, query, keys, values, bias, logs
    )
    rights = (grad_query, grad_key, grad_value, attended)
    lefts = (act_one, act_one, act_one, grad_attn_low)

    vectors, sends, keeps = [sums_two, sums_heads, sum_up], [], []

    def early(sent, own):
        vectors.extend([sent[2], own[2]])
        sends.extend(attn_grads(perm, lefts, rights, vectors, 8, ()))
        return sends[-1:]

    def beside(far_a):
        keeps.extend(attn_grads(perm, lefts, rights, vectors, 0, (far_a,)))
        return keeps[-1:]

    terms_a, terms_b, _ = scatter_rows(
        rights[:3], (w_query, w_key, w_value), True, early, beside, normal_low
    )
    *keeps, keeps_done = keeps
    *sent, _ = sends

    def exchange(step):
        return [over_dp(value, order[step][0]) for value, order in zip(sent, ORDERS)]

    gots = exchange(0)
    share_up, share_down = split(ffn_share)
    output_rows, spread_done = spread(
        place_ranked, tokens, living_column, output_live, (keeps_done, share_up)
    )
    sent = halve(keeps, gots, 4, 1, (), True)
    keeps = halve(keeps, gots, 4, 0, sent[:1], True)
    _, _, input_mine, _ = norm_back(
        terms_a,
        terms_b,
        ((normal_one, 0), (normal_one, 1)),
        ((grad_hidden_mine, 0), (grad_hidden_mine, 1)),
        scale_one,
        gain_one_f,
        sent[:1],
    )
    input_live = lax.all_gather(input_mine, "tensor", axis=0, tiled=True)
    gots = exchange(1)
    sent = halve(keeps, gots, 2, 1, (spread_done,))
    keeps = halve(keeps, gots, 2, 0, sent[:1])
    gots = exchange(2)
    sent = halve(keeps, gots, 1, 1)
    keeps = halve(keeps, gots, 1, 0, sent[:1])
    gots = exchange(3)
    *attn_shares, own_share = last_step(keeps, gots)
    common_share = own_share
    for pairs in (CORE, X_NEAR, X_FAR):
        common_share = common_share + over_tensor(common_share, pairs)
    input_rows, _ = spread(place_gathered, cotangent, living_column, input_live)

    return (
        output_rows,
        input_rows,
        attn_shares[0],
        own_share[6, 0:16],
        attn_shares[1],
        attn_shares[2],
        own_share[7, 0:16],
        attn_shares[3],
        common_share[4],
        common_share[0],
        common_share[1],
        common_share[2],
        common_share[3],
        share_up,
        own_share[6, 64:128],
        share_down,
        common_share[5],
    )


def solution(mesh):
    in_specs = (
        P("dp", None),
        P("dp", None),
        P("dp", None),
        P("dp"),
        P(None, "tensor"),
        P("tensor"),
        P(None, "tensor"),
        P(None, "tensor"),
        P("tensor"),
        P("tensor", None),
        P(),
        P(),
        P(),
        P(),
        P(),
        P(None, "tensor"),
        P("tensor"),
        P("tensor", None),
        P(),
    )
    out_specs = (
        P("dp", None),
        P("dp", None),
        P("dp", "tensor"),
        P(("tensor", "dp")),
        P("dp", "tensor"),
        P("dp", "tensor"),
        P(("tensor", "dp")),
        P("tensor", "dp"),
        P("dp"),
        P("dp"),
        P("dp"),
        P("dp"),
        P("dp"),
        P("dp", "tensor"),
        P(("tensor", "dp")),
        P("tensor", "dp"),
        P("dp"),
    )
    return jax.shard_map(local, mesh=mesh, in_specs=in_specs, out_specs=out_specs, check_vma=False)
```

```python
import functools

import jax
import jax.numpy as jnp
from jax import lax
from jax.experimental import pallas as pl
from jax.experimental.pallas import tpu as pltpu
from jax.sharding import PartitionSpec as P

HEAD = 64
LAYER = 12
LIVE = 512
FFN_COLS = 1024
NEG_BIG = -1e30
EPSILON = 1e-05
GELU_A = 0.7978845608028654
GELU_B = 0.044715

CORE = [(i, i ^ 1) for i in range(8)]
X_NEAR = [(2 * x + c, 2 * (x ^ 1) + c) for x in range(4) for c in range(2)]
X_FAR = [(2 * x + c, 2 * (3 - x) + c) for x in range(4) for c in range(2)]
Y_NEAR = [(4 * y + z, 4 * (y ^ 1) + z) for y in range(4) for z in range(4)]
Y_FAR = [(4 * y + z, 4 * (3 - y) + z) for y in range(4) for z in range(4)]
Z_NEAR = [(4 * y + z, 4 * y + (z ^ 1)) for y in range(4) for z in range(4)]
Z_FAR = [(4 * y + z, 4 * y + (3 - z)) for y in range(4) for z in range(4)]
HALVES = ((Y_NEAR, 0), (Y_FAR, 1), (Z_NEAR, 2), (Z_FAR, 3))


def over_tensor(value, pairs):
    return lax.ppermute(value, "tensor", pairs)


def over_dp(value, pairs):
    return lax.ppermute(value, "dp", pairs)


def dot(left, right):
    return jnp.dot(left, right, preferred_element_type=jnp.float32)


def back_dot(left, right):
    return lax.dot_general(
        left, right, (((1,), (1,)), ((), ())), preferred_element_type=jnp.float32
    )


def outer_sum(left, right):
    return lax.dot_general(
        left, right, (((0,), (0,)), ((), ())), preferred_element_type=jnp.float32
    )


def normed(values):
    average = jnp.mean(values, axis=-1, keepdims=True)
    centred = values - average
    spread = jnp.mean(centred * centred, axis=-1, keepdims=True)
    scale = lax.rsqrt(spread + EPSILON)
    return centred * scale, scale


def grant(mib, **more):
    return pltpu.CompilerParams(vmem_limit_bytes=mib << 20, **more)


def cost(flops, mib, transcendentals=0):
    return pl.CostEstimate(
        flops=flops, bytes_accessed=int(mib * 1048576), transcendentals=transcendentals
    )


ANYWHERE = pl.BlockSpec(memory_space=pl.ANY)


def far_away(*values):
    return [pltpu.with_memory_space_constraint(value, pltpu.HBM) for value in values]


def in_hbm(shape, dtype):
    return pltpu.HBM(shape, dtype)


DONE = jax.ShapeDtypeStruct((8, 128), jnp.float32)


def whole(shape):
    return pl.BlockSpec(shape, lambda *i: (0,) * len(shape))


def parts_kernel(transposed, left_ref, right_ref, *refs):
    total = (back_dot if transposed else dot)(left_ref[...], right_ref[...])
    first, second = refs[-2:]
    first[...] = total[0:128]
    second[...] = total[128:256]


def parts(lefts, rights, transposed, half, after=()):
    (left,), (right,) = lefts, rights
    depth = left.shape[1]
    features = right.shape[0 if transposed else 1]
    cols = 512
    block = (
        pl.BlockSpec((cols, depth), lambda i: (i, 0))
        if transposed
        else pl.BlockSpec((depth, cols), lambda i: (0, i))
    )
    return pl.pallas_call(
        functools.partial(parts_kernel, transposed),
        grid=(features // cols,),
        in_specs=[pl.BlockSpec((256, depth), lambda i: (half, 0)), block] + [ANYWHERE] * len(after),
        out_specs=[pl.BlockSpec((128, cols), lambda i: (0, i))] * 2,
        out_shape=[jax.ShapeDtypeStruct((128, features), jnp.float32)] * 2,
        compiler_params=grant(9),
        cost_estimate=cost(2 * 256 * depth * features, 6),
        name="parts",
    )(left, right, *after)


def all_parts_kernel(count, *refs):
    total = None
    for left, right in zip(refs[:count], refs[count : 2 * count]):
        product = back_dot(left[...], right[...])
        total = product if total is None else total + product
    normal_ref, sum_ref = refs[2 * count], refs[-1]
    sum_ref[...] = jnp.zeros_like(sum_ref)
    sum_ref[0:1, :] = jnp.sum(total * normal_ref[...].astype(jnp.float32), axis=0, keepdims=True)
    sum_ref[1:2, :] = jnp.sum(total, axis=0, keepdims=True)
    for i in range(4):
        refs[2 * count + 1 + i][...] = total[128 * i : 128 * i + 128]


def all_parts(lefts, rights, normal):
    count, depth = len(lefts), lefts[0].shape[1]
    features = rights[0].shape[0]
    cols = 1024
    return pl.pallas_call(
        functools.partial(all_parts_kernel, count),
        grid=(features // cols,),
        in_specs=[whole((LIVE, depth))] * count
        + [pl.BlockSpec((cols, depth), lambda i: (i, 0))] * count
        + [pl.BlockSpec((LIVE, cols), lambda i: (0, i))],
        out_specs=[pl.BlockSpec((128, cols), lambda i: (0, i))] * 4
        + [pl.BlockSpec((8, cols), lambda i: (0, i))],
        out_shape=[jax.ShapeDtypeStruct((128, features), jnp.float32)] * 4
        + [jax.ShapeDtypeStruct((8, features), jnp.float32)],
        compiler_params=grant(26),
        cost_estimate=cost(2 * LIVE * depth * count * features, 10),
        name="all_parts",
    )(*far_away(*lefts, *rights, normal))


def add_kernel(counts, *refs):
    outs = refs[-len(counts) :]
    first = 0
    for out_ref, count in zip(outs, counts):
        out_ref[...] = summed(refs[first : first + count])
        first += count


def add(sums, rows, after=()):
    features = sums[0][0][0].shape[1]
    cols = 1024
    return pl.pallas_call(
        functools.partial(add_kernel, [len(terms) for terms in sums]),
        grid=(features // cols,),
        in_specs=[
            pl.BlockSpec((rows, cols), lambda i, block=block: (block, i))
            for terms in sums
            for _, block in terms
        ]
        + [ANYWHERE] * len(after),
        out_specs=[pl.BlockSpec((rows, cols), lambda i: (0, i))] * len(sums),
        out_shape=[jax.ShapeDtypeStruct((rows, features), jnp.float32)] * len(sums),
        compiler_params=grant(6),
        cost_estimate=cost(0, 2),
        name="add",
    )(*[array for terms in sums for array, _ in terms], *after)


def scatter_begin(pieces, early=None):
    near, far = pieces[0:2]
    core_far = over_tensor(pieces[3], CORE)
    core_near = over_tensor(pieces[2], CORE)
    done = early() if early else ()
    far_a, far_b = add([[(far, i), (core_far, i)] for i in range(2)], 64, (*done, core_near))
    got_a = over_tensor(far_a, X_NEAR)
    got_b = over_tensor(far_b, X_FAR)
    return near, core_near, got_a, got_b, far_a


def scatter_end(begun, after=()):
    near, core_near, got_a, got_b, _ = begun
    sends = [
        add([[(near, block), (core_near, block), (got, 1)]], 32, after)[0]
        for got, block in ((got_a, 1), (got_b, 3))
    ]
    last_a, last_b = [over_tensor(send, pairs) for send, pairs in zip(sends, (X_FAR, X_NEAR))]
    return (
        [(near, 0), (core_near, 0), (got_a, 0), (last_a, 0)],
        [(near, 2), (core_near, 2), (got_b, 0), (last_b, 0)],
        sends,
    )


def both_parts(left, right, transposed, after=()):
    sent = parts((left,), (right,), transposed, 1, after)
    return [*parts((left,), (right,), transposed, 0, sent[0:1]), *sent]


def join_kernel(*refs):
    rows = refs[0].shape[0]
    for i in range(4):
        refs[4][rows * i : rows * i + rows, :] = refs[i][...]


def join(pieces):
    rows, features = pieces[0].shape
    cols = 512
    return pl.pallas_call(
        join_kernel,
        grid=(features // cols,),
        in_specs=[pl.BlockSpec((rows, cols), lambda i: (0, i))] * 4,
        out_specs=pl.BlockSpec((4 * rows, cols), lambda i: (0, i)),
        out_shape=jax.ShapeDtypeStruct((4 * rows, features), jnp.float32),
        compiler_params=grant(5),
        cost_estimate=cost(0, 2),
        name="join",
    )(*pieces)


def gather_rows(mine_a, mine_b):
    a01 = over_tensor(mine_a, X_FAR)
    b01 = over_tensor(mine_b, X_NEAR)
    a10 = over_tensor(mine_a, X_NEAR)
    b10 = over_tensor(mine_b, X_FAR)
    a11 = over_tensor(a01, X_NEAR)
    b11 = over_tensor(b01, X_FAR)
    first = join((mine_a, a01, mine_b, b01))
    second = join((a10, a11, b10, b11))
    return (first, second, over_tensor(first, CORE), over_tensor(second, CORE)), (a11, b11)


def row_block(pair, features):
    return pl.BlockSpec((32, features), lambda i, block=pair[1]: (block, 0))


def summed(refs):
    return sum(ref[...].astype(jnp.float32) for ref in refs[1:]) + refs[0][...]


def norm_two_kernel(*refs):
    bias_ref, hidden_ref, scale_ref = refs[10], refs[11], refs[14]
    for i in range(2):
        here = slice(32 * i, 32 * i + 32)
        hidden = summed(refs[5 * i : 5 * i + 5]) + bias_ref[...]
        normal, scale = normed(hidden)
        hidden_ref[here, :] = hidden
        refs[12 + i][...] = normal
        scale_ref[here, :] = jnp.broadcast_to(scale, (32, 128))


def norm_two(terms_a, terms_b, bias):
    features = bias.shape[1]
    terms = terms_a + terms_b
    piece = jax.ShapeDtypeStruct((32, features), jnp.float32)
    return pl.pallas_call(
        norm_two_kernel,
        grid=(1,),
        in_specs=[row_block(term, features) for term in terms] + [whole((1, features))],
        out_specs=[whole((64, features)), whole((32, features)), whole((32, features)), whole((64, 128))],
        out_shape=[
            jax.ShapeDtypeStruct((64, features), jnp.float32),
            piece,
            piece,
            jax.ShapeDtypeStruct((64, 128), jnp.float32),
        ],
        compiler_params=grant(8),
        cost_estimate=cost(20 * 64 * features, 4),
        name="norm_two",
    )(*[term[0] for term in terms], bias)


def last_rows_kernel(*refs):
    hidden_ref, bias_ref, input_ref = refs[8:11]
    for i in range(2):
        here = slice(32 * i, 32 * i + 32)
        out_ref = refs[-2 + i]
        out_ref[0:32, :] = summed(refs[4 * i : 4 * i + 4]) + (hidden_ref[here, :] + bias_ref[...])
        out_ref[32:64, :] = input_ref[here, :]


def last_rows(terms_a, terms_b, hidden, bias, input_mine):
    features = bias.shape[1]
    terms = terms_a + terms_b
    rows = whole((64, features))
    return pl.pallas_call(
        last_rows_kernel,
        grid=(1,),
        in_specs=[row_block(term, features) for term in terms] + [rows, whole((1, features)), rows],
        out_specs=[rows] * 2,
        out_shape=[jax.ShapeDtypeStruct((64, features), jnp.float32)] * 2,
        compiler_params=grant(12),
        cost_estimate=cost(20 * 64 * features, 4),
        name="last_rows",
    )(*[term[0] for term in terms], hidden, bias, input_mine)


def norm_back_kernel(*refs):
    scale_ref, gain_ref = refs[12:14]
    pieces, total_ref, sums_ref = refs[-4:-2], refs[-2], refs[-1]
    sums_ref[...] = jnp.zeros_like(sums_ref)
    for i in range(2):
        here = slice(32 * i, 32 * i + 32)
        grad = summed(refs[4 * i : 4 * i + 4])
        normal = refs[8 + 2 * i][...]
        base = refs[9 + 2 * i][...].astype(jnp.float32)
        scaled = grad * gain_ref[...]
        first = jnp.mean(scaled, axis=-1, keepdims=True)
        second = jnp.mean(scaled * normal, axis=-1, keepdims=True)
        norm = scale_ref[here, 0:1] * (scaled - first - normal * second)
        total = base + norm
        pieces[i][...] = total
        total_ref[here, :] = total
        sums_ref[0:1, :] += jnp.sum(grad * normal, axis=0, keepdims=True)
        sums_ref[1:2, :] += jnp.sum(grad, axis=0, keepdims=True)
        sums_ref[2:3, :] += jnp.sum(total, axis=0, keepdims=True)
        sums_ref[3:4, :] += jnp.sum(base, axis=0, keepdims=True)


def norm_back(terms_a, terms_b, normals, bases, scale, gain, after=()):
    features = gain.shape[1]
    terms = terms_a + terms_b + [normals[0], bases[0], normals[1], bases[1]]
    piece = jax.ShapeDtypeStruct((32, features), jnp.float32)
    return pl.pallas_call(
        norm_back_kernel,
        grid=(1,),
        in_specs=[row_block(term, features) for term in terms]
        + [whole((64, 128)), whole((1, features))]
        + [ANYWHERE] * len(after),
        out_specs=[whole((32, features))] * 2 + [whole((64, features)), whole((8, features))],
        out_shape=[
            piece,
            piece,
            jax.ShapeDtypeStruct((64, features), jnp.float32),
            jax.ShapeDtypeStruct((8, features), jnp.float32),
        ],
        compiler_params=grant(8),
        cost_estimate=cost(20 * 64 * features, 4),
        name="norm_back",
    )(*[term[0] for term in terms], scale, gain, *after)


def own_bits():
    at = lax.axis_index("tensor")
    high = at >> 2
    return at & 1, ((at >> 1) & 1) ^ high, high


def own_place(rank, bits):
    core, gray, high = bits
    side = (rank >> 6) & 1
    one = side * high + (1 - side) * gray
    two = side * gray + (1 - side) * high
    return rank ^ (core << 8) ^ (one << 7) ^ (two << 5)


def iota(shape, axis):
    return lax.broadcasted_iota(jnp.int32, shape, axis)


def live_ranks(exits):
    living = exits > LAYER
    ones = jnp.where(living, 1.0, 0.0)
    up_to = (iota((128, 128), 0) <= iota((128, 128), 1)).astype(jnp.bfloat16)
    within = dot(ones.astype(jnp.bfloat16), up_to)
    totals = jnp.broadcast_to(jnp.sum(ones, axis=1, keepdims=True), (8, 128))
    before = jnp.zeros((8, 128), jnp.float32)
    for i in range(7):
        before += jnp.where(iota((8, 128), 0) > i, totals[i : i + 1, :], 0.0)
    return living, (within + before).astype(jnp.int32) - 1


def front_kernel(
    lengths_ref, exits_ref, tokens_ref, gain_ref, shift_ref, wq_hbm, wk_hbm, wv_hbm, bq_ref, bv_ref,
    pick_hbm, bias_hbm, source_ref, act_hbm, normal_hbm, q_ref, k_ref, v_ref, out_ref, lse_ref,
    rows_ref, w_ref, pick_ref, bias_ref, act_ref, normal_ref, sems, out_sems,
):
    step = pl.program_id(0)
    copies = [
        pltpu.make_async_copy(
            weight, w_ref.at[:, pl.ds(i * weight.shape[1], weight.shape[1])], sems.at[i]
        )
        for i, weight in enumerate((wq_hbm, wk_hbm, wv_hbm))
    ]
    outs = [
        pltpu.make_async_copy(here, there, out_sems.at[i])
        for i, (here, there) in enumerate(
            (
                (pick_ref, pick_hbm),
                (bias_ref, bias_hbm),
                (act_ref, act_hbm),
                (normal_ref, normal_hbm),
            )
        )
    ]

    @pl.when(step == 0)
    def _():
        for copy in copies:
            copy.start()
        bits = own_bits()
        living, rank = live_ranks(exits_ref[...])
        row_of = jnp.where(living, own_place(rank, bits), -1)
        for i in range(8):
            pick_ref[:, 128 * i : 128 * i + 128] = jnp.where(
                iota((LIVE, 128), 0) == row_of[i : i + 1, :], 1.0, 0.0
            ).astype(jnp.bfloat16)
        token = 128 * iota((8, 128), 0) + iota((8, 128), 1)
        rank_row = own_place(iota((1, LIVE), 1), bits)
        rank_column = own_place(iota((LIVE, 1), 0), bits)
        segment_row, segment_column = jnp.zeros_like(rank_row), jnp.zeros_like(rank_column)
        bound = 0
        for i in range(lengths_ref.shape[1] - 1):
            bound = bound + lengths_ref[0, i]
            count = jnp.sum(jnp.where(living & (token < bound), 1, 0))
            segment_row += (rank_row >= count).astype(jnp.int32)
            segment_column += (rank_column >= count).astype(jnp.int32)
        allowed = (segment_column == segment_row) & (rank_row <= rank_column)
        bias_ref[...] = jnp.where(allowed, 0.0, NEG_BIG)
        for out in outs[:2]:
            out.start()

    cols = tokens_ref.shape[1]
    found = dot(pick_ref[...], tokens_ref[...]).astype(jnp.bfloat16)
    source_ref[...] = found
    for i in range(2):

        @pl.when(step == i)
        def _(i=i):
            rows_ref[:, cols * i : cols * i + cols] = found

    @pl.when(step == pl.num_programs(0) - 1)
    def _():
        gain, shift = wide_row(gain_ref), wide_row(shift_ref)

        def some(i, carry):
            here = pl.ds(pl.multiple_of(i * 16, 16), 16)
            normal, _ = normed(rows_ref[here, :].astype(jnp.float32))
            normal_ref[here, :] = normal.astype(jnp.bfloat16)
            act_ref[here, :] = (normal * gain + shift).astype(jnp.bfloat16)
            return carry

        lax.fori_loop(0, LIVE // 16, some, 0, unroll=8)
        for out in outs[2:]:
            out.start()
        for copy in copies:
            copy.wait()
        width = q_ref.shape[1]
        product = dot(act_ref[...], w_ref[...])
        q_ref[...] = ((product[:, 0:width] + wide_row(bq_ref)) * 0.125).astype(jnp.bfloat16)
        k_ref[...] = product[:, width : 2 * width].astype(jnp.bfloat16)
        v_ref[...] = (product[:, 2 * width :] + wide_row(bv_ref)).astype(jnp.bfloat16)
        rows = LIVE
        lane = iota((1, 128), 1)
        for pair in range(q_ref.shape[1] // 128):
            at = slice(128 * pair, 128 * pair + 128)
            for part in range(LIVE // rows):
                here = slice(part * rows, part * rows + rows)
                bias = bias_ref[here, :]
                total = jnp.zeros((rows, 128), jnp.float32)
                logs = jnp.zeros((rows, 128), jnp.float32)
                for head in range(2):
                    inside = (lane // HEAD) == head
                    query = jnp.where(inside, q_ref[here, at], 0)
                    scores = back_dot(query, k_ref[:, at]) + bias
                    peak = jnp.max(scores, axis=-1, keepdims=True)
                    expo = jnp.exp(scores - peak)
                    total_expo = jnp.sum(expo, axis=-1, keepdims=True)
                    prob = (expo * (1.0 / total_expo)).astype(jnp.bfloat16)
                    total = jnp.where(inside, dot(prob, v_ref[:, at]), total)
                    logs = jnp.where(inside, peak + jnp.log(total_expo), logs)
                out_ref[here, at] = total.astype(jnp.bfloat16)
                lse_ref[here, at] = logs
        for out in outs:
            out.wait()


def wide_row(ref):
    return ref[...].astype(jnp.float32).reshape(1, -1)


def front(lengths, exits, tokens, gain, shift, weights, b_query, b_value):
    features, cols = weights[0].shape
    rows = tokens.shape[0]
    block = features // 2
    low = jax.ShapeDtypeStruct((LIVE, cols), jnp.bfloat16)
    row = whole((features,))
    heads = whole((LIVE, cols))
    return pl.pallas_call(
        front_kernel,
        grid=(2,),
        in_specs=[
            pl.BlockSpec(memory_space=pltpu.SMEM),
            whole((8, rows // 8)),
            pl.BlockSpec((rows, block), lambda i: (0, i)),
            row,
            row,
        ]
        + [ANYWHERE] * 3
        + [whole((cols,))] * 2,
        out_specs=[ANYWHERE] * 2
        + [pl.BlockSpec((LIVE, block), lambda i: (0, i))]
        + [ANYWHERE] * 2
        + [heads] * 5,
        out_shape=[
            in_hbm((LIVE, rows), jnp.bfloat16),
            in_hbm((LIVE, LIVE), jnp.float32),
        ]
        + [in_hbm((LIVE, features), jnp.bfloat16)] * 3
        + [in_hbm((LIVE, cols), jnp.bfloat16)] * 3
        + [low]
        + [in_hbm((LIVE, cols), jnp.float32)],
        scratch_shapes=[
            pltpu.VMEM((LIVE, features), jnp.bfloat16),
            pltpu.VMEM((features, 3 * cols), jnp.bfloat16),
            pltpu.VMEM((LIVE, rows), jnp.bfloat16),
            pltpu.VMEM((LIVE, LIVE), jnp.float32),
            pltpu.VMEM((LIVE, features), jnp.bfloat16),
            pltpu.VMEM((LIVE, features), jnp.bfloat16),
            pltpu.SemaphoreType.DMA((3,)),
            pltpu.SemaphoreType.DMA((4,)),
        ],
        compiler_params=grant(44),
        cost_estimate=cost(
            2 * LIVE * features * (rows + 3 * cols) + 16 * LIVE * LIVE * 128, 16, 4 * LIVE * LIVE
        ),
        name="front",
    )(
        lengths,
        *far_away(
            exits.reshape(8, rows // 8), tokens, gain, shift, *weights, b_query, b_value
        ),
    )


def pick_rows_kernel(pick_ref, full_ref, w_ref, *refs):
    rows_ref, product_ref = refs[-2:]
    rows = dot(pick_ref[...], full_ref[...]).astype(jnp.bfloat16)
    rows_ref[...] = rows
    product = back_dot(rows, w_ref[...])

    @pl.when(pl.program_id(0) == 0)
    def _():
        product_ref[...] = product

    @pl.when(pl.program_id(0) > 0)
    def _():
        product_ref[...] += product


def pick_rows(pick, full, weight, after):
    tokens, features = full.shape
    width = weight.shape[0]
    cols = 512
    return pl.pallas_call(
        pick_rows_kernel,
        grid=(features // cols,),
        in_specs=[
            whole((LIVE, tokens)),
            pl.BlockSpec((tokens, cols), lambda i: (0, i)),
            pl.BlockSpec((width, cols), lambda i: (0, i)),
        ]
        + [ANYWHERE] * len(after),
        out_specs=[pl.BlockSpec((LIVE, cols), lambda i: (0, i)), whole((LIVE, width))],
        out_shape=[
            in_hbm((LIVE, features), jnp.bfloat16),
            in_hbm((LIVE, width), jnp.float32),
        ],
        compiler_params=grant(18),
        cost_estimate=cost(2 * LIVE * features * (tokens + width), 12),
        name="pick_rows",
    )(*far_away(pick, full, weight), *after)


def piece_specs(cols):
    return [pl.BlockSpec((128, cols), lambda i: (0, i))] * 4


def together(pieces):
    return jnp.concatenate([piece[...] for piece in pieces], axis=0)


def attend_back_kernel(
    p0, p1, p2, p3, w_ref, q_ref, k_ref, v_ref, bias_ref, lse_ref, after_ref,
    low_ref, gq_ref, gk_ref, gv_ref, sum_ref, mixed, key_sum, value_sum,
):
    step = pl.program_id(0)
    low = together((p0, p1, p2, p3)).astype(jnp.bfloat16)
    low_ref[...] = low
    product = back_dot(low, w_ref[...])

    @pl.when(step == 0)
    def _():
        mixed[...] = product

    @pl.when(step > 0)
    def _():
        mixed[...] += product

    @pl.when(step == pl.num_programs(0) - 1)
    def _():
        rows = LIVE
        width = q_ref.shape[1]
        lane = lax.broadcasted_iota(jnp.int32, (1, 128), 1)
        sum_ref[...] = jnp.zeros_like(sum_ref)
        for pair in range(width // 128):
            cols = slice(128 * pair, 128 * pair + 128)
            key_sum[...] = jnp.zeros_like(key_sum)
            value_sum[...] = jnp.zeros_like(value_sum)
            for part in range(LIVE // rows):
                here = slice(part * rows, part * rows + rows)
                bias = bias_ref[here, :]
                total = jnp.zeros((rows, 128), jnp.float32)
                for head in range(2):
                    inside = (lane // HEAD) == head
                    query = jnp.where(inside, q_ref[here, cols], 0)
                    grad = jnp.where(inside, mixed[here, cols], 0.0).astype(jnp.bfloat16)
                    first = 128 * pair + head * HEAD
                    logs = lse_ref[here, first : first + 1]
                    prob = jnp.exp(back_dot(query, k_ref[:, cols]) + bias - logs)
                    grad_prob = back_dot(grad, v_ref[:, cols])
                    inner = jnp.sum(prob * grad_prob, axis=-1, keepdims=True)
                    grad_scores = (prob * (grad_prob - inner)).astype(jnp.bfloat16)
                    total = jnp.where(inside, dot(grad_scores, k_ref[:, cols]), total)
                    key_sum[...] += outer_sum(grad_scores, query)
                    value_sum[...] += outer_sum(prob.astype(jnp.bfloat16), grad)
                grad_query = total.astype(jnp.bfloat16) * jnp.bfloat16(0.125)
                gq_ref[here, cols] = grad_query
                sum_ref[0:1, cols] += jnp.sum(
                    grad_query.astype(jnp.float32), axis=0, keepdims=True
                )
            gk_ref[:, cols] = key_sum[...].astype(jnp.bfloat16)
            grad_value = value_sum[...].astype(jnp.bfloat16)
            gv_ref[:, cols] = grad_value
            sum_ref[1:2, cols] = jnp.sum(grad_value.astype(jnp.float32), axis=0, keepdims=True)


def attend_back(pieces, w_out, query, keys, values, bias, logs, after):
    cols, features = w_out.shape
    block = 1024
    wide = pl.BlockSpec((LIVE, block), lambda i: (0, i))
    heads = whole((LIVE, cols))
    return pl.pallas_call(
        attend_back_kernel,
        grid=(features // block,),
        in_specs=piece_specs(block)
        + [pl.BlockSpec((cols, block), lambda i: (0, i))]
        + [heads] * 3
        + [whole((LIVE, LIVE)), heads, ANYWHERE],
        out_specs=[wide] + [heads] * 3 + [whole((8, cols))],
        out_shape=[in_hbm((LIVE, features), jnp.bfloat16)]
        + [in_hbm((LIVE, cols), jnp.bfloat16)] * 3
        + [jax.ShapeDtypeStruct((8, cols), jnp.float32)],
        scratch_shapes=[pltpu.VMEM((LIVE, cols), jnp.float32)]
        + [pltpu.VMEM((LIVE, 128), jnp.float32)] * 2,
        compiler_params=grant(26),
        cost_estimate=cost(40 * LIVE * LIVE * 128, 11, 4 * LIVE * LIVE),
        name="attend_back",
    )(*pieces, *far_away(w_out, query, keys, values, bias, logs), after)


def ffn_kernel(
    p0, p1, p2, p3, gain_ref, shift_ref, up_ref, bias_ref, grad_ref,
    act_ref, inner_ref, pre_ref, sum_ref, total,
):
    step = pl.program_id(0)
    act = (together((p0, p1, p2, p3)) * gain_ref[...] + shift_ref[...]).astype(jnp.bfloat16)
    act_ref[...] = act
    product = dot(act, up_ref[...])

    @pl.when(step == 0)
    def _():
        total[...] = product

    @pl.when(step > 0)
    def _():
        total[...] += product

    @pl.when(step == pl.num_programs(0) - 1)
    def _():
        sum_ref[...] = jnp.zeros_like(sum_ref)

        def some(i, carry):
            here = pl.ds(pl.multiple_of(i * 32, 32), 32)
            pre = total[here, :] + bias_ref[...]
            square = pre * pre
            bent = jnp.tanh(GELU_A * pre * (1.0 + GELU_B * square))
            half = 0.5 * (1.0 + bent)
            inner_ref[here, :] = (pre * half).astype(jnp.bfloat16)
            slope = half + 0.5 * GELU_A * pre * (1.0 - bent * bent) * (
                1.0 + 3.0 * GELU_B * square
            )
            grad = (slope * grad_ref[here, :]).astype(jnp.bfloat16)
            pre_ref[here, :] = grad
            sum_ref[...] += jnp.sum(grad.astype(jnp.float32).reshape(4, 8, -1), axis=0)
            return carry

        lax.fori_loop(0, LIVE // 32, some, 0)


def ffn(pieces, gain, shift, w_up, b_up, grad_inner):
    features, width = w_up.shape
    full = whole((LIVE, width))
    row = pl.BlockSpec((1, FFN_COLS), lambda i: (0, i))
    low = jax.ShapeDtypeStruct((LIVE, width), jnp.bfloat16)
    return pl.pallas_call(
        ffn_kernel,
        grid=(features // FFN_COLS,),
        in_specs=piece_specs(FFN_COLS)
        + [row, row, pl.BlockSpec((FFN_COLS, width), lambda i: (i, 0))]
        + [pl.BlockSpec((1, width), lambda i: (0, 0)), full],
        out_specs=[pl.BlockSpec((LIVE, FFN_COLS), lambda i: (0, i)), full, full]
        + [pl.BlockSpec((8, width), lambda i: (0, 0))],
        out_shape=[
            jax.ShapeDtypeStruct((LIVE, features), jnp.bfloat16),
            low,
            low,
            jax.ShapeDtypeStruct((8, width), jnp.float32),
        ],
        scratch_shapes=[pltpu.VMEM((LIVE, width), jnp.float32)],
        compiler_params=grant(28),
        cost_estimate=pl.CostEstimate(
            flops=2 * LIVE * features * width, bytes_accessed=16 << 20, transcendentals=LIVE * width
        ),
        name="ffn",
    )(*pieces, gain, shift, *far_away(w_up), b_up, *far_away(grad_inner))


def ffn_grads_kernel(out_grad_ref, inner_ref, act_ref, pre_ref, out_ref, done_ref):
    width = inner_ref.shape[1]
    done_ref[...] = jnp.zeros_like(done_ref)
    out_ref[:, 0:width] = outer_sum(out_grad_ref[...], inner_ref[...])
    out_ref[:, width:] = outer_sum(act_ref[...], pre_ref[...])


def ffn_grads(out_grad, inner, act, grad_pre):
    features, width = act.shape[1], inner.shape[1]
    half = grad_pre.shape[1] // 2
    rows = 512
    left = pl.BlockSpec((LIVE, rows), lambda i: (0, i))
    return pl.pallas_call(
        ffn_grads_kernel,
        grid=(features // rows,),
        in_specs=[left, whole((LIVE, width)), left, whole((LIVE, half))],
        out_specs=[pl.BlockSpec((rows, width + half), lambda i: (i, 0)), whole((8, 128))],
        out_shape=[in_hbm((features, width + half), jnp.float32), DONE],
        compiler_params=grant(24),
        cost_estimate=cost(3 * LIVE * features * width, 18),
        name="ffn_grads",
    )(*far_away(out_grad), inner, *far_away(act), grad_pre)


def more_grads_kernel(act_two_ref, pre_ref, act_one_ref, gq, gk, gv, attn_ref, attended_ref, out_ref):
    half, cols = pre_ref.shape[1], gq.shape[1]
    out_ref[:, 0:half] = outer_sum(act_two_ref[...], pre_ref[...])
    act_one = act_one_ref[...]
    for i, grad_ref in enumerate((gq, gk, gv)):
        out_ref[:, half + cols * i : half + cols * i + cols] = outer_sum(act_one, grad_ref[...])
    out_ref[:, half + 3 * cols :] = outer_sum(attn_ref[...], attended_ref[...])


def more_grads(act_two, grad_pre, act_one, heads, grad_attn, attended):
    features, cols = act_two.shape[1], attended.shape[1]
    half = grad_pre.shape[1] // 2
    rows = 512
    left = pl.BlockSpec((LIVE, rows), lambda i: (0, i))
    head = whole((LIVE, cols))
    width = half + 4 * cols
    return pl.pallas_call(
        more_grads_kernel,
        grid=(features // rows,),
        in_specs=[left, pl.BlockSpec((LIVE, half), lambda i: (0, 1)), left]
        + [head] * 3
        + [left, head],
        out_specs=pl.BlockSpec((rows, width), lambda i: (i, 0)),
        out_shape=in_hbm((features, width), jnp.float32),
        compiler_params=grant(24),
        cost_estimate=cost(2 * LIVE * features * width, 20),
        name="more_grads",
    )(*far_away(act_two, grad_pre, act_one, *heads, grad_attn, attended))


def vectors_kernel(perm_ref, norm_one_ref, norm_two_ref, heads_ref, up_ref, out_ref):
    lane = iota((8, 128), 1)
    for place in range(16):
        share = perm_ref[place]
        here = pl.ds(pl.multiple_of(share * 128, 128), 128)
        heads = heads_ref[:, pl.ds(pl.multiple_of((share >> 3) * 128, 128), 128)]
        heads = pltpu.roll(heads, 128 - 16 * (share & 7), 1)
        up = up_ref[:, pl.ds(pl.multiple_of((share >> 1) * 128, 128), 128)]
        up = pltpu.roll(up, 64 * (1 - (share & 1)), 1)
        up = jnp.broadcast_to(jnp.sum(up, axis=0, keepdims=True), (8, 128))
        own = jnp.where(lane < 16, heads, jnp.where(lane < 64, 0.0, up))
        out_ref[8 * place : 8 * place + 2, :] = norm_one_ref[0:2, here]
        out_ref[8 * place + 2 : 8 * place + 6, :] = norm_two_ref[0:4, here]
        out_ref[8 * place + 6 : 8 * place + 8, :] = own[0:2, :]


def vectors_of(perm, norm_one, norm_two, heads, up):
    values = (norm_one, norm_two, heads, up)
    return pl.pallas_call(
        vectors_kernel,
        in_specs=[pl.BlockSpec(memory_space=pltpu.SMEM)]
        + [pl.BlockSpec(value.shape, lambda: (0, 0)) for value in values],
        out_specs=pl.BlockSpec((128, 128), lambda: (0, 0)),
        out_shape=jax.ShapeDtypeStruct((128, 128), jnp.float32),
        compiler_params=grant(6),
        cost_estimate=cost(0, 1),
        name="vectors_of",
    )(perm, *values)


def turn_kernel(share_ref, out_ref):
    out_ref[...] = share_ref[...].T


def turn(share, width):
    rows = share.shape[0]
    return pl.pallas_call(
        turn_kernel,
        grid=(1,),
        in_specs=[pl.BlockSpec((rows, width), lambda i: (0, 0))],
        out_specs=whole((width, rows)),
        out_shape=in_hbm((width, rows), jnp.float32),
        compiler_params=grant(6),
        cost_estimate=cost(0, 2),
        name="turn",
    )(*far_away(share))


def deal_kernel(left_ref, right_ref, up_ref, gq, gk, gv, out_ref):
    half, cols = left_ref.shape[1], gq.shape[1]
    up_ref[:, 0:half] = left_ref[...]
    up_ref[:, half:] = right_ref[:, 0:half]
    for i, ref in enumerate((gq, gk, gv)):
        ref[...] = right_ref[:, half + cols * i : half + cols * i + cols]
    out_ref[...] = right_ref[:, half + 3 * cols :].T


def deal(first, second, half, cols):
    rows = first.shape[0]
    shapes = [(rows, 2 * half)] + [(rows, cols)] * 3 + [(cols, rows)]
    return pl.pallas_call(
        deal_kernel,
        grid=(1,),
        in_specs=[
            pl.BlockSpec((rows, half), lambda i: (0, first.shape[1] // half - 1)),
            whole(second.shape),
        ],
        out_specs=[whole(shape) for shape in shapes],
        out_shape=[in_hbm(shape, jnp.float32) for shape in shapes],
        compiler_params=grant(8),
        cost_estimate=cost(0, 3),
        name="deal",
    )(*far_away(first, second))


def spread_kernel(place_ref, tokens_ref, grads_ref, live_ref, *refs):
    for i, (full_ref, out_ref) in enumerate(zip((tokens_ref, grads_ref), refs[-2:])):
        rows = jnp.concatenate(
            [
                ref[64 * part + 32 * i : 64 * part + 32 * i + 32, :]
                for ref in refs[:4]
                for part in range(4)
            ],
            axis=0,
        )
        wide = dot(place_ref[...], rows.astype(jnp.bfloat16)).astype(jnp.bfloat16)
        for first in range(0, wide.shape[1], 128):
            here = slice(first, first + 128)
            out_ref[:, here] = jnp.where(live_ref[...] > 0, wide[:, here], full_ref[:, here])


def spread(place, tokens, grads, live, pieces):
    count, features = tokens.shape
    cols = 512
    block = pl.BlockSpec((count, cols), lambda i: (0, i))
    return pl.pallas_call(
        spread_kernel,
        grid=(features // cols,),
        in_specs=[whole((count, LIVE)), block, block, whole((count, 128))]
        + [pl.BlockSpec((256, cols), lambda i: (0, i))] * 4,
        out_specs=[block] * 2,
        out_shape=[in_hbm(tokens.shape, jnp.bfloat16)] * 2,
        compiler_params=grant(32),
        cost_estimate=cost(4 * count * LIVE * features, 28),
        name="spread",
    )(place, *far_away(tokens, grads), live, *pieces)


def local(
    tokens,
    cotangent,
    lengths,
    exits,
    w_query,
    b_query,
    w_key,
    w_value,
    b_value,
    w_out,
    b_out,
    gain_one,
    shift_one,
    gain_two,
    shift_two,
    w_up,
    b_up,
    w_down,
    b_down,
):
    f32, bf16 = jnp.float32, jnp.bfloat16
    bits = own_bits()
    at_dp = lax.axis_index("dp")
    y_high, z_high = at_dp >> 3, (at_dp >> 1) & 1
    y_gray, z_gray = ((at_dp >> 2) & 1) ^ y_high, (at_dp & 1) ^ z_high
    dp_bits = (y_gray, y_high, z_gray, z_high)

    def direct_place(rank):
        side, one, two = (rank >> 6) & 1, (rank >> 7) & 1, (rank >> 5) & 1
        gray, high = jnp.where(side == 1, two, one), jnp.where(side == 1, one, two)
        distance = (x_place - (2 * high + (gray ^ high))) & 3
        return 256 * ((rank >> 8) ^ bits[0]) + 64 * distance + 32 * side + (rank & 31)

    def dp_blocks(order):
        own = jnp.arange(16, dtype=jnp.int32)
        bits = [None] * 4
        for place, (_, bit) in enumerate(order):
            bits[bit] = ((own >> (3 - place)) & 1) ^ dp_bits[bit]
        return 4 * (2 * bits[1] + (bits[0] ^ bits[1])) + 2 * bits[3] + (bits[2] ^ bits[3])

    perm = dp_blocks(HALVES)

    gain_one_f, gain_two_f = gain_one.astype(f32)[None], gain_two.astype(f32)[None]
    pick, bias, source_low, act_one, normal_low, query, keys, values, attended, logs = front(
        lengths,
        exits,
        tokens,
        gain_one,
        shift_one,
        (w_query, w_key, w_value),
        b_query,
        b_value,
    )

    source_mine = jnp.concatenate([source_low[0:32], source_low[64:96]], axis=0).astype(f32)
    normal_one, scale_one = normed(source_mine)
    scale_one = jnp.broadcast_to(scale_one, (64, 128))
    begun = scatter_begin(both_parts(attended, w_out, False))
    grad_out_low, grad_inner = pick_rows(pick, cotangent, w_down, begun[4:])
    terms_a, terms_b, _ = scatter_end(begun, (grad_inner, normal_one))
    hidden_mine, normal_a, normal_b, scale_two = norm_two(
        terms_a + [(source_low, 0)], terms_b + [(source_low, 2)], b_out.astype(f32)[None]
    )
    place_all = jnp.arange(tokens.shape[0], dtype=jnp.int32)
    living = exits > LAYER
    below = (place_all[None, :] <= place_all[:, None]) & living[None, :]
    rank = jnp.sum(jnp.where(below, 1, 0), axis=1) - 1
    own_index = jnp.arange(LIVE, dtype=jnp.int32)
    living_column = jnp.broadcast_to(living.astype(bf16)[:, None], (tokens.shape[0], 128))
    row_of = jnp.where(living, own_place(rank, bits), -1)
    place = (row_of[:, None] == own_index[None, :]).astype(bf16)

    act_two, inner, grad_pre, sum_up = ffn(
        gather_rows(normal_a, normal_b)[0],
        gain_two_f,
        shift_two.astype(f32)[None],
        w_up,
        b_up.astype(f32)[None],
        grad_inner,
    )
    first_grads, first_done = ffn_grads(grad_out_low, inner, act_two, grad_pre)
    begun = scatter_begin(both_parts(grad_pre, w_up, True, (first_done,)))
    first_share = lax.psum_scatter(first_grads, "dp", scatter_dimension=0, tiled=True)
    terms_a, terms_b, sent = scatter_end(begun)

    out_pieces = both_parts(inner, w_down, False, sent)
    hidden_a, hidden_b, grad_hidden_mine, sums_two = norm_back(
        terms_a,
        terms_b,
        ((normal_a, 0), (normal_b, 0)),
        ((grad_out_low, 0), (grad_out_low, 2)),
        scale_two,
        gain_two_f,
        out_pieces[0:1],
    )
    hidden_pieces, last_pieces = gather_rows(hidden_a, hidden_b)
    out_begun = scatter_begin(out_pieces, lambda: last_pieces)
    grad_attn_low, grad_query, grad_key, grad_value, sums_heads = attend_back(
        hidden_pieces, w_out, query, keys, values, bias, logs, out_begun[4]
    )
    heads = (grad_query, grad_key, grad_value)
    *pieces, sums_one = all_parts(heads, (w_query, w_key, w_value), normal_low)
    second_grads = more_grads(act_two, grad_pre, act_one, heads, grad_attn_low, attended)
    second_share = lax.psum_scatter(second_grads, "dp", scatter_dimension=0, tiled=True)
    out_a, out_b, out_sent = scatter_end(out_begun, (sums_one,))
    begun = scatter_begin(pieces, lambda: out_sent)
    terms_a, terms_b, _ = scatter_end(begun)

    _, _, input_mine, _ = norm_back(
        terms_a,
        terms_b,
        ((normal_one, 0), (normal_one, 1)),
        ((grad_hidden_mine, 0), (grad_hidden_mine, 1)),
        scale_one,
        gain_one_f,
    )
    mine = last_rows(out_a, out_b, hidden_mine, b_down.astype(f32)[None], input_mine)
    output_full, input_full = spread(
        place, tokens, cotangent, living_column, gather_rows(*mine)[0]
    )

    shares = vectors_of(perm, sums_one, sums_two, sums_heads, sum_up)
    for count, (pairs, _) in zip((64, 32, 16, 8), HALVES):
        shares = shares[0:count] + over_dp(shares[count : 2 * count], pairs)
    own_share = shares
    share_down = turn(first_share, inner.shape[1])
    share_up, *attn_shares = deal(first_share, second_share, inner.shape[1] // 2, attended.shape[1])
    common_share = own_share
    for pairs in (CORE, X_NEAR, X_FAR):
        common_share = common_share + over_tensor(common_share, pairs)
    return (
        output_full,
        input_full,
        attn_shares[0],
        own_share[6, 0:16],
        attn_shares[1],
        attn_shares[2],
        own_share[7, 0:16],
        attn_shares[3],
        common_share[4],
        common_share[0],
        common_share[1],
        common_share[2],
        common_share[3],
        share_up,
        own_share[6, 64:128],
        share_down,
        common_share[5],
    )


def solution(mesh):
    in_specs = (
        P("dp", None),
        P("dp", None),
        P("dp", None),
        P("dp"),
        P(None, "tensor"),
        P("tensor"),
        P(None, "tensor"),
        P(None, "tensor"),
        P("tensor"),
        P("tensor", None),
        P(),
        P(),
        P(),
        P(),
        P(),
        P(None, "tensor"),
        P("tensor"),
        P("tensor", None),
        P(),
    )
    out_specs = (
        P("dp", None),
        P("dp", None),
        P("dp", "tensor"),
        P(("tensor", "dp")),
        P("dp", "tensor"),
        P("dp", "tensor"),
        P(("tensor", "dp")),
        P("tensor", "dp"),
        P("dp"),
        P("dp"),
        P("dp"),
        P("dp"),
        P("dp"),
        P("dp", "tensor"),
        P(("tensor", "dp")),
        P("tensor", "dp"),
        P("dp"),
    )
    return jax.shard_map(local, mesh=mesh, in_specs=in_specs, out_specs=out_specs, check_vma=False)
```

```python
import functools

import jax
import jax.numpy as jnp
from jax import lax
from jax.experimental import pallas as pl
from jax.experimental.pallas import tpu as pltpu
from jax.sharding import PartitionSpec as P

HEAD = 64
LAYER = 12
LIVE = 512
NEG_BIG = -1e30
EPSILON = 1e-05
GELU_A = 0.7978845608028654
GELU_B = 0.044715

CORE = [(i, i ^ 1) for i in range(8)]
X_NEAR = [(2 * x + c, 2 * (x ^ 1) + c) for x in range(4) for c in range(2)]
X_FAR = [(2 * x + c, 2 * (3 - x) + c) for x in range(4) for c in range(2)]
Y_NEAR = [(4 * y + z, 4 * (y ^ 1) + z) for y in range(4) for z in range(4)]
Y_FAR = [(4 * y + z, 4 * (3 - y) + z) for y in range(4) for z in range(4)]
Z_NEAR = [(4 * y + z, 4 * y + (z ^ 1)) for y in range(4) for z in range(4)]
Z_FAR = [(4 * y + z, 4 * y + (3 - z)) for y in range(4) for z in range(4)]
HALVES = ((Y_NEAR, 0), (Y_FAR, 1), (Z_NEAR, 2), (Z_FAR, 3))


def over_tensor(value, pairs):
    return lax.ppermute(value, "tensor", pairs)


def over_dp(value, pairs):
    return lax.ppermute(value, "dp", pairs)


def dot(left, right):
    return jnp.dot(left, right, preferred_element_type=jnp.float32)


def back_dot(left, right):
    return lax.dot_general(
        left, right, (((1,), (1,)), ((), ())), preferred_element_type=jnp.float32
    )


def outer_sum(left, right):
    return lax.dot_general(
        left, right, (((0,), (0,)), ((), ())), preferred_element_type=jnp.float32
    )


def normed(values):
    average = jnp.mean(values, axis=-1, keepdims=True)
    centred = values - average
    spread = jnp.mean(centred * centred, axis=-1, keepdims=True)
    scale = lax.rsqrt(spread + EPSILON)
    return centred * scale, scale


def grant(mib, **more):
    return pltpu.CompilerParams(vmem_limit_bytes=mib << 20, **more)


def cost(flops, mib, transcendentals=0):
    return pl.CostEstimate(
        flops=flops, bytes_accessed=int(mib * 1048576), transcendentals=transcendentals
    )


ANYWHERE = pl.BlockSpec(memory_space=pl.ANY)


def far_away(*values):
    return [pltpu.with_memory_space_constraint(value, pltpu.HBM) for value in values]


def in_hbm(shape, dtype):
    return pltpu.HBM(shape, dtype)


DONE = jax.ShapeDtypeStruct((8, 128), jnp.float32)


def whole(shape):
    return pl.BlockSpec(shape, lambda *i: (0,) * len(shape))


def parts_kernel(transposed, left_ref, right_ref, *refs):
    total = (back_dot if transposed else dot)(left_ref[...], right_ref[...])
    first, second = refs[-2:]
    first[...] = total[0:128]
    second[...] = total[128:256]


def parts(lefts, rights, transposed, half, after=()):
    (left,), (right,) = lefts, rights
    depth = left.shape[1]
    features = right.shape[0 if transposed else 1]
    cols = 512
    block = (
        pl.BlockSpec((cols, depth), lambda i: (i, 0))
        if transposed
        else pl.BlockSpec((depth, cols), lambda i: (0, i))
    )
    return pl.pallas_call(
        functools.partial(parts_kernel, transposed),
        grid=(features // cols,),
        in_specs=[pl.BlockSpec((256, depth), lambda i: (half, 0)), block] + [ANYWHERE] * len(after),
        out_specs=[pl.BlockSpec((128, cols), lambda i: (0, i))] * 2,
        out_shape=[jax.ShapeDtypeStruct((128, features), jnp.float32)] * 2,
        compiler_params=grant(9),
        cost_estimate=cost(2 * 256 * depth * features, 6),
        name="parts",
    )(left, right, *after)


def all_parts_kernel(count, *refs):
    total = None
    for left, right in zip(refs[:count], refs[count : 2 * count]):
        product = back_dot(left[...], right[...])
        total = product if total is None else total + product
    normal_ref, sum_ref = refs[2 * count], refs[-1]
    sum_ref[...] = jnp.zeros_like(sum_ref)
    sum_ref[0:1, :] = jnp.sum(total * normal_ref[...].astype(jnp.float32), axis=0, keepdims=True)
    sum_ref[1:2, :] = jnp.sum(total, axis=0, keepdims=True)
    for i in range(4):
        refs[2 * count + 1 + i][...] = total[128 * i : 128 * i + 128]


def all_parts(lefts, rights, normal):
    count, depth = len(lefts), lefts[0].shape[1]
    features = rights[0].shape[0]
    cols = 1024
    return pl.pallas_call(
        functools.partial(all_parts_kernel, count),
        grid=(features // cols,),
        in_specs=[whole((LIVE, depth))] * count
        + [pl.BlockSpec((cols, depth), lambda i: (i, 0))] * count
        + [pl.BlockSpec((LIVE, cols), lambda i: (0, i))],
        out_specs=[pl.BlockSpec((128, cols), lambda i: (0, i))] * 4
        + [pl.BlockSpec((8, cols), lambda i: (0, i))],
        out_shape=[jax.ShapeDtypeStruct((128, features), jnp.float32)] * 4
        + [jax.ShapeDtypeStruct((8, features), jnp.float32)],
        compiler_params=grant(26),
        cost_estimate=cost(2 * LIVE * depth * count * features, 10),
        name="all_parts",
    )(*far_away(*lefts, *rights, normal))


def add_kernel(counts, *refs):
    outs = refs[-len(counts) :]
    first = 0
    for out_ref, count in zip(outs, counts):
        out_ref[...] = summed(refs[first : first + count])
        first += count


def add(sums, rows, after=()):
    features = sums[0][0][0].shape[1]
    cols = 1024
    return pl.pallas_call(
        functools.partial(add_kernel, [len(terms) for terms in sums]),
        grid=(features // cols,),
        in_specs=[
            pl.BlockSpec((rows, cols), lambda i, block=block: (block, i))
            for terms in sums
            for _, block in terms
        ]
        + [ANYWHERE] * len(after),
        out_specs=[pl.BlockSpec((rows, cols), lambda i: (0, i))] * len(sums),
        out_shape=[jax.ShapeDtypeStruct((rows, features), jnp.float32)] * len(sums),
        compiler_params=grant(6),
        cost_estimate=cost(0, 2),
        name="add",
    )(*[array for terms in sums for array, _ in terms], *after)


def scatter_begin(pieces, early=None):
    near, far = pieces[0:2]
    core_far = over_tensor(pieces[3], CORE)
    core_near = over_tensor(pieces[2], CORE)
    done = early() if early else ()
    far_a, far_b = add([[(far, i), (core_far, i)] for i in range(2)], 64, done)
    got_a = over_tensor(far_a, X_NEAR)
    got_b = over_tensor(far_b, X_FAR)
    return near, core_near, got_a, got_b, far_a


def scatter_end(begun, after=()):
    near, core_near, got_a, got_b, _ = begun
    sends = [
        add([[(near, block), (core_near, block), (got, 1)]], 32, after)[0]
        for got, block in ((got_a, 1), (got_b, 3))
    ]
    last_a, last_b = [over_tensor(send, pairs) for send, pairs in zip(sends, (X_FAR, X_NEAR))]
    return (
        [(near, 0), (core_near, 0), (got_a, 0), (last_a, 0)],
        [(near, 2), (core_near, 2), (got_b, 0), (last_b, 0)],
        sends,
    )


def both_parts(left, right, transposed, after=()):
    sent = parts((left,), (right,), transposed, 1, after)
    return [*parts((left,), (right,), transposed, 0, sent[0:1]), *sent]


def join_kernel(*refs):
    rows = refs[0].shape[0]
    for i in range(4):
        refs[4][rows * i : rows * i + rows, :] = refs[i][...]


def join(pieces):
    rows, features = pieces[0].shape
    cols = 512
    return pl.pallas_call(
        join_kernel,
        grid=(features // cols,),
        in_specs=[pl.BlockSpec((rows, cols), lambda i: (0, i))] * 4,
        out_specs=pl.BlockSpec((4 * rows, cols), lambda i: (0, i)),
        out_shape=jax.ShapeDtypeStruct((4 * rows, features), jnp.float32),
        compiler_params=grant(5),
        cost_estimate=cost(0, 2),
        name="join",
    )(*pieces)


def gather_rows(mine_a, mine_b):
    a01 = over_tensor(mine_a, X_FAR)
    b01 = over_tensor(mine_b, X_NEAR)
    a10 = over_tensor(mine_a, X_NEAR)
    b10 = over_tensor(mine_b, X_FAR)
    a11 = over_tensor(a01, X_NEAR)
    b11 = over_tensor(b01, X_FAR)
    first = join((mine_a, a01, mine_b, b01))
    second = join((a10, a11, b10, b11))
    return (first, second, over_tensor(first, CORE), over_tensor(second, CORE)), (a11, b11)


def row_block(pair, features):
    return pl.BlockSpec((32, features), lambda i, block=pair[1]: (block, 0))


def summed(refs):
    return sum(ref[...].astype(jnp.float32) for ref in refs[1:]) + refs[0][...]


def norm_two_kernel(*refs):
    bias_ref, hidden_ref, scale_ref = refs[10], refs[11], refs[14]
    for i in range(2):
        here = slice(32 * i, 32 * i + 32)
        hidden = summed(refs[5 * i : 5 * i + 5]) + bias_ref[...]
        normal, scale = normed(hidden)
        hidden_ref[here, :] = hidden
        refs[12 + i][...] = normal
        scale_ref[here, :] = jnp.broadcast_to(scale, (32, 128))


def norm_two(terms_a, terms_b, bias):
    features = bias.shape[1]
    terms = terms_a + terms_b
    piece = jax.ShapeDtypeStruct((32, features), jnp.float32)
    return pl.pallas_call(
        norm_two_kernel,
        grid=(1,),
        in_specs=[row_block(term, features) for term in terms] + [whole((1, features))],
        out_specs=[whole((64, features)), whole((32, features)), whole((32, features)), whole((64, 128))],
        out_shape=[
            jax.ShapeDtypeStruct((64, features), jnp.float32),
            piece,
            piece,
            jax.ShapeDtypeStruct((64, 128), jnp.float32),
        ],
        compiler_params=grant(8),
        cost_estimate=cost(20 * 64 * features, 4),
        name="norm_two",
    )(*[term[0] for term in terms], bias)


def last_rows_kernel(*refs):
    hidden_ref, bias_ref, input_ref = refs[8:11]
    for i in range(2):
        here = slice(32 * i, 32 * i + 32)
        out_ref = refs[-2 + i]
        out_ref[0:32, :] = summed(refs[4 * i : 4 * i + 4]) + (hidden_ref[here, :] + bias_ref[...])
        out_ref[32:64, :] = input_ref[here, :]


def last_rows(terms_a, terms_b, hidden, bias, input_mine):
    features = bias.shape[1]
    terms = terms_a + terms_b
    rows = whole((64, features))
    return pl.pallas_call(
        last_rows_kernel,
        grid=(1,),
        in_specs=[row_block(term, features) for term in terms] + [rows, whole((1, features)), rows],
        out_specs=[rows] * 2,
        out_shape=[jax.ShapeDtypeStruct((64, features), jnp.float32)] * 2,
        compiler_params=grant(12),
        cost_estimate=cost(20 * 64 * features, 4),
        name="last_rows",
    )(*[term[0] for term in terms], hidden, bias, input_mine)


def norm_back_kernel(*refs):
    scale_ref, gain_ref = refs[12:14]
    pieces, total_ref, sums_ref = refs[-4:-2], refs[-2], refs[-1]
    sums_ref[...] = jnp.zeros_like(sums_ref)
    for i in range(2):
        here = slice(32 * i, 32 * i + 32)
        grad = summed(refs[4 * i : 4 * i + 4])
        normal = refs[8 + 2 * i][...]
        base = refs[9 + 2 * i][...].astype(jnp.float32)
        scaled = grad * gain_ref[...]
        first = jnp.mean(scaled, axis=-1, keepdims=True)
        second = jnp.mean(scaled * normal, axis=-1, keepdims=True)
        norm = scale_ref[here, 0:1] * (scaled - first - normal * second)
        total = base + norm
        pieces[i][...] = total
        total_ref[here, :] = total
        sums_ref[0:1, :] += jnp.sum(grad * normal, axis=0, keepdims=True)
        sums_ref[1:2, :] += jnp.sum(grad, axis=0, keepdims=True)
        sums_ref[2:3, :] += jnp.sum(total, axis=0, keepdims=True)
        sums_ref[3:4, :] += jnp.sum(base, axis=0, keepdims=True)


def norm_back(terms_a, terms_b, normals, bases, scale, gain, after=()):
    features = gain.shape[1]
    terms = terms_a + terms_b + [normals[0], bases[0], normals[1], bases[1]]
    piece = jax.ShapeDtypeStruct((32, features), jnp.float32)
    return pl.pallas_call(
        norm_back_kernel,
        grid=(1,),
        in_specs=[row_block(term, features) for term in terms]
        + [whole((64, 128)), whole((1, features))]
        + [ANYWHERE] * len(after),
        out_specs=[whole((32, features))] * 2 + [whole((64, features)), whole((8, features))],
        out_shape=[
            piece,
            piece,
            jax.ShapeDtypeStruct((64, features), jnp.float32),
            jax.ShapeDtypeStruct((8, features), jnp.float32),
        ],
        compiler_params=grant(8),
        cost_estimate=cost(20 * 64 * features, 4),
        name="norm_back",
    )(*[term[0] for term in terms], scale, gain, *after)


def own_bits():
    at = lax.axis_index("tensor")
    high = at >> 2
    return at & 1, ((at >> 1) & 1) ^ high, high


def own_place(rank, bits):
    core, gray, high = bits
    side = (rank >> 6) & 1
    one = side * high + (1 - side) * gray
    two = side * gray + (1 - side) * high
    return rank ^ (core << 8) ^ (one << 7) ^ (two << 5)


def iota(shape, axis):
    return lax.broadcasted_iota(jnp.int32, shape, axis)


def live_ranks(exits):
    living = exits > LAYER
    ones = jnp.where(living, 1.0, 0.0)
    up_to = (iota((128, 128), 0) <= iota((128, 128), 1)).astype(jnp.bfloat16)
    within = dot(ones.astype(jnp.bfloat16), up_to)
    totals = jnp.broadcast_to(jnp.sum(ones, axis=1, keepdims=True), (8, 128))
    before = jnp.zeros((8, 128), jnp.float32)
    for i in range(7):
        before += jnp.where(iota((8, 128), 0) > i, totals[i : i + 1, :], 0.0)
    return living, (within + before).astype(jnp.int32) - 1


def front_kernel(
    lengths_ref, exits_ref, tokens_ref, gain_ref, shift_ref, wq_hbm, wk_hbm, wv_hbm, bq_ref, bv_ref,
    pick_hbm, bias_hbm, source_ref, act_hbm, normal_hbm, q_ref, k_ref, v_ref, out_ref, lse_ref,
    rows_ref, w_ref, pick_ref, bias_ref, act_ref, normal_ref, sems, out_sems,
):
    step = pl.program_id(0)
    copies = [
        pltpu.make_async_copy(
            weight, w_ref.at[:, pl.ds(i * weight.shape[1], weight.shape[1])], sems.at[i]
        )
        for i, weight in enumerate((wq_hbm, wk_hbm, wv_hbm))
    ]
    outs = [
        pltpu.make_async_copy(here, there, out_sems.at[i])
        for i, (here, there) in enumerate(
            (
                (pick_ref, pick_hbm),
                (bias_ref, bias_hbm),
                (act_ref, act_hbm),
                (normal_ref, normal_hbm),
            )
        )
    ]

    @pl.when(step == 0)
    def _():
        for copy in copies:
            copy.start()
        bits = own_bits()
        living, rank = live_ranks(exits_ref[...])
        row_of = jnp.where(living, own_place(rank, bits), -1)
        for i in range(8):
            pick_ref[:, 128 * i : 128 * i + 128] = jnp.where(
                iota((LIVE, 128), 0) == row_of[i : i + 1, :], 1.0, 0.0
            ).astype(jnp.bfloat16)
        token = 128 * iota((8, 128), 0) + iota((8, 128), 1)
        rank_row = own_place(iota((1, LIVE), 1), bits)
        rank_column = own_place(iota((LIVE, 1), 0), bits)
        segment_row, segment_column = jnp.zeros_like(rank_row), jnp.zeros_like(rank_column)
        bound = 0
        for i in range(lengths_ref.shape[1] - 1):
            bound = bound + lengths_ref[0, i]
            count = jnp.sum(jnp.where(living & (token < bound), 1, 0))
            segment_row += (rank_row >= count).astype(jnp.int32)
            segment_column += (rank_column >= count).astype(jnp.int32)
        allowed = (segment_column == segment_row) & (rank_row <= rank_column)
        bias_ref[...] = jnp.where(allowed, 0.0, NEG_BIG)
        for out in outs[:2]:
            out.start()

    cols = tokens_ref.shape[1]
    found = dot(pick_ref[...], tokens_ref[...]).astype(jnp.bfloat16)
    source_ref[...] = found
    for i in range(2):

        @pl.when(step == i)
        def _(i=i):
            rows_ref[:, cols * i : cols * i + cols] = found

    @pl.when(step == pl.num_programs(0) - 1)
    def _():
        gain, shift = wide_row(gain_ref), wide_row(shift_ref)

        def some(i, carry):
            here = pl.ds(pl.multiple_of(i * 16, 16), 16)
            normal, _ = normed(rows_ref[here, :].astype(jnp.float32))
            normal_ref[here, :] = normal.astype(jnp.bfloat16)
            act_ref[here, :] = (normal * gain + shift).astype(jnp.bfloat16)
            return carry

        lax.fori_loop(0, LIVE // 16, some, 0, unroll=8)
        for out in outs[2:]:
            out.start()
        for copy in copies:
            copy.wait()
        width = q_ref.shape[1]
        product = dot(act_ref[...], w_ref[...])
        q_ref[...] = ((product[:, 0:width] + wide_row(bq_ref)) * 0.125).astype(jnp.bfloat16)
        k_ref[...] = product[:, width : 2 * width].astype(jnp.bfloat16)
        v_ref[...] = (product[:, 2 * width :] + wide_row(bv_ref)).astype(jnp.bfloat16)
        rows = LIVE
        lane = iota((1, 128), 1)
        for pair in range(q_ref.shape[1] // 128):
            at = slice(128 * pair, 128 * pair + 128)
            for part in range(LIVE // rows):
                here = slice(part * rows, part * rows + rows)
                bias = bias_ref[here, :]
                total = jnp.zeros((rows, 128), jnp.float32)
                logs = jnp.zeros((rows, 128), jnp.float32)
                for head in range(2):
                    inside = (lane // HEAD) == head
                    query = jnp.where(inside, q_ref[here, at], 0)
                    scores = back_dot(query, k_ref[:, at]) + bias
                    peak = jnp.max(scores, axis=-1, keepdims=True)
                    expo = jnp.exp(scores - peak)
                    total_expo = jnp.sum(expo, axis=-1, keepdims=True)
                    prob = (expo * (1.0 / total_expo)).astype(jnp.bfloat16)
                    total = jnp.where(inside, dot(prob, v_ref[:, at]), total)
                    logs = jnp.where(inside, peak + jnp.log(total_expo), logs)
                out_ref[here, at] = total.astype(jnp.bfloat16)
                lse_ref[here, at] = logs
        for out in outs:
            out.wait()


def wide_row(ref):
    return ref[...].astype(jnp.float32).reshape(1, -1)


def front(lengths, exits, tokens, gain, shift, weights, b_query, b_value):
    features, cols = weights[0].shape
    rows = tokens.shape[0]
    block = features // 2
    low = jax.ShapeDtypeStruct((LIVE, cols), jnp.bfloat16)
    row = whole((features,))
    heads = whole((LIVE, cols))
    return pl.pallas_call(
        front_kernel,
        grid=(2,),
        in_specs=[
            pl.BlockSpec(memory_space=pltpu.SMEM),
            whole((8, rows // 8)),
            pl.BlockSpec((rows, block), lambda i: (0, i)),
            row,
            row,
        ]
        + [ANYWHERE] * 3
        + [whole((cols,))] * 2,
        out_specs=[ANYWHERE] * 2
        + [pl.BlockSpec((LIVE, block), lambda i: (0, i))]
        + [ANYWHERE] * 2
        + [heads] * 5,
        out_shape=[
            in_hbm((LIVE, rows), jnp.bfloat16),
            in_hbm((LIVE, LIVE), jnp.float32),
        ]
        + [in_hbm((LIVE, features), jnp.bfloat16)] * 3
        + [in_hbm((LIVE, cols), jnp.bfloat16)] * 3
        + [low]
        + [in_hbm((LIVE, cols), jnp.float32)],
        scratch_shapes=[
            pltpu.VMEM((LIVE, features), jnp.bfloat16),
            pltpu.VMEM((features, 3 * cols), jnp.bfloat16),
            pltpu.VMEM((LIVE, rows), jnp.bfloat16),
            pltpu.VMEM((LIVE, LIVE), jnp.float32),
            pltpu.VMEM((LIVE, features), jnp.bfloat16),
            pltpu.VMEM((LIVE, features), jnp.bfloat16),
            pltpu.SemaphoreType.DMA((3,)),
            pltpu.SemaphoreType.DMA((4,)),
        ],
        compiler_params=grant(44),
        cost_estimate=cost(
            2 * LIVE * features * (rows + 3 * cols) + 16 * LIVE * LIVE * 128, 16, 4 * LIVE * LIVE
        ),
        name="front",
    )(
        lengths,
        *far_away(
            exits.reshape(8, rows // 8), tokens, gain, shift, *weights, b_query, b_value
        ),
    )


def pick_rows_kernel(pick_ref, full_ref, w_ref, *refs):
    rows_ref, product_ref, done_ref = refs[-3:]
    done_ref[...] = jnp.zeros_like(done_ref)
    rows = dot(pick_ref[...], full_ref[...]).astype(jnp.bfloat16)
    rows_ref[...] = rows
    product = back_dot(rows, w_ref[...])

    @pl.when(pl.program_id(0) == 0)
    def _():
        product_ref[...] = product

    @pl.when(pl.program_id(0) > 0)
    def _():
        product_ref[...] += product


def pick_rows(pick, full, weight, after):
    tokens, features = full.shape
    width = weight.shape[0]
    cols = 512
    return pl.pallas_call(
        pick_rows_kernel,
        grid=(features // cols,),
        in_specs=[
            whole((LIVE, tokens)),
            pl.BlockSpec((tokens, cols), lambda i: (0, i)),
            pl.BlockSpec((width, cols), lambda i: (0, i)),
        ]
        + [ANYWHERE] * len(after),
        out_specs=[pl.BlockSpec((LIVE, cols), lambda i: (0, i)), whole((LIVE, width)), whole((8, 128))],
        out_shape=[
            in_hbm((LIVE, features), jnp.bfloat16),
            in_hbm((LIVE, width), jnp.float32),
            DONE,
        ],
        compiler_params=grant(18),
        cost_estimate=cost(2 * LIVE * features * (tokens + width), 12),
        name="pick_rows",
    )(*far_away(pick, full, weight), *after)


def piece_specs(cols):
    return [pl.BlockSpec((128, cols), lambda i: (0, i))] * 4


def together(pieces):
    return jnp.concatenate([piece[...] for piece in pieces], axis=0)


def attend_back_kernel(
    p0, p1, p2, p3, w_ref, q_ref, k_ref, v_ref, bias_ref, lse_ref,
    low_ref, gq_ref, gk_ref, gv_ref, sum_ref, mixed, key_sum, value_sum,
):
    step = pl.program_id(0)
    low = together((p0, p1, p2, p3)).astype(jnp.bfloat16)
    low_ref[...] = low
    product = back_dot(low, w_ref[...])

    @pl.when(step == 0)
    def _():
        mixed[...] = product

    @pl.when(step > 0)
    def _():
        mixed[...] += product

    @pl.when(step == pl.num_programs(0) - 1)
    def _():
        rows = LIVE
        width = q_ref.shape[1]
        lane = lax.broadcasted_iota(jnp.int32, (1, 128), 1)
        sum_ref[...] = jnp.zeros_like(sum_ref)
        for pair in range(width // 128):
            cols = slice(128 * pair, 128 * pair + 128)
            key_sum[...] = jnp.zeros_like(key_sum)
            value_sum[...] = jnp.zeros_like(value_sum)
            for part in range(LIVE // rows):
                here = slice(part * rows, part * rows + rows)
                bias = bias_ref[here, :]
                total = jnp.zeros((rows, 128), jnp.float32)
                for head in range(2):
                    inside = (lane // HEAD) == head
                    query = jnp.where(inside, q_ref[here, cols], 0)
                    grad = jnp.where(inside, mixed[here, cols], 0.0).astype(jnp.bfloat16)
                    first = 128 * pair + head * HEAD
                    logs = lse_ref[here, first : first + 1]
                    prob = jnp.exp(back_dot(query, k_ref[:, cols]) + bias - logs)
                    grad_prob = back_dot(grad, v_ref[:, cols])
                    inner = jnp.sum(prob * grad_prob, axis=-1, keepdims=True)
                    grad_scores = (prob * (grad_prob - inner)).astype(jnp.bfloat16)
                    total = jnp.where(inside, dot(grad_scores, k_ref[:, cols]), total)
                    key_sum[...] += outer_sum(grad_scores, query)
                    value_sum[...] += outer_sum(prob.astype(jnp.bfloat16), grad)
                grad_query = total.astype(jnp.bfloat16) * jnp.bfloat16(0.125)
                gq_ref[here, cols] = grad_query
                sum_ref[0:1, cols] += jnp.sum(
                    grad_query.astype(jnp.float32), axis=0, keepdims=True
                )
            gk_ref[:, cols] = key_sum[...].astype(jnp.bfloat16)
            grad_value = value_sum[...].astype(jnp.bfloat16)
            gv_ref[:, cols] = grad_value
            sum_ref[1:2, cols] = jnp.sum(grad_value.astype(jnp.float32), axis=0, keepdims=True)


def attend_back(pieces, w_out, query, keys, values, bias, logs):
    cols, features = w_out.shape
    block = 1024
    wide = pl.BlockSpec((LIVE, block), lambda i: (0, i))
    heads = whole((LIVE, cols))
    return pl.pallas_call(
        attend_back_kernel,
        grid=(features // block,),
        in_specs=piece_specs(block)
        + [pl.BlockSpec((cols, block), lambda i: (0, i))]
        + [heads] * 3
        + [whole((LIVE, LIVE)), heads],
        out_specs=[wide] + [heads] * 3 + [whole((8, cols))],
        out_shape=[in_hbm((LIVE, features), jnp.bfloat16)]
        + [in_hbm((LIVE, cols), jnp.bfloat16)] * 3
        + [jax.ShapeDtypeStruct((8, cols), jnp.float32)],
        scratch_shapes=[pltpu.VMEM((LIVE, cols), jnp.float32)]
        + [pltpu.VMEM((LIVE, 128), jnp.float32)] * 2,
        compiler_params=grant(26),
        cost_estimate=cost(40 * LIVE * LIVE * 128, 11, 4 * LIVE * LIVE),
        name="attend_back",
    )(*pieces, *far_away(w_out, query, keys, values, bias, logs))


def ffn_kernel(half, p0, p1, gain_ref, shift_ref, up_ref, bias_ref, grad_hbm, *refs):
    act_hbm, inner_hbm, pre_hbm, sum_ref = refs[-10:-6]
    act_ref, inner_ref, pre_ref, grad_ref, in_sems, out_sems = refs[-6:]

    def copies(here, there, sems, inward):
        pairs = [
            (here.at[pl.ds(128 * i, 128), :], there.at[pl.ds(256 * i + 128 * half, 128), :])
            for i in range(2)
        ]
        return [
            pltpu.make_async_copy(*(pair[::-1] if inward else pair), sems.at[i])
            for i, pair in enumerate(pairs)
        ]

    grads = copies(grad_ref, grad_hbm, in_sems, True)
    for copy in grads:
        copy.start()
    for i, piece in enumerate((p0, p1)):
        act_ref[128 * i : 128 * i + 128, :] = (piece[...] * gain_ref[...] + shift_ref[...]).astype(
            jnp.bfloat16
        )
    outs = copies(act_ref, act_hbm, out_sems.at[0], False)
    for copy in outs:
        copy.start()
    total = dot(act_ref[...], up_ref[...]) + bias_ref[...]
    for copy in grads:
        copy.wait()
    square = total * total
    bent = jnp.tanh(GELU_A * total * (1.0 + GELU_B * square))
    side = 0.5 * (1.0 + bent)
    inner_ref[...] = (total * side).astype(jnp.bfloat16)
    slope = side + 0.5 * GELU_A * total * (1.0 - bent * bent) * (1.0 + 3.0 * GELU_B * square)
    grad = (slope * grad_ref[...]).astype(jnp.bfloat16)
    pre_ref[...] = grad
    for k, pair in enumerate(((inner_ref, inner_hbm), (pre_ref, pre_hbm))):
        more = copies(*pair, out_sems.at[k + 1], False)
        for copy in more:
            copy.start()
        outs += more
    sum_ref[...] = jnp.sum(grad.astype(jnp.float32).reshape(32, 8, -1), axis=0)
    for copy in outs:
        copy.wait()


def ffn(half, pieces, gain, shift, w_up, b_up, grad_inner, before=()):
    features, width = w_up.shape
    near = pl.BlockSpec(memory_space=pltpu.VMEM)
    shapes = [(LIVE, features), (LIVE, width), (LIVE, width)]
    return pl.pallas_call(
        functools.partial(ffn_kernel, half),
        in_specs=[near] * 6 + [ANYWHERE] * (1 + len(before)),
        out_specs=[ANYWHERE] * 3 + [near],
        out_shape=[in_hbm(shape, jnp.bfloat16) for shape in shapes]
        + [jax.ShapeDtypeStruct((8, width), jnp.float32)],
        input_output_aliases={7 + i: i for i in range(len(before))},
        scratch_shapes=[
            pltpu.VMEM((256, features), jnp.bfloat16),
            pltpu.VMEM((256, width), jnp.bfloat16),
            pltpu.VMEM((256, width), jnp.bfloat16),
            pltpu.VMEM((256, width), jnp.float32),
            pltpu.SemaphoreType.DMA((2,)),
            pltpu.SemaphoreType.DMA((3, 2)),
        ],
        compiler_params=grant(20),
        cost_estimate=cost(LIVE * features * width, 4, LIVE * width // 2),
        name="ffn",
    )(*pieces, gain, shift, w_up, b_up, *far_away(grad_inner, *before))


def ffn_grads_kernel(out_grad_ref, inner_ref, act_ref, pre_ref, out_ref, done_ref):
    width = inner_ref.shape[1]
    done_ref[...] = jnp.zeros_like(done_ref)
    out_ref[:, 0:width] = outer_sum(out_grad_ref[...], inner_ref[...])
    out_ref[:, width:] = outer_sum(act_ref[...], pre_ref[...])


def ffn_grads(out_grad, inner, act, grad_pre):
    features, width = act.shape[1], inner.shape[1]
    half = grad_pre.shape[1] // 2
    rows = 512
    left = pl.BlockSpec((LIVE, rows), lambda i: (0, i))
    return pl.pallas_call(
        ffn_grads_kernel,
        grid=(features // rows,),
        in_specs=[left, whole((LIVE, width)), left, whole((LIVE, half))],
        out_specs=[pl.BlockSpec((rows, width + half), lambda i: (i, 0)), whole((8, 128))],
        out_shape=[in_hbm((features, width + half), jnp.float32), DONE],
        compiler_params=grant(18),
        cost_estimate=cost(3 * LIVE * features * width, 18),
        name="ffn_grads",
    )(*far_away(out_grad, inner, act, grad_pre))


def more_grads_kernel(act_two_ref, pre_ref, act_one_ref, gq, gk, gv, attn_ref, attended_ref, *refs):
    out_ref = refs[-1]
    half, cols = pre_ref.shape[1], gq.shape[1]
    out_ref[:, 0:half] = outer_sum(act_two_ref[...], pre_ref[...])
    act_one = act_one_ref[...]
    for i, grad_ref in enumerate((gq, gk, gv)):
        out_ref[:, half + cols * i : half + cols * i + cols] = outer_sum(act_one, grad_ref[...])
    out_ref[:, half + 3 * cols :] = outer_sum(attn_ref[...], attended_ref[...])


def more_grads(act_two, grad_pre, act_one, heads, grad_attn, attended, after):
    features, cols = act_two.shape[1], attended.shape[1]
    half = grad_pre.shape[1] // 2
    rows = 512
    left = pl.BlockSpec((LIVE, rows), lambda i: (0, i))
    head = whole((LIVE, cols))
    width = half + 4 * cols
    return pl.pallas_call(
        more_grads_kernel,
        grid=(features // rows,),
        in_specs=[left, pl.BlockSpec((LIVE, half), lambda i: (0, 1)), left]
        + [head] * 3
        + [left, head]
        + [ANYWHERE] * len(after),
        out_specs=pl.BlockSpec((rows, width), lambda i: (i, 0)),
        out_shape=in_hbm((features, width), jnp.float32),
        compiler_params=grant(18),
        cost_estimate=cost(2 * LIVE * features * width, 20),
        name="more_grads",
    )(*far_away(act_two, grad_pre, act_one, *heads, grad_attn, attended), *after)


def vectors_kernel(perm_ref, norm_one_ref, norm_two_ref, heads_ref, up_ref, out_ref):
    lane = iota((8, 128), 1)
    for place in range(16):
        share = perm_ref[place]
        here = pl.ds(pl.multiple_of(share * 128, 128), 128)
        heads = heads_ref[:, pl.ds(pl.multiple_of((share >> 3) * 128, 128), 128)]
        heads = pltpu.roll(heads, 128 - 16 * (share & 7), 1)
        up = up_ref[:, pl.ds(pl.multiple_of((share >> 1) * 128, 128), 128)]
        up = pltpu.roll(up, 64 * (1 - (share & 1)), 1)
        up = jnp.broadcast_to(jnp.sum(up, axis=0, keepdims=True), (8, 128))
        own = jnp.where(lane < 16, heads, jnp.where(lane < 64, 0.0, up))
        out_ref[8 * place : 8 * place + 2, :] = norm_one_ref[0:2, here]
        out_ref[8 * place + 2 : 8 * place + 6, :] = norm_two_ref[0:4, here]
        out_ref[8 * place + 6 : 8 * place + 8, :] = own[0:2, :]


def vectors_of(perm, norm_one, norm_two, heads, up):
    values = (norm_one, norm_two, heads, up)
    return pl.pallas_call(
        vectors_kernel,
        in_specs=[pl.BlockSpec(memory_space=pltpu.SMEM)]
        + [pl.BlockSpec(value.shape, lambda: (0, 0)) for value in values],
        out_specs=pl.BlockSpec((128, 128), lambda: (0, 0)),
        out_shape=jax.ShapeDtypeStruct((128, 128), jnp.float32),
        compiler_params=grant(6),
        cost_estimate=cost(0, 1),
        name="vectors_of",
    )(perm, *values)


def turn_kernel(share_ref, out_ref):
    out_ref[...] = share_ref[...].T


def turn(share, width):
    rows = share.shape[0]
    return pl.pallas_call(
        turn_kernel,
        grid=(1,),
        in_specs=[pl.BlockSpec((rows, width), lambda i: (0, 0))],
        out_specs=whole((width, rows)),
        out_shape=in_hbm((width, rows), jnp.float32),
        compiler_params=grant(6),
        cost_estimate=cost(0, 2),
        name="turn",
    )(*far_away(share))


def deal_kernel(left_ref, right_ref, up_ref, gq, gk, gv, out_ref):
    half, cols = left_ref.shape[1], gq.shape[1]
    up_ref[:, 0:half] = left_ref[...]
    up_ref[:, half:] = right_ref[:, 0:half]
    for i, ref in enumerate((gq, gk, gv)):
        ref[...] = right_ref[:, half + cols * i : half + cols * i + cols]
    out_ref[...] = right_ref[:, half + 3 * cols :].T


def deal(first, second, half, cols):
    rows = first.shape[0]
    shapes = [(rows, 2 * half)] + [(rows, cols)] * 3 + [(cols, rows)]
    return pl.pallas_call(
        deal_kernel,
        grid=(1,),
        in_specs=[
            pl.BlockSpec((rows, half), lambda i: (0, first.shape[1] // half - 1)),
            whole(second.shape),
        ],
        out_specs=[whole(shape) for shape in shapes],
        out_shape=[in_hbm(shape, jnp.float32) for shape in shapes],
        compiler_params=grant(8),
        cost_estimate=cost(0, 3),
        name="deal",
    )(*far_away(first, second))


def spread_kernel(place_ref, tokens_ref, grads_ref, live_ref, *refs):
    for i, (full_ref, out_ref) in enumerate(zip((tokens_ref, grads_ref), refs[-2:])):
        rows = jnp.concatenate(
            [
                ref[64 * part + 32 * i : 64 * part + 32 * i + 32, :]
                for ref in refs[:4]
                for part in range(4)
            ],
            axis=0,
        )
        wide = dot(place_ref[...], rows.astype(jnp.bfloat16)).astype(jnp.bfloat16)
        for first in range(0, wide.shape[1], 128):
            here = slice(first, first + 128)
            out_ref[:, here] = jnp.where(live_ref[...] > 0, wide[:, here], full_ref[:, here])


def spread(place, tokens, grads, live, pieces):
    count, features = tokens.shape
    cols = 512
    block = pl.BlockSpec((count, cols), lambda i: (0, i))
    return pl.pallas_call(
        spread_kernel,
        grid=(features // cols,),
        in_specs=[whole((count, LIVE)), block, block, whole((count, 128))]
        + [pl.BlockSpec((256, cols), lambda i: (0, i))] * 4,
        out_specs=[block] * 2,
        out_shape=[in_hbm(tokens.shape, jnp.bfloat16)] * 2,
        compiler_params=grant(32),
        cost_estimate=cost(4 * count * LIVE * features, 28),
        name="spread",
    )(place, *far_away(tokens, grads), live, *pieces)


def local(
    tokens,
    cotangent,
    lengths,
    exits,
    w_query,
    b_query,
    w_key,
    w_value,
    b_value,
    w_out,
    b_out,
    gain_one,
    shift_one,
    gain_two,
    shift_two,
    w_up,
    b_up,
    w_down,
    b_down,
):
    f32, bf16 = jnp.float32, jnp.bfloat16
    bits = own_bits()
    at_dp = lax.axis_index("dp")
    y_high, z_high = at_dp >> 3, (at_dp >> 1) & 1
    y_gray, z_gray = ((at_dp >> 2) & 1) ^ y_high, (at_dp & 1) ^ z_high
    dp_bits = (y_gray, y_high, z_gray, z_high)

    def direct_place(rank):
        side, one, two = (rank >> 6) & 1, (rank >> 7) & 1, (rank >> 5) & 1
        gray, high = jnp.where(side == 1, two, one), jnp.where(side == 1, one, two)
        distance = (x_place - (2 * high + (gray ^ high))) & 3
        return 256 * ((rank >> 8) ^ bits[0]) + 64 * distance + 32 * side + (rank & 31)

    def dp_blocks(order):
        own = jnp.arange(16, dtype=jnp.int32)
        bits = [None] * 4
        for place, (_, bit) in enumerate(order):
            bits[bit] = ((own >> (3 - place)) & 1) ^ dp_bits[bit]
        return 4 * (2 * bits[1] + (bits[0] ^ bits[1])) + 2 * bits[3] + (bits[2] ^ bits[3])

    perm = dp_blocks(HALVES)

    gain_one_f, gain_two_f = gain_one.astype(f32)[None], gain_two.astype(f32)[None]
    pick, bias, source_low, act_one, normal_low, query, keys, values, attended, logs = front(
        lengths,
        exits,
        tokens,
        gain_one,
        shift_one,
        (w_query, w_key, w_value),
        b_query,
        b_value,
    )

    source_mine = jnp.concatenate([source_low[0:32], source_low[64:96]], axis=0).astype(f32)
    normal_one, scale_one = normed(source_mine)
    scale_one = jnp.broadcast_to(scale_one, (64, 128))
    begun = scatter_begin(both_parts(attended, w_out, False))
    grad_out_low, grad_inner, picked = pick_rows(pick, cotangent, w_down, begun[4:])
    terms_a, terms_b, _ = scatter_end(begun, (picked,))
    hidden_mine, normal_a, normal_b, scale_two = norm_two(
        terms_a + [(source_low, 0)], terms_b + [(source_low, 2)], b_out.astype(f32)[None]
    )
    place_all = jnp.arange(tokens.shape[0], dtype=jnp.int32)
    living = exits > LAYER
    below = (place_all[None, :] <= place_all[:, None]) & living[None, :]
    rank = jnp.sum(jnp.where(below, 1, 0), axis=1) - 1
    own_index = jnp.arange(LIVE, dtype=jnp.int32)
    living_column = jnp.broadcast_to(living.astype(bf16)[:, None], (tokens.shape[0], 128))
    row_of = jnp.where(living, own_place(rank, bits), -1)
    place = (row_of[:, None] == own_index[None, :]).astype(bf16)

    normal_pieces, _ = gather_rows(normal_a, normal_b)
    shift_two_f, b_up_f = shift_two.astype(f32)[None], b_up.astype(f32)[None]
    *begun, sum_up = ffn(
        0, normal_pieces[0::2], gain_two_f, shift_two_f, w_up, b_up_f, grad_inner
    )
    act_two, inner, grad_pre, more_up = ffn(
        1, normal_pieces[1::2], gain_two_f, shift_two_f, w_up, b_up_f, grad_inner, begun
    )
    first_grads, first_done = ffn_grads(grad_out_low, inner, act_two, grad_pre)
    begun = scatter_begin(both_parts(grad_pre, w_up, True, (first_done,)))
    first_share = lax.psum_scatter(first_grads, "dp", scatter_dimension=0, tiled=True)
    terms_a, terms_b, sent = scatter_end(begun)

    out_pieces = both_parts(inner, w_down, False, sent)
    hidden_a, hidden_b, grad_hidden_mine, sums_two = norm_back(
        terms_a,
        terms_b,
        ((normal_a, 0), (normal_b, 0)),
        ((grad_out_low, 0), (grad_out_low, 2)),
        scale_two,
        gain_two_f,
        out_pieces[0:1],
    )
    hidden_pieces, last_pieces = gather_rows(hidden_a, hidden_b)
    out_begun = scatter_begin(out_pieces, lambda: last_pieces)
    grad_attn_low, grad_query, grad_key, grad_value, sums_heads = attend_back(
        hidden_pieces, w_out, query, keys, values, bias, logs
    )
    heads = (grad_query, grad_key, grad_value)
    *pieces, sums_one = all_parts(heads, (w_query, w_key, w_value), normal_low)

    shares = [vectors_of(perm, sums_one, sums_two, sums_heads, sum_up + more_up)]
    for count, (pairs, _) in zip((64, 32, 16, 8), HALVES):
        last = shares[-1]
        shares.append(last[0:count] + over_dp(last[count : 2 * count], pairs))

    out_a, out_b, out_sent = scatter_end(out_begun, (sums_one,))
    second_grads = more_grads(
        act_two, grad_pre, act_one, heads, grad_attn_low, attended, (sums_one, *out_sent)
    )
    begun = scatter_begin(pieces, lambda: (*out_sent, shares[1]))
    second_share = lax.psum_scatter(second_grads, "dp", scatter_dimension=0, tiled=True)
    terms_a, terms_b, _ = scatter_end(begun, (shares[3],))

    _, _, input_mine, _ = norm_back(
        terms_a,
        terms_b,
        ((normal_one, 0), (normal_one, 1)),
        ((grad_hidden_mine, 0), (grad_hidden_mine, 1)),
        scale_one,
        gain_one_f,
        (shares[4],),
    )
    mine = last_rows(out_a, out_b, hidden_mine, b_down.astype(f32)[None], input_mine)
    output_full, input_full = spread(
        place, tokens, cotangent, living_column, gather_rows(*mine)[0]
    )

    own_share = shares[4]
    share_down = turn(first_share, inner.shape[1])
    share_up, *attn_shares = deal(first_share, second_share, inner.shape[1] // 2, attended.shape[1])
    common_share = own_share
    for pairs in (CORE, X_NEAR, X_FAR):
        common_share = common_share + over_tensor(common_share, pairs)
    return (
        output_full,
        input_full,
        attn_shares[0],
        own_share[6, 0:16],
        attn_shares[1],
        attn_shares[2],
        own_share[7, 0:16],
        attn_shares[3],
        common_share[4],
        common_share[0],
        common_share[1],
        common_share[2],
        common_share[3],
        share_up,
        own_share[6, 64:128],
        share_down,
        common_share[5],
    )


def solution(mesh):
    in_specs = (
        P("dp", None),
        P("dp", None),
        P("dp", None),
        P("dp"),
        P(None, "tensor"),
        P("tensor"),
        P(None, "tensor"),
        P(None, "tensor"),
        P("tensor"),
        P("tensor", None),
        P(),
        P(),
        P(),
        P(),
        P(),
        P(None, "tensor"),
        P("tensor"),
        P("tensor", None),
        P(),
    )
    out_specs = (
        P("dp", None),
        P("dp", None),
        P("dp", "tensor"),
        P(("tensor", "dp")),
        P("dp", "tensor"),
        P("dp", "tensor"),
        P(("tensor", "dp")),
        P("tensor", "dp"),
        P("dp"),
        P("dp"),
        P("dp"),
        P("dp"),
        P("dp"),
        P("dp", "tensor"),
        P(("tensor", "dp")),
        P("tensor", "dp"),
        P("dp"),
    )
    return jax.shard_map(local, mesh=mesh, in_specs=in_specs, out_specs=out_specs, check_vma=False)
```

```python
import functools

import jax
import jax.numpy as jnp
from jax import lax
from jax.experimental import pallas as pl
from jax.experimental.pallas import tpu as pltpu
from jax.sharding import PartitionSpec as P

HEAD = 64
LAYER = 12
LIVE = 512
NEG_BIG = -1e30
EPSILON = 1e-05
GELU_A = 0.7978845608028654
GELU_B = 0.044715

CORE = [(i, i ^ 1) for i in range(8)]
X_NEAR = [(2 * x + c, 2 * (x ^ 1) + c) for x in range(4) for c in range(2)]
X_FAR = [(2 * x + c, 2 * (3 - x) + c) for x in range(4) for c in range(2)]
Y_NEAR = [(4 * y + z, 4 * (y ^ 1) + z) for y in range(4) for z in range(4)]
Y_FAR = [(4 * y + z, 4 * (3 - y) + z) for y in range(4) for z in range(4)]
Z_NEAR = [(4 * y + z, 4 * y + (z ^ 1)) for y in range(4) for z in range(4)]
Z_FAR = [(4 * y + z, 4 * y + (3 - z)) for y in range(4) for z in range(4)]
HALVES = ((Y_NEAR, 0), (Y_FAR, 1), (Z_NEAR, 2), (Z_FAR, 3))


def over_tensor(value, pairs):
    return lax.ppermute(value, "tensor", pairs)


def over_dp(value, pairs):
    return lax.ppermute(value, "dp", pairs)


def dot(left, right):
    return jnp.dot(left, right, preferred_element_type=jnp.float32)


def back_dot(left, right):
    return lax.dot_general(
        left, right, (((1,), (1,)), ((), ())), preferred_element_type=jnp.float32
    )


def outer_sum(left, right):
    return lax.dot_general(
        left, right, (((0,), (0,)), ((), ())), preferred_element_type=jnp.float32
    )


def normed(values):
    average = jnp.mean(values, axis=-1, keepdims=True)
    centred = values - average
    spread = jnp.mean(centred * centred, axis=-1, keepdims=True)
    scale = lax.rsqrt(spread + EPSILON)
    return centred * scale, scale


def grant(mib, **more):
    return pltpu.CompilerParams(vmem_limit_bytes=mib << 20, **more)


def cost(flops, mib, transcendentals=0):
    return pl.CostEstimate(
        flops=flops, bytes_accessed=int(mib * 1048576), transcendentals=transcendentals
    )


ANYWHERE = pl.BlockSpec(memory_space=pl.ANY)


def far_away(*values):
    return [pltpu.with_memory_space_constraint(value, pltpu.HBM) for value in values]


def in_hbm(shape, dtype):
    return pltpu.HBM(shape, dtype)


DONE = jax.ShapeDtypeStruct((8, 128), jnp.float32)


def whole(shape):
    return pl.BlockSpec(shape, lambda *i: (0,) * len(shape))


def parts_kernel(transposed, left_ref, right_ref, *refs):
    total = (back_dot if transposed else dot)(left_ref[...], right_ref[...])
    first, second = refs[-2:]
    first[...] = total[0:128]
    second[...] = total[128:256]


def parts(lefts, rights, transposed, half, after=()):
    (left,), (right,) = lefts, rights
    depth = left.shape[1]
    features = right.shape[0 if transposed else 1]
    cols = 512
    block = (
        pl.BlockSpec((cols, depth), lambda i: (i, 0))
        if transposed
        else pl.BlockSpec((depth, cols), lambda i: (0, i))
    )
    return pl.pallas_call(
        functools.partial(parts_kernel, transposed),
        grid=(features // cols,),
        in_specs=[pl.BlockSpec((256, depth), lambda i: (half, 0)), block] + [ANYWHERE] * len(after),
        out_specs=[pl.BlockSpec((128, cols), lambda i: (0, i))] * 2,
        out_shape=[jax.ShapeDtypeStruct((128, features), jnp.float32)] * 2,
        compiler_params=grant(9),
        cost_estimate=cost(2 * 256 * depth * features, 6),
        name="parts",
    )(left, right, *after)


def all_parts_kernel(count, *refs):
    total = None
    for left, right in zip(refs[:count], refs[count : 2 * count]):
        product = back_dot(left[...], right[...])
        total = product if total is None else total + product
    normal_ref, sum_ref = refs[2 * count], refs[-1]
    sum_ref[...] = jnp.zeros_like(sum_ref)
    sum_ref[0:1, :] = jnp.sum(total * normal_ref[...].astype(jnp.float32), axis=0, keepdims=True)
    sum_ref[1:2, :] = jnp.sum(total, axis=0, keepdims=True)
    for i in range(4):
        refs[2 * count + 1 + i][...] = total[128 * i : 128 * i + 128]


def all_parts(lefts, rights, normal):
    count, depth = len(lefts), lefts[0].shape[1]
    features = rights[0].shape[0]
    cols = 1024
    return pl.pallas_call(
        functools.partial(all_parts_kernel, count),
        grid=(features // cols,),
        in_specs=[whole((LIVE, depth))] * count
        + [pl.BlockSpec((cols, depth), lambda i: (i, 0))] * count
        + [pl.BlockSpec((LIVE, cols), lambda i: (0, i))],
        out_specs=[pl.BlockSpec((128, cols), lambda i: (0, i))] * 4
        + [pl.BlockSpec((8, cols), lambda i: (0, i))],
        out_shape=[jax.ShapeDtypeStruct((128, features), jnp.float32)] * 4
        + [jax.ShapeDtypeStruct((8, features), jnp.float32)],
        compiler_params=grant(26),
        cost_estimate=cost(2 * LIVE * depth * count * features, 10),
        name="all_parts",
    )(*far_away(*lefts, *rights, normal))


def add_kernel(counts, *refs):
    outs = refs[-len(counts) :]
    first = 0
    for out_ref, count in zip(outs, counts):
        out_ref[...] = summed(refs[first : first + count])
        first += count


def add(sums, rows, after=()):
    features = sums[0][0][0].shape[1]
    cols = 1024
    return pl.pallas_call(
        functools.partial(add_kernel, [len(terms) for terms in sums]),
        grid=(features // cols,),
        in_specs=[
            pl.BlockSpec((rows, cols), lambda i, block=block: (block, i))
            for terms in sums
            for _, block in terms
        ]
        + [ANYWHERE] * len(after),
        out_specs=[pl.BlockSpec((rows, cols), lambda i: (0, i))] * len(sums),
        out_shape=[jax.ShapeDtypeStruct((rows, features), jnp.float32)] * len(sums),
        compiler_params=grant(6),
        cost_estimate=cost(0, 2),
        name="add",
    )(*[array for terms in sums for array, _ in terms], *after)


def scatter_begin(pieces, early=None):
    near, far = pieces[0:2]
    core_far = over_tensor(pieces[3], CORE)
    core_near = over_tensor(pieces[2], CORE)
    done = early() if early else ()
    far_a, far_b = add([[(far, i), (core_far, i)] for i in range(2)], 64, done)
    got_a = over_tensor(far_a, X_NEAR)
    got_b = over_tensor(far_b, X_FAR)
    return near, core_near, got_a, got_b, far_a


def scatter_end(begun, after=()):
    near, core_near, got_a, got_b, _ = begun
    sends = [
        add([[(near, block), (core_near, block), (got, 1)]], 32, after)[0]
        for got, block in ((got_a, 1), (got_b, 3))
    ]
    last_a, last_b = [over_tensor(send, pairs) for send, pairs in zip(sends, (X_FAR, X_NEAR))]
    return (
        [(near, 0), (core_near, 0), (got_a, 0), (last_a, 0)],
        [(near, 2), (core_near, 2), (got_b, 0), (last_b, 0)],
        sends,
    )


def both_parts(left, right, transposed, after=()):
    sent = parts((left,), (right,), transposed, 1, after)
    return [*parts((left,), (right,), transposed, 0, sent[0:1]), *sent]


def join_kernel(*refs):
    rows = refs[0].shape[0]
    for i in range(4):
        refs[-1][rows * i : rows * i + rows, :] = refs[i][...]


def join(pieces, after=()):
    rows, features = pieces[0].shape
    cols = 512
    return pl.pallas_call(
        join_kernel,
        grid=(features // cols,),
        in_specs=[pl.BlockSpec((rows, cols), lambda i: (0, i))] * 4 + [ANYWHERE] * len(after),
        out_specs=pl.BlockSpec((4 * rows, cols), lambda i: (0, i)),
        out_shape=jax.ShapeDtypeStruct((4 * rows, features), jnp.float32),
        compiler_params=grant(5),
        cost_estimate=cost(0, 2),
        name="join",
    )(*pieces, *after)


def gather_rows(mine_a, mine_b, beside=None):
    a01 = over_tensor(mine_a, X_FAR)
    b01 = over_tensor(mine_b, X_NEAR)
    a10 = over_tensor(mine_a, X_NEAR)
    b10 = over_tensor(mine_b, X_FAR)
    a11 = over_tensor(a01, X_NEAR)
    b11 = over_tensor(b01, X_FAR)
    first = join((mine_a, a01, mine_b, b01))
    second = join((a10, a11, b10, b11), beside(first) if beside else ())
    return (first, second, over_tensor(first, CORE), over_tensor(second, CORE)), (a11, b11)


def row_block(pair, features):
    return pl.BlockSpec((32, features), lambda i, block=pair[1]: (block, 0))


def summed(refs):
    return sum(ref[...].astype(jnp.float32) for ref in refs[1:]) + refs[0][...]


def norm_two_kernel(*refs):
    bias_ref, hidden_ref, rows_ref, scale_ref = refs[10], refs[11], refs[12], refs[15]
    for i in range(2):
        here = slice(32 * i, 32 * i + 32)
        hidden = summed(refs[5 * i : 5 * i + 5]) + bias_ref[...]
        normal, scale = normed(hidden)
        hidden_ref[here, :] = hidden
        rows_ref[here, :] = normal
        refs[13 + i][...] = normal
        scale_ref[here, :] = jnp.broadcast_to(scale, (32, 128))


def norm_two(terms_a, terms_b, bias):
    features = bias.shape[1]
    terms = terms_a + terms_b
    rows, piece = (64, features), (32, features)
    return pl.pallas_call(
        norm_two_kernel,
        grid=(1,),
        in_specs=[row_block(term, features) for term in terms] + [whole((1, features))],
        out_specs=[whole(rows)] * 2 + [whole(piece)] * 2 + [whole((64, 128))],
        out_shape=[in_hbm(rows, jnp.float32)] * 2
        + [jax.ShapeDtypeStruct(piece, jnp.float32)] * 2
        + [in_hbm((64, 128), jnp.float32)],
        compiler_params=grant(10),
        cost_estimate=cost(20 * 64 * features, 4),
        name="norm_two",
    )(*[term[0] for term in terms], bias)


def last_rows_kernel(*refs):
    hidden_ref, bias_ref, input_ref = refs[8:11]
    for i in range(2):
        here = slice(32 * i, 32 * i + 32)
        out_ref = refs[-2 + i]
        out_ref[0:32, :] = summed(refs[4 * i : 4 * i + 4]) + (hidden_ref[here, :] + bias_ref[...])
        out_ref[32:64, :] = input_ref[here, :]


def last_rows(terms_a, terms_b, hidden, bias, input_mine):
    features = bias.shape[1]
    terms = terms_a + terms_b
    rows = whole((64, features))
    return pl.pallas_call(
        last_rows_kernel,
        grid=(1,),
        in_specs=[row_block(term, features) for term in terms] + [rows, whole((1, features)), rows],
        out_specs=[rows] * 2,
        out_shape=[jax.ShapeDtypeStruct((64, features), jnp.float32)] * 2,
        compiler_params=grant(12),
        cost_estimate=cost(20 * 64 * features, 4),
        name="last_rows",
    )(*[term[0] for term in terms], hidden, bias, input_mine)


def norm_back_kernel(*refs):
    scale_ref, gain_ref = refs[12:14]
    pieces, total_ref, sums_ref = refs[-4:-2], refs[-2], refs[-1]
    sums_ref[...] = jnp.zeros_like(sums_ref)
    for i in range(2):
        here = slice(32 * i, 32 * i + 32)
        grad = summed(refs[4 * i : 4 * i + 4])
        normal = refs[8 + 2 * i][...]
        base = refs[9 + 2 * i][...].astype(jnp.float32)
        scaled = grad * gain_ref[...]
        first = jnp.mean(scaled, axis=-1, keepdims=True)
        second = jnp.mean(scaled * normal, axis=-1, keepdims=True)
        norm = scale_ref[here, 0:1] * (scaled - first - normal * second)
        total = base + norm
        pieces[i][...] = total
        total_ref[here, :] = total
        sums_ref[0:1, :] += jnp.sum(grad * normal, axis=0, keepdims=True)
        sums_ref[1:2, :] += jnp.sum(grad, axis=0, keepdims=True)
        sums_ref[2:3, :] += jnp.sum(total, axis=0, keepdims=True)
        sums_ref[3:4, :] += jnp.sum(base, axis=0, keepdims=True)


def norm_back(terms_a, terms_b, normals, bases, scale, gain, after=()):
    features = gain.shape[1]
    terms = terms_a + terms_b + [normals[0], bases[0], normals[1], bases[1]]
    piece = jax.ShapeDtypeStruct((32, features), jnp.float32)
    return pl.pallas_call(
        norm_back_kernel,
        grid=(1,),
        in_specs=[row_block(term, features) for term in terms]
        + [whole((64, 128)), whole((1, features))]
        + [ANYWHERE] * len(after),
        out_specs=[whole((32, features))] * 2 + [whole((64, features)), whole((8, features))],
        out_shape=[
            piece,
            piece,
            jax.ShapeDtypeStruct((64, features), jnp.float32),
            jax.ShapeDtypeStruct((8, features), jnp.float32),
        ],
        compiler_params=grant(8),
        cost_estimate=cost(20 * 64 * features, 4),
        name="norm_back",
    )(*[term[0] for term in terms], scale, gain, *after)


def own_bits():
    at = lax.axis_index("tensor")
    high = at >> 2
    return at & 1, ((at >> 1) & 1) ^ high, high


def own_place(rank, bits):
    core, gray, high = bits
    side = (rank >> 6) & 1
    one = side * high + (1 - side) * gray
    two = side * gray + (1 - side) * high
    return rank ^ (core << 8) ^ (one << 7) ^ (two << 5)


def iota(shape, axis):
    return lax.broadcasted_iota(jnp.int32, shape, axis)


def live_ranks(exits):
    living = exits > LAYER
    ones = jnp.where(living, 1.0, 0.0)
    up_to = (iota((128, 128), 0) <= iota((128, 128), 1)).astype(jnp.bfloat16)
    within = dot(ones.astype(jnp.bfloat16), up_to)
    totals = jnp.broadcast_to(jnp.sum(ones, axis=1, keepdims=True), (8, 128))
    before = jnp.zeros((8, 128), jnp.float32)
    for i in range(7):
        before += jnp.where(iota((8, 128), 0) > i, totals[i : i + 1, :], 0.0)
    return living, (within + before).astype(jnp.int32) - 1


def front_kernel(
    lengths_ref, exits_ref, tokens_ref, gain_ref, shift_ref, wq_hbm, wk_hbm, wv_hbm, bq_ref, bv_ref,
    pick_hbm, bias_hbm, source_ref, act_hbm, normal_hbm, q_ref, k_ref, v_ref, out_ref, lse_ref,
    rows_ref, w_ref, pick_ref, bias_ref, act_ref, normal_ref, sems, out_sems,
):
    step = pl.program_id(0)
    copies = [
        pltpu.make_async_copy(
            weight, w_ref.at[:, pl.ds(i * weight.shape[1], weight.shape[1])], sems.at[i]
        )
        for i, weight in enumerate((wq_hbm, wk_hbm, wv_hbm))
    ]
    outs = [
        pltpu.make_async_copy(here, there, out_sems.at[i])
        for i, (here, there) in enumerate(
            (
                (pick_ref, pick_hbm),
                (bias_ref, bias_hbm),
                (act_ref, act_hbm),
                (normal_ref, normal_hbm),
            )
        )
    ]

    @pl.when(step == 0)
    def _():
        for copy in copies:
            copy.start()
        bits = own_bits()
        living, rank = live_ranks(exits_ref[...])
        row_of = jnp.where(living, own_place(rank, bits), -1)
        for i in range(8):
            pick_ref[:, 128 * i : 128 * i + 128] = jnp.where(
                iota((LIVE, 128), 0) == row_of[i : i + 1, :], 1.0, 0.0
            ).astype(jnp.bfloat16)
        token = 128 * iota((8, 128), 0) + iota((8, 128), 1)
        rank_row = own_place(iota((1, LIVE), 1), bits)
        rank_column = own_place(iota((LIVE, 1), 0), bits)
        segment_row, segment_column = jnp.zeros_like(rank_row), jnp.zeros_like(rank_column)
        bound = 0
        for i in range(lengths_ref.shape[1] - 1):
            bound = bound + lengths_ref[0, i]
            count = jnp.sum(jnp.where(living & (token < bound), 1, 0))
            segment_row += (rank_row >= count).astype(jnp.int32)
            segment_column += (rank_column >= count).astype(jnp.int32)
        allowed = (segment_column == segment_row) & (rank_row <= rank_column)
        bias_ref[...] = jnp.where(allowed, 0.0, NEG_BIG)
        for out in outs[:2]:
            out.start()

    cols = tokens_ref.shape[1]
    found = dot(pick_ref[...], tokens_ref[...]).astype(jnp.bfloat16)
    source_ref[...] = found
    for i in range(2):

        @pl.when(step == i)
        def _(i=i):
            rows_ref[:, cols * i : cols * i + cols] = found

    @pl.when(step == pl.num_programs(0) - 1)
    def _():
        gain, shift = wide_row(gain_ref), wide_row(shift_ref)

        def some(i, carry):
            here = pl.ds(pl.multiple_of(i * 16, 16), 16)
            normal, _ = normed(rows_ref[here, :].astype(jnp.float32))
            normal_ref[here, :] = normal.astype(jnp.bfloat16)
            act_ref[here, :] = (normal * gain + shift).astype(jnp.bfloat16)
            return carry

        lax.fori_loop(0, LIVE // 16, some, 0, unroll=8)
        for out in outs[2:]:
            out.start()
        for copy in copies:
            copy.wait()
        width = q_ref.shape[1]
        product = dot(act_ref[...], w_ref[...])
        q_ref[...] = ((product[:, 0:width] + wide_row(bq_ref)) * 0.125).astype(jnp.bfloat16)
        k_ref[...] = product[:, width : 2 * width].astype(jnp.bfloat16)
        v_ref[...] = (product[:, 2 * width :] + wide_row(bv_ref)).astype(jnp.bfloat16)
        rows = LIVE
        lane = iota((1, 128), 1)
        for pair in range(q_ref.shape[1] // 128):
            at = slice(128 * pair, 128 * pair + 128)
            for part in range(LIVE // rows):
                here = slice(part * rows, part * rows + rows)
                bias = bias_ref[here, :]
                total = jnp.zeros((rows, 128), jnp.float32)
                logs = jnp.zeros((rows, 128), jnp.float32)
                for head in range(2):
                    inside = (lane // HEAD) == head
                    query = jnp.where(inside, q_ref[here, at], 0)
                    scores = back_dot(query, k_ref[:, at]) + bias
                    peak = jnp.max(scores, axis=-1, keepdims=True)
                    expo = jnp.exp(scores - peak)
                    total_expo = jnp.sum(expo, axis=-1, keepdims=True)
                    prob = (expo * (1.0 / total_expo)).astype(jnp.bfloat16)
                    total = jnp.where(inside, dot(prob, v_ref[:, at]), total)
                    logs = jnp.where(inside, peak + jnp.log(total_expo), logs)
                out_ref[here, at] = total.astype(jnp.bfloat16)
                lse_ref[here, at] = logs
        for out in outs:
            out.wait()


def wide_row(ref):
    return ref[...].astype(jnp.float32).reshape(1, -1)


def front(lengths, exits, tokens, gain, shift, weights, b_query, b_value):
    features, cols = weights[0].shape
    rows = tokens.shape[0]
    block = features // 2
    low = jax.ShapeDtypeStruct((LIVE, cols), jnp.bfloat16)
    row = whole((features,))
    heads = whole((LIVE, cols))
    return pl.pallas_call(
        front_kernel,
        grid=(2,),
        in_specs=[
            pl.BlockSpec(memory_space=pltpu.SMEM),
            whole((8, rows // 8)),
            pl.BlockSpec((rows, block), lambda i: (0, i)),
            row,
            row,
        ]
        + [ANYWHERE] * 3
        + [whole((cols,))] * 2,
        out_specs=[ANYWHERE] * 2
        + [pl.BlockSpec((LIVE, block), lambda i: (0, i))]
        + [ANYWHERE] * 2
        + [heads] * 5,
        out_shape=[
            in_hbm((LIVE, rows), jnp.bfloat16),
            in_hbm((LIVE, LIVE), jnp.float32),
        ]
        + [in_hbm((LIVE, features), jnp.bfloat16)] * 3
        + [in_hbm((LIVE, cols), jnp.bfloat16)] * 3
        + [low]
        + [in_hbm((LIVE, cols), jnp.float32)],
        scratch_shapes=[
            pltpu.VMEM((LIVE, features), jnp.bfloat16),
            pltpu.VMEM((features, 3 * cols), jnp.bfloat16),
            pltpu.VMEM((LIVE, rows), jnp.bfloat16),
            pltpu.VMEM((LIVE, LIVE), jnp.float32),
            pltpu.VMEM((LIVE, features), jnp.bfloat16),
            pltpu.VMEM((LIVE, features), jnp.bfloat16),
            pltpu.SemaphoreType.DMA((3,)),
            pltpu.SemaphoreType.DMA((4,)),
        ],
        compiler_params=grant(44),
        cost_estimate=cost(
            2 * LIVE * features * (rows + 3 * cols) + 16 * LIVE * LIVE * 128, 16, 4 * LIVE * LIVE
        ),
        name="front",
    )(
        *far_away(
            lengths, exits.reshape(8, rows // 8), tokens, gain, shift, *weights, b_query, b_value
        ),
    )


def pick_rows_kernel(pick_ref, full_ref, w_ref, *refs):
    rows_ref, product_ref, done_ref = refs[-3:]
    done_ref[...] = jnp.zeros_like(done_ref)
    rows = dot(pick_ref[...], full_ref[...]).astype(jnp.bfloat16)
    rows_ref[...] = rows
    product = back_dot(rows, w_ref[...])

    @pl.when(pl.program_id(0) == 0)
    def _():
        product_ref[...] = product

    @pl.when(pl.program_id(0) > 0)
    def _():
        product_ref[...] += product


def pick_rows(pick, full, weight, after):
    tokens, features = full.shape
    width = weight.shape[0]
    cols = 512
    return pl.pallas_call(
        pick_rows_kernel,
        grid=(features // cols,),
        in_specs=[
            whole((LIVE, tokens)),
            pl.BlockSpec((tokens, cols), lambda i: (0, i)),
            pl.BlockSpec((width, cols), lambda i: (0, i)),
        ]
        + [ANYWHERE] * len(after),
        out_specs=[pl.BlockSpec((LIVE, cols), lambda i: (0, i)), whole((LIVE, width)), whole((8, 128))],
        out_shape=[
            in_hbm((LIVE, features), jnp.bfloat16),
            in_hbm((LIVE, width), jnp.float32),
            DONE,
        ],
        compiler_params=grant(18),
        cost_estimate=cost(2 * LIVE * features * (tokens + width), 12),
        name="pick_rows",
    )(*far_away(pick, full, weight), *after)


def piece_specs(cols):
    return [pl.BlockSpec((128, cols), lambda i: (0, i))] * 4


def together(pieces):
    return jnp.concatenate([piece[...] for piece in pieces], axis=0)


def attend_back_kernel(
    p0, p1, p2, p3, w_ref, q_ref, k_ref, v_ref, bias_ref, lse_ref,
    low_ref, gq_ref, gk_ref, gv_ref, sum_ref, mixed, key_sum, value_sum,
):
    step = pl.program_id(0)
    low = together((p0, p1, p2, p3)).astype(jnp.bfloat16)
    low_ref[...] = low
    product = back_dot(low, w_ref[...])

    @pl.when(step == 0)
    def _():
        mixed[...] = product

    @pl.when(step > 0)
    def _():
        mixed[...] += product

    @pl.when(step == pl.num_programs(0) - 1)
    def _():
        rows = LIVE
        width = q_ref.shape[1]
        lane = lax.broadcasted_iota(jnp.int32, (1, 128), 1)
        sum_ref[...] = jnp.zeros_like(sum_ref)
        for pair in range(width // 128):
            cols = slice(128 * pair, 128 * pair + 128)
            key_sum[...] = jnp.zeros_like(key_sum)
            value_sum[...] = jnp.zeros_like(value_sum)
            for part in range(LIVE // rows):
                here = slice(part * rows, part * rows + rows)
                bias = bias_ref[here, :]
                total = jnp.zeros((rows, 128), jnp.float32)
                for head in range(2):
                    inside = (lane // HEAD) == head
                    query = jnp.where(inside, q_ref[here, cols], 0)
                    grad = jnp.where(inside, mixed[here, cols], 0.0).astype(jnp.bfloat16)
                    first = 128 * pair + head * HEAD
                    logs = lse_ref[here, first : first + 1]
                    prob = jnp.exp(back_dot(query, k_ref[:, cols]) + bias - logs)
                    grad_prob = back_dot(grad, v_ref[:, cols])
                    inner = jnp.sum(prob * grad_prob, axis=-1, keepdims=True)
                    grad_scores = (prob * (grad_prob - inner)).astype(jnp.bfloat16)
                    total = jnp.where(inside, dot(grad_scores, k_ref[:, cols]), total)
                    key_sum[...] += outer_sum(grad_scores, query)
                    value_sum[...] += outer_sum(prob.astype(jnp.bfloat16), grad)
                grad_query = total.astype(jnp.bfloat16) * jnp.bfloat16(0.125)
                gq_ref[here, cols] = grad_query
                sum_ref[0:1, cols] += jnp.sum(
                    grad_query.astype(jnp.float32), axis=0, keepdims=True
                )
            gk_ref[:, cols] = key_sum[...].astype(jnp.bfloat16)
            grad_value = value_sum[...].astype(jnp.bfloat16)
            gv_ref[:, cols] = grad_value
            sum_ref[1:2, cols] = jnp.sum(grad_value.astype(jnp.float32), axis=0, keepdims=True)


def attend_back(pieces, w_out, query, keys, values, bias, logs):
    cols, features = w_out.shape
    block = 1024
    wide = pl.BlockSpec((LIVE, block), lambda i: (0, i))
    heads = whole((LIVE, cols))
    return pl.pallas_call(
        attend_back_kernel,
        grid=(features // block,),
        in_specs=piece_specs(block)
        + [pl.BlockSpec((cols, block), lambda i: (0, i))]
        + [heads] * 3
        + [whole((LIVE, LIVE)), heads],
        out_specs=[wide] + [heads] * 3 + [whole((8, cols))],
        out_shape=[in_hbm((LIVE, features), jnp.bfloat16)]
        + [in_hbm((LIVE, cols), jnp.bfloat16)] * 3
        + [jax.ShapeDtypeStruct((8, cols), jnp.float32)],
        scratch_shapes=[pltpu.VMEM((LIVE, cols), jnp.float32)]
        + [pltpu.VMEM((LIVE, 128), jnp.float32)] * 2,
        compiler_params=grant(26),
        cost_estimate=cost(40 * LIVE * LIVE * 128, 11, 4 * LIVE * LIVE),
        name="attend_back",
    )(*pieces, *far_away(w_out, query, keys, values, bias, logs))


def ffn_kernel(places, *refs):
    count = len(places)
    gain_ref, shift_ref, up_ref, bias_ref, grad_hbm = refs[count : count + 5]
    act_hbm, inner_hbm, pre_hbm, sum_ref = refs[-10:-6]
    act_ref, inner_ref, pre_ref, grad_ref, in_sems, out_sems = refs[-6:]

    def rows_of(ref, i):
        return ref.at[pl.ds(128 * i, 128), :]

    grads = [
        pltpu.make_async_copy(rows_of(grad_hbm, place), rows_of(grad_ref, i), in_sems.at[i])
        for i, place in enumerate(places)
    ]
    outs = [
        [
            pltpu.make_async_copy(rows_of(here, i), rows_of(there, place), out_sems.at[k, i])
            for i, place in enumerate(places)
        ]
        for k, (here, there) in enumerate(
            ((act_ref, act_hbm), (inner_ref, inner_hbm), (pre_ref, pre_hbm))
        )
    ]
    for copy in grads:
        copy.start()
    sum_ref[...] = jnp.zeros_like(sum_ref)
    for i in range(count):
        here = slice(128 * i, 128 * i + 128)
        act = (refs[i][...] * gain_ref[...] + shift_ref[...]).astype(jnp.bfloat16)
        act_ref[here, :] = act
        outs[0][i].start()
        total = dot(act, up_ref[...]) + bias_ref[...]
        grads[i].wait()
        square = total * total
        bent = jnp.tanh(GELU_A * total * (1.0 + GELU_B * square))
        side = 0.5 * (1.0 + bent)
        inner_ref[here, :] = (total * side).astype(jnp.bfloat16)
        outs[1][i].start()
        slope = side + 0.5 * GELU_A * total * (1.0 - bent * bent) * (1.0 + 3.0 * GELU_B * square)
        grad = (slope * grad_ref[here, :]).astype(jnp.bfloat16)
        pre_ref[here, :] = grad
        outs[2][i].start()
        sum_ref[...] += jnp.sum(grad.astype(jnp.float32).reshape(16, 8, -1), axis=0)
    for copies in outs:
        for copy in copies:
            copy.wait()


def ffn(places, pieces, gain, shift, w_up, b_up, grad_inner, before=()):
    features, width = w_up.shape
    count = len(places)
    near = pl.BlockSpec(memory_space=pltpu.VMEM)
    shapes = [(LIVE, features), (LIVE, width), (LIVE, width)]
    return pl.pallas_call(
        functools.partial(ffn_kernel, places),
        in_specs=[near] * (count + 4) + [ANYWHERE] * (1 + len(before)),
        out_specs=[ANYWHERE] * 3 + [near],
        out_shape=[in_hbm(shape, jnp.bfloat16) for shape in shapes]
        + [jax.ShapeDtypeStruct((8, width), jnp.float32)],
        input_output_aliases={count + 5 + i: i for i in range(len(before))},
        scratch_shapes=[
            pltpu.VMEM((128 * count, features), jnp.bfloat16),
            pltpu.VMEM((128 * count, width), jnp.bfloat16),
            pltpu.VMEM((128 * count, width), jnp.bfloat16),
            pltpu.VMEM((128 * count, width), jnp.float32),
            pltpu.SemaphoreType.DMA((count,)),
            pltpu.SemaphoreType.DMA((3, count)),
        ],
        compiler_params=grant(20),
        cost_estimate=cost(256 * count * features * width, 4, 128 * count * width),
        name="ffn",
    )(*pieces, gain, shift, w_up, b_up, *far_away(grad_inner, *before))


def ffn_grads_kernel(out_grad_ref, inner_ref, act_ref, pre_ref, out_ref, done_ref):
    width = inner_ref.shape[1]
    done_ref[...] = jnp.zeros_like(done_ref)
    out_ref[:, 0:width] = outer_sum(out_grad_ref[...], inner_ref[...])
    out_ref[:, width:] = outer_sum(act_ref[...], pre_ref[...])


def ffn_grads(out_grad, inner, act, grad_pre):
    features, width = act.shape[1], inner.shape[1]
    half = grad_pre.shape[1] // 2
    rows = 512
    left = pl.BlockSpec((LIVE, rows), lambda i: (0, i))
    return pl.pallas_call(
        ffn_grads_kernel,
        grid=(features // rows,),
        in_specs=[left, whole((LIVE, width)), left, whole((LIVE, half))],
        out_specs=[pl.BlockSpec((rows, width + half), lambda i: (i, 0)), whole((8, 128))],
        out_shape=[in_hbm((features, width + half), jnp.float32), DONE],
        compiler_params=grant(18),
        cost_estimate=cost(3 * LIVE * features * width, 18),
        name="ffn_grads",
    )(*far_away(out_grad, inner, act, grad_pre))


def more_grads_kernel(act_two_ref, pre_ref, act_one_ref, gq, gk, gv, attn_ref, attended_ref, *refs):
    out_ref = refs[-1]
    half, cols = pre_ref.shape[1], gq.shape[1]
    out_ref[:, 0:half] = outer_sum(act_two_ref[...], pre_ref[...])
    act_one = act_one_ref[...]
    for i, grad_ref in enumerate((gq, gk, gv)):
        out_ref[:, half + cols * i : half + cols * i + cols] = outer_sum(act_one, grad_ref[...])
    out_ref[:, half + 3 * cols :] = outer_sum(attn_ref[...], attended_ref[...])


def more_grads(act_two, grad_pre, act_one, heads, grad_attn, attended, after):
    features, cols = act_two.shape[1], attended.shape[1]
    half = grad_pre.shape[1] // 2
    rows = 512
    left = pl.BlockSpec((LIVE, rows), lambda i: (0, i))
    head = whole((LIVE, cols))
    width = half + 4 * cols
    return pl.pallas_call(
        more_grads_kernel,
        grid=(features // rows,),
        in_specs=[left, pl.BlockSpec((LIVE, half), lambda i: (0, 1)), left]
        + [head] * 3
        + [left, head]
        + [ANYWHERE] * len(after),
        out_specs=pl.BlockSpec((rows, width), lambda i: (i, 0)),
        out_shape=in_hbm((features, width), jnp.float32),
        compiler_params=grant(18),
        cost_estimate=cost(2 * LIVE * features * width, 20),
        name="more_grads",
    )(*far_away(act_two, grad_pre, act_one, *heads, grad_attn, attended), *after)


def vectors_kernel(perm_ref, norm_one_ref, norm_two_ref, heads_ref, up_ref, out_ref):
    lane = iota((8, 128), 1)
    for place in range(16):
        share = perm_ref[place]
        here = pl.ds(pl.multiple_of(share * 128, 128), 128)
        heads = heads_ref[:, pl.ds(pl.multiple_of((share >> 3) * 128, 128), 128)]
        heads = pltpu.roll(heads, 128 - 16 * (share & 7), 1)
        up = up_ref[:, pl.ds(pl.multiple_of((share >> 1) * 128, 128), 128)]
        up = pltpu.roll(up, 64 * (1 - (share & 1)), 1)
        up = jnp.broadcast_to(jnp.sum(up, axis=0, keepdims=True), (8, 128))
        own = jnp.where(lane < 16, heads, jnp.where(lane < 64, 0.0, up))
        out_ref[8 * place : 8 * place + 2, :] = norm_one_ref[0:2, here]
        out_ref[8 * place + 2 : 8 * place + 6, :] = norm_two_ref[0:4, here]
        out_ref[8 * place + 6 : 8 * place + 8, :] = own[0:2, :]


def vectors_of(perm, norm_one, norm_two, heads, up):
    values = (norm_one, norm_two, heads, up)
    return pl.pallas_call(
        vectors_kernel,
        in_specs=[pl.BlockSpec(memory_space=pltpu.SMEM)]
        + [pl.BlockSpec(value.shape, lambda: (0, 0)) for value in values],
        out_specs=pl.BlockSpec((128, 128), lambda: (0, 0)),
        out_shape=jax.ShapeDtypeStruct((128, 128), jnp.float32),
        compiler_params=grant(6),
        cost_estimate=cost(0, 1),
        name="vectors_of",
    )(perm, *values)


def turn_kernel(share_ref, out_ref):
    out_ref[...] = share_ref[...].T


def turn(share, width):
    rows = share.shape[0]
    return pl.pallas_call(
        turn_kernel,
        grid=(1,),
        in_specs=[pl.BlockSpec((rows, width), lambda i: (0, 0))],
        out_specs=whole((width, rows)),
        out_shape=in_hbm((width, rows), jnp.float32),
        compiler_params=grant(6),
        cost_estimate=cost(0, 2),
        name="turn",
    )(*far_away(share))


def deal_kernel(left_ref, right_ref, up_ref, gq, gk, gv, out_ref):
    half, cols = left_ref.shape[1], gq.shape[1]
    up_ref[:, 0:half] = left_ref[...]
    up_ref[:, half:] = right_ref[:, 0:half]
    for i, ref in enumerate((gq, gk, gv)):
        ref[...] = right_ref[:, half + cols * i : half + cols * i + cols]
    out_ref[...] = right_ref[:, half + 3 * cols :].T


def deal(first, second, half, cols):
    rows = first.shape[0]
    shapes = [(rows, 2 * half)] + [(rows, cols)] * 3 + [(cols, rows)]
    return pl.pallas_call(
        deal_kernel,
        grid=(1,),
        in_specs=[
            pl.BlockSpec((rows, half), lambda i: (0, first.shape[1] // half - 1)),
            whole(second.shape),
        ],
        out_specs=[whole(shape) for shape in shapes],
        out_shape=[in_hbm(shape, jnp.float32) for shape in shapes],
        compiler_params=grant(8),
        cost_estimate=cost(0, 3),
        name="deal",
    )(*far_away(first, second))


def spread_kernel(place_ref, tokens_ref, grads_ref, live_ref, *refs):
    for i, (full_ref, out_ref) in enumerate(zip((tokens_ref, grads_ref), refs[-2:])):
        rows = jnp.concatenate(
            [
                ref[64 * part + 32 * i : 64 * part + 32 * i + 32, :]
                for ref in refs[:4]
                for part in range(4)
            ],
            axis=0,
        )
        wide = dot(place_ref[...], rows.astype(jnp.bfloat16)).astype(jnp.bfloat16)
        for first in range(0, wide.shape[1], 128):
            here = slice(first, first + 128)
            out_ref[:, here] = jnp.where(live_ref[...] > 0, wide[:, here], full_ref[:, here])


def spread(place, tokens, grads, live, pieces):
    count, features = tokens.shape
    cols = 512
    block = pl.BlockSpec((count, cols), lambda i: (0, i))
    return pl.pallas_call(
        spread_kernel,
        grid=(features // cols,),
        in_specs=[whole((count, LIVE)), block, block, whole((count, 128))]
        + [pl.BlockSpec((256, cols), lambda i: (0, i))] * 4,
        out_specs=[block] * 2,
        out_shape=[in_hbm(tokens.shape, jnp.bfloat16)] * 2,
        compiler_params=grant(32),
        cost_estimate=cost(4 * count * LIVE * features, 28),
        name="spread",
    )(place, *far_away(tokens, grads), live, *pieces)


def local(
    tokens,
    cotangent,
    lengths,
    exits,
    w_query,
    b_query,
    w_key,
    w_value,
    b_value,
    w_out,
    b_out,
    gain_one,
    shift_one,
    gain_two,
    shift_two,
    w_up,
    b_up,
    w_down,
    b_down,
):
    f32, bf16 = jnp.float32, jnp.bfloat16
    bits = own_bits()
    at_dp = lax.axis_index("dp")
    y_high, z_high = at_dp >> 3, (at_dp >> 1) & 1
    y_gray, z_gray = ((at_dp >> 2) & 1) ^ y_high, (at_dp & 1) ^ z_high
    dp_bits = (y_gray, y_high, z_gray, z_high)

    def direct_place(rank):
        side, one, two = (rank >> 6) & 1, (rank >> 7) & 1, (rank >> 5) & 1
        gray, high = jnp.where(side == 1, two, one), jnp.where(side == 1, one, two)
        distance = (x_place - (2 * high + (gray ^ high))) & 3
        return 256 * ((rank >> 8) ^ bits[0]) + 64 * distance + 32 * side + (rank & 31)

    def dp_blocks(order):
        own = jnp.arange(16, dtype=jnp.int32)
        bits = [None] * 4
        for place, (_, bit) in enumerate(order):
            bits[bit] = ((own >> (3 - place)) & 1) ^ dp_bits[bit]
        return 4 * (2 * bits[1] + (bits[0] ^ bits[1])) + 2 * bits[3] + (bits[2] ^ bits[3])

    perm = dp_blocks(HALVES)

    gain_one_f, gain_two_f = gain_one.astype(f32)[None], gain_two.astype(f32)[None]
    pick, bias, source_low, act_one, normal_low, query, keys, values, attended, logs = front(
        lengths,
        exits,
        tokens,
        gain_one,
        shift_one,
        (w_query, w_key, w_value),
        b_query,
        b_value,
    )

    source_mine = jnp.concatenate([source_low[0:32], source_low[64:96]], axis=0).astype(f32)
    normal_one, scale_one = normed(source_mine)
    scale_one = jnp.broadcast_to(scale_one, (64, 128))
    begun = scatter_begin(both_parts(attended, w_out, False))
    grad_out_low, grad_inner, picked = pick_rows(pick, cotangent, w_down, begun[4:])
    terms_a, terms_b, _ = scatter_end(begun, (picked,))
    hidden_mine, normal_two, normal_a, normal_b, scale_two = norm_two(
        terms_a + [(source_low, 0)], terms_b + [(source_low, 2)], b_out.astype(f32)[None]
    )
    place_all = jnp.arange(tokens.shape[0], dtype=jnp.int32)
    living = exits > LAYER
    below = (place_all[None, :] <= place_all[:, None]) & living[None, :]
    rank = jnp.sum(jnp.where(below, 1, 0), axis=1) - 1
    own_index = jnp.arange(LIVE, dtype=jnp.int32)
    living_column = jnp.broadcast_to(living.astype(bf16)[:, None], (tokens.shape[0], 128))
    row_of = jnp.where(living, own_place(rank, bits), -1)
    place = (row_of[:, None] == own_index[None, :]).astype(bf16)

    shift_two_f, b_up_f = shift_two.astype(f32)[None], b_up.astype(f32)[None]
    weights = (gain_two_f, shift_two_f, w_up, b_up_f, grad_inner)
    begun = []

    def first_piece(piece):
        begun.extend(ffn((0,), (piece,), *weights))
        return begun[3:]

    normal_pieces, _ = gather_rows(normal_a, normal_b, first_piece)
    *begun, sum_up = begun
    *begun, more_up = ffn((1, 2), normal_pieces[1:3], *weights, begun)
    act_two, inner, grad_pre, last_up = ffn((3,), normal_pieces[3:], *weights, begun)
    sum_up = sum_up + more_up + last_up
    first_grads, first_done = ffn_grads(grad_out_low, inner, act_two, grad_pre)
    begun = scatter_begin(both_parts(grad_pre, w_up, True, (first_done,)))
    first_share = lax.psum_scatter(first_grads, "dp", scatter_dimension=0, tiled=True)
    terms_a, terms_b, sent = scatter_end(begun)

    out_pieces = both_parts(inner, w_down, False, sent)
    hidden_a, hidden_b, grad_hidden_mine, sums_two = norm_back(
        terms_a,
        terms_b,
        ((normal_two, 0), (normal_two, 1)),
        ((grad_out_low, 0), (grad_out_low, 2)),
        scale_two,
        gain_two_f,
        out_pieces[0:1],
    )
    hidden_pieces, last_pieces = gather_rows(hidden_a, hidden_b)
    out_begun = scatter_begin(out_pieces, lambda: last_pieces)
    grad_attn_low, grad_query, grad_key, grad_value, sums_heads = attend_back(
        hidden_pieces, w_out, query, keys, values, bias, logs
    )
    heads = (grad_query, grad_key, grad_value)
    *pieces, sums_one = all_parts(heads, (w_query, w_key, w_value), normal_low)

    shares = [vectors_of(perm, sums_one, sums_two, sums_heads, sum_up)]
    for count, (pairs, _) in zip((64, 32, 16, 8), HALVES):
        last = shares[-1]
        shares.append(last[0:count] + over_dp(last[count : 2 * count], pairs))

    out_a, out_b, out_sent = scatter_end(out_begun, (sums_one,))
    second_grads = more_grads(
        act_two, grad_pre, act_one, heads, grad_attn_low, attended, (sums_one, *out_sent)
    )
    begun = scatter_begin(pieces, lambda: (*out_sent, shares[1]))
    second_share = lax.psum_scatter(second_grads, "dp", scatter_dimension=0, tiled=True)
    terms_a, terms_b, _ = scatter_end(begun, (shares[3],))

    _, _, input_mine, _ = norm_back(
        terms_a,
        terms_b,
        ((normal_one, 0), (normal_one, 1)),
        ((grad_hidden_mine, 0), (grad_hidden_mine, 1)),
        scale_one,
        gain_one_f,
        (shares[4],),
    )
    mine = last_rows(out_a, out_b, hidden_mine, b_down.astype(f32)[None], input_mine)
    output_full, input_full = spread(
        place, tokens, cotangent, living_column, gather_rows(*mine)[0]
    )
    share_down = turn(first_share, inner.shape[1])

    own_share = shares[4]
    share_up, *attn_shares = deal(first_share, second_share, inner.shape[1] // 2, attended.shape[1])
    common_share = own_share
    for pairs in (CORE, X_NEAR, X_FAR):
        common_share = common_share + over_tensor(common_share, pairs)
    return (
        output_full,
        input_full,
        attn_shares[0],
        own_share[6, 0:16],
        attn_shares[1],
        attn_shares[2],
        own_share[7, 0:16],
        attn_shares[3],
        common_share[4],
        common_share[0],
        common_share[1],
        common_share[2],
        common_share[3],
        share_up,
        own_share[6, 64:128],
        share_down,
        common_share[5],
    )


def solution(mesh):
    in_specs = (
        P("dp", None),
        P("dp", None),
        P("dp", None),
        P("dp"),
        P(None, "tensor"),
        P("tensor"),
        P(None, "tensor"),
        P(None, "tensor"),
        P("tensor"),
        P("tensor", None),
        P(),
        P(),
        P(),
        P(),
        P(),
        P(None, "tensor"),
        P("tensor"),
        P("tensor", None),
        P(),
    )
    out_specs = (
        P("dp", None),
        P("dp", None),
        P("dp", "tensor"),
        P(("tensor", "dp")),
        P("dp", "tensor"),
        P("dp", "tensor"),
        P(("tensor", "dp")),
        P("tensor", "dp"),
        P("dp"),
        P("dp"),
        P("dp"),
        P("dp"),
        P("dp"),
        P("dp", "tensor"),
        P(("tensor", "dp")),
        P("tensor", "dp"),
        P("dp"),
    )
    return jax.shard_map(local, mesh=mesh, in_specs=in_specs, out_specs=out_specs, check_vma=False)
```

```python
import functools

import jax
import jax.numpy as jnp
from jax import lax
from jax.experimental import pallas as pl
from jax.experimental.pallas import tpu as pltpu
from jax.sharding import PartitionSpec as P

HEAD = 64
LAYER = 12
LIVE = 512
NEG_BIG = -1e30
EPSILON = 1e-05
GELU_A = 0.7978845608028654
GELU_B = 0.044715

CORE = [(i, i ^ 1) for i in range(8)]
X_NEAR = [(2 * x + c, 2 * (x ^ 1) + c) for x in range(4) for c in range(2)]
X_FAR = [(2 * x + c, 2 * (3 - x) + c) for x in range(4) for c in range(2)]
Y_NEAR = [(4 * y + z, 4 * (y ^ 1) + z) for y in range(4) for z in range(4)]
Y_FAR = [(4 * y + z, 4 * (3 - y) + z) for y in range(4) for z in range(4)]
Z_NEAR = [(4 * y + z, 4 * y + (z ^ 1)) for y in range(4) for z in range(4)]
Z_FAR = [(4 * y + z, 4 * y + (3 - z)) for y in range(4) for z in range(4)]
HALVES = ((Y_NEAR, 0), (Y_FAR, 1), (Z_NEAR, 2), (Z_FAR, 3))


def over_tensor(value, pairs):
    return lax.ppermute(value, "tensor", pairs)


def over_dp(value, pairs):
    return lax.ppermute(value, "dp", pairs)


def dot(left, right):
    return jnp.dot(left, right, preferred_element_type=jnp.float32)


def back_dot(left, right):
    return lax.dot_general(
        left, right, (((1,), (1,)), ((), ())), preferred_element_type=jnp.float32
    )


def outer_sum(left, right):
    return lax.dot_general(
        left, right, (((0,), (0,)), ((), ())), preferred_element_type=jnp.float32
    )


def normed(values):
    average = jnp.mean(values, axis=-1, keepdims=True)
    centred = values - average
    spread = jnp.mean(centred * centred, axis=-1, keepdims=True)
    scale = lax.rsqrt(spread + EPSILON)
    return centred * scale, scale


def grant(mib, **more):
    return pltpu.CompilerParams(vmem_limit_bytes=mib << 20, **more)


def cost(flops, mib, transcendentals=0):
    return pl.CostEstimate(
        flops=flops, bytes_accessed=int(mib * 1048576), transcendentals=transcendentals
    )


ANYWHERE = pl.BlockSpec(memory_space=pl.ANY)


def far_away(*values):
    return [pltpu.with_memory_space_constraint(value, pltpu.HBM) for value in values]


def in_hbm(shape, dtype):
    return pltpu.HBM(shape, dtype)


DONE = jax.ShapeDtypeStruct((8, 128), jnp.float32)


def whole(shape):
    return pl.BlockSpec(shape, lambda *i: (0,) * len(shape))


def parts_kernel(transposed, left_ref, right_ref, *refs):
    total = (back_dot if transposed else dot)(left_ref[...], right_ref[...])
    first, second = refs[-2:]
    first[...] = total[0:128]
    second[...] = total[128:256]


def parts(lefts, rights, transposed, half, after=()):
    (left,), (right,) = lefts, rights
    depth = left.shape[1]
    features = right.shape[0 if transposed else 1]
    cols = 1024
    block = (
        pl.BlockSpec((cols, depth), lambda i: (i, 0))
        if transposed
        else pl.BlockSpec((depth, cols), lambda i: (0, i))
    )
    return pl.pallas_call(
        functools.partial(parts_kernel, transposed),
        grid=(features // cols,),
        in_specs=[pl.BlockSpec((256, depth), lambda i: (half, 0)), block] + [ANYWHERE] * len(after),
        out_specs=[pl.BlockSpec((128, cols), lambda i: (0, i))] * 2,
        out_shape=[jax.ShapeDtypeStruct((128, features), jnp.float32)] * 2,
        compiler_params=grant(18),
        cost_estimate=cost(2 * 256 * depth * features, 6),
        name="parts",
    )(left, right, *after)


def all_parts_kernel(count, *refs):
    total = None
    for left, right in zip(refs[:count], refs[count : 2 * count]):
        product = back_dot(left[...], right[...])
        total = product if total is None else total + product
    normal_ref, sum_ref = refs[2 * count], refs[-1]
    sum_ref[...] = jnp.zeros_like(sum_ref)
    sum_ref[0:1, :] = jnp.sum(total * normal_ref[...].astype(jnp.float32), axis=0, keepdims=True)
    sum_ref[1:2, :] = jnp.sum(total, axis=0, keepdims=True)
    for i in range(4):
        refs[2 * count + 1 + i][...] = total[128 * i : 128 * i + 128]


def all_parts(lefts, rights, normal):
    count, depth = len(lefts), lefts[0].shape[1]
    features = rights[0].shape[0]
    cols = 1024
    return pl.pallas_call(
        functools.partial(all_parts_kernel, count),
        grid=(features // cols,),
        in_specs=[whole((LIVE, depth))] * count
        + [pl.BlockSpec((cols, depth), lambda i: (i, 0))] * count
        + [pl.BlockSpec((LIVE, cols), lambda i: (0, i))],
        out_specs=[pl.BlockSpec((128, cols), lambda i: (0, i))] * 4
        + [pl.BlockSpec((8, cols), lambda i: (0, i))],
        out_shape=[jax.ShapeDtypeStruct((128, features), jnp.float32)] * 4
        + [jax.ShapeDtypeStruct((8, features), jnp.float32)],
        compiler_params=grant(26),
        cost_estimate=cost(2 * LIVE * depth * count * features, 10),
        name="all_parts",
    )(*far_away(*lefts, *rights, normal))


def add_kernel(counts, *refs):
    outs = refs[-len(counts) :]
    first = 0
    for out_ref, count in zip(outs, counts):
        out_ref[...] = summed(refs[first : first + count])
        first += count


def add(sums, rows, after=()):
    features = sums[0][0][0].shape[1]
    cols = 1024
    return pl.pallas_call(
        functools.partial(add_kernel, [len(terms) for terms in sums]),
        grid=(features // cols,),
        in_specs=[
            pl.BlockSpec((rows, cols), lambda i, block=block: (block, i))
            for terms in sums
            for _, block in terms
        ]
        + [ANYWHERE] * len(after),
        out_specs=[pl.BlockSpec((rows, cols), lambda i: (0, i))] * len(sums),
        out_shape=[jax.ShapeDtypeStruct((rows, features), jnp.float32)] * len(sums),
        compiler_params=grant(6),
        cost_estimate=cost(0, 2),
        name="add",
    )(*[array for terms in sums for array, _ in terms], *after)


def scatter_begin(pieces, early=None):
    near, far = pieces[0:2]
    core_far = over_tensor(pieces[3], CORE)
    core_near = over_tensor(pieces[2], CORE)
    done = early() if early else ()
    far_a, far_b = add([[(far, i), (core_far, i)] for i in range(2)], 64, done)
    got_a = over_tensor(far_a, X_NEAR)
    got_b = over_tensor(far_b, X_FAR)
    return near, core_near, got_a, got_b, far_a


def scatter_end(begun, after=()):
    near, core_near, got_a, got_b, _ = begun
    sends = [
        add([[(near, block), (core_near, block), (got, 1)]], 32, after)[0]
        for got, block in ((got_a, 1), (got_b, 3))
    ]
    last_a, last_b = [over_tensor(send, pairs) for send, pairs in zip(sends, (X_FAR, X_NEAR))]
    return (
        [(near, 0), (core_near, 0), (got_a, 0), (last_a, 0)],
        [(near, 2), (core_near, 2), (got_b, 0), (last_b, 0)],
        sends,
    )


def both_parts(left, right, transposed, after=()):
    sent = parts((left,), (right,), transposed, 1, after)
    return [*parts((left,), (right,), transposed, 0, sent[0:1]), *sent]


def join_kernel(*refs):
    rows = refs[0].shape[0]
    for i in range(4):
        refs[-1][rows * i : rows * i + rows, :] = refs[i][...]


def join(pieces, after=()):
    rows, features = pieces[0].shape
    cols = 1024
    return pl.pallas_call(
        join_kernel,
        grid=(features // cols,),
        in_specs=[pl.BlockSpec((rows, cols), lambda i: (0, i))] * 4 + [ANYWHERE] * len(after),
        out_specs=pl.BlockSpec((4 * rows, cols), lambda i: (0, i)),
        out_shape=jax.ShapeDtypeStruct((4 * rows, features), jnp.float32),
        compiler_params=grant(10),
        cost_estimate=cost(0, 2),
        name="join",
    )(*pieces, *after)


def gather_rows(mine_a, mine_b, beside=None):
    a01 = over_tensor(mine_a, X_FAR)
    b01 = over_tensor(mine_b, X_NEAR)
    a10 = over_tensor(mine_a, X_NEAR)
    b10 = over_tensor(mine_b, X_FAR)
    a11 = over_tensor(a01, X_NEAR)
    b11 = over_tensor(b01, X_FAR)
    first = join((mine_a, a01, mine_b, b01))
    second = join((a10, a11, b10, b11), beside(first) if beside else ())
    return (first, second, over_tensor(first, CORE), over_tensor(second, CORE)), (a11, b11)


def row_block(pair, features):
    return pl.BlockSpec((32, features), lambda i, block=pair[1]: (block, 0))


def summed(refs):
    return sum(ref[...].astype(jnp.float32) for ref in refs[1:]) + refs[0][...]


def norm_two_kernel(*refs):
    bias_ref, hidden_ref, rows_ref, scale_ref = refs[10], refs[11], refs[12], refs[15]
    for i in range(2):
        here = slice(32 * i, 32 * i + 32)
        hidden = summed(refs[5 * i : 5 * i + 5]) + bias_ref[...]
        normal, scale = normed(hidden)
        hidden_ref[here, :] = hidden
        rows_ref[here, :] = normal
        refs[13 + i][...] = normal
        scale_ref[here, :] = jnp.broadcast_to(scale, (32, 128))


def norm_two(terms_a, terms_b, bias):
    features = bias.shape[1]
    terms = terms_a + terms_b
    rows, piece = (64, features), (32, features)
    return pl.pallas_call(
        norm_two_kernel,
        grid=(1,),
        in_specs=[row_block(term, features) for term in terms] + [whole((1, features))],
        out_specs=[whole(rows)] * 2 + [whole(piece)] * 2 + [whole((64, 128))],
        out_shape=[in_hbm(rows, jnp.float32)] * 2
        + [jax.ShapeDtypeStruct(piece, jnp.float32)] * 2
        + [in_hbm((64, 128), jnp.float32)],
        compiler_params=grant(10),
        cost_estimate=cost(20 * 64 * features, 4),
        name="norm_two",
    )(*[term[0] for term in terms], bias)


def last_rows_kernel(*refs):
    hidden_ref, bias_ref, input_ref = refs[8:11]
    for i in range(2):
        here = slice(32 * i, 32 * i + 32)
        out_ref = refs[-2 + i]
        out_ref[0:32, :] = summed(refs[4 * i : 4 * i + 4]) + (hidden_ref[here, :] + bias_ref[...])
        out_ref[32:64, :] = input_ref[here, :]


def last_rows(terms_a, terms_b, hidden, bias, input_mine):
    features = bias.shape[1]
    terms = terms_a + terms_b
    rows = whole((64, features))
    return pl.pallas_call(
        last_rows_kernel,
        grid=(1,),
        in_specs=[row_block(term, features) for term in terms] + [rows, whole((1, features)), rows],
        out_specs=[rows] * 2,
        out_shape=[jax.ShapeDtypeStruct((64, features), jnp.float32)] * 2,
        compiler_params=grant(12),
        cost_estimate=cost(20 * 64 * features, 4),
        name="last_rows",
    )(*[term[0] for term in terms], hidden, bias, input_mine)


def norm_back_kernel(*refs):
    scale_ref, gain_ref = refs[12:14]
    pieces, total_ref, sums_ref = refs[-4:-2], refs[-2], refs[-1]
    sums_ref[...] = jnp.zeros_like(sums_ref)
    for i in range(2):
        here = slice(32 * i, 32 * i + 32)
        grad = summed(refs[4 * i : 4 * i + 4])
        normal = refs[8 + 2 * i][...]
        base = refs[9 + 2 * i][...].astype(jnp.float32)
        scaled = grad * gain_ref[...]
        first = jnp.mean(scaled, axis=-1, keepdims=True)
        second = jnp.mean(scaled * normal, axis=-1, keepdims=True)
        norm = scale_ref[here, 0:1] * (scaled - first - normal * second)
        total = base + norm
        pieces[i][...] = total
        total_ref[here, :] = total
        sums_ref[0:1, :] += jnp.sum(grad * normal, axis=0, keepdims=True)
        sums_ref[1:2, :] += jnp.sum(grad, axis=0, keepdims=True)
        sums_ref[2:3, :] += jnp.sum(total, axis=0, keepdims=True)
        sums_ref[3:4, :] += jnp.sum(base, axis=0, keepdims=True)


def norm_back(terms_a, terms_b, normals, bases, scale, gain, after=()):
    features = gain.shape[1]
    terms = terms_a + terms_b + [normals[0], bases[0], normals[1], bases[1]]
    piece = jax.ShapeDtypeStruct((32, features), jnp.float32)
    return pl.pallas_call(
        norm_back_kernel,
        grid=(1,),
        in_specs=[row_block(term, features) for term in terms]
        + [whole((64, 128)), whole((1, features))]
        + [ANYWHERE] * len(after),
        out_specs=[whole((32, features))] * 2 + [whole((64, features)), whole((8, features))],
        out_shape=[
            piece,
            piece,
            jax.ShapeDtypeStruct((64, features), jnp.float32),
            jax.ShapeDtypeStruct((8, features), jnp.float32),
        ],
        compiler_params=grant(8),
        cost_estimate=cost(20 * 64 * features, 4),
        name="norm_back",
    )(*[term[0] for term in terms], scale, gain, *after)


def own_bits():
    at = lax.axis_index("tensor")
    high = at >> 2
    return at & 1, ((at >> 1) & 1) ^ high, high


def own_place(rank, bits):
    core, gray, high = bits
    side = (rank >> 6) & 1
    one = side * high + (1 - side) * gray
    two = side * gray + (1 - side) * high
    return rank ^ (core << 8) ^ (one << 7) ^ (two << 5)


def iota(shape, axis):
    return lax.broadcasted_iota(jnp.int32, shape, axis)


def live_ranks(exits):
    living = exits > LAYER
    ones = jnp.where(living, 1.0, 0.0)
    up_to = (iota((128, 128), 0) <= iota((128, 128), 1)).astype(jnp.bfloat16)
    within = dot(ones.astype(jnp.bfloat16), up_to)
    totals = jnp.broadcast_to(jnp.sum(ones, axis=1, keepdims=True), (8, 128))
    before = jnp.zeros((8, 128), jnp.float32)
    for i in range(7):
        before += jnp.where(iota((8, 128), 0) > i, totals[i : i + 1, :], 0.0)
    return living, (within + before).astype(jnp.int32) - 1


def front_kernel(
    lengths_ref, exits_ref, tokens_ref, gain_ref, shift_ref, wq_hbm, wk_hbm, wv_hbm, bq_ref, bv_ref,
    pick_hbm, bias_hbm, source_ref, act_hbm, normal_hbm, q_ref, k_ref, v_ref, out_ref, lse_ref,
    rows_ref, w_ref, pick_ref, bias_ref, act_ref, normal_ref, sems, out_sems,
):
    step = pl.program_id(0)
    copies = [
        pltpu.make_async_copy(
            weight, w_ref.at[:, pl.ds(i * weight.shape[1], weight.shape[1])], sems.at[i]
        )
        for i, weight in enumerate((wq_hbm, wk_hbm, wv_hbm))
    ]
    outs = [
        pltpu.make_async_copy(here, there, out_sems.at[i])
        for i, (here, there) in enumerate(
            (
                (pick_ref, pick_hbm),
                (bias_ref, bias_hbm),
                (act_ref, act_hbm),
                (normal_ref, normal_hbm),
            )
        )
    ]

    @pl.when(step == 0)
    def _():
        for copy in copies:
            copy.start()
        bits = own_bits()
        living, rank = live_ranks(exits_ref[...])
        row_of = jnp.where(living, own_place(rank, bits), -1)
        for i in range(8):
            pick_ref[:, 128 * i : 128 * i + 128] = jnp.where(
                iota((LIVE, 128), 0) == row_of[i : i + 1, :], 1.0, 0.0
            ).astype(jnp.bfloat16)
        token = 128 * iota((8, 128), 0) + iota((8, 128), 1)
        rank_row = own_place(iota((1, LIVE), 1), bits)
        rank_column = own_place(iota((LIVE, 1), 0), bits)
        segment_row, segment_column = jnp.zeros_like(rank_row), jnp.zeros_like(rank_column)
        bound = 0
        for i in range(lengths_ref.shape[1] - 1):
            bound = bound + lengths_ref[0, i]
            count = jnp.sum(jnp.where(living & (token < bound), 1, 0))
            segment_row += (rank_row >= count).astype(jnp.int32)
            segment_column += (rank_column >= count).astype(jnp.int32)
        allowed = (segment_column == segment_row) & (rank_row <= rank_column)
        bias_ref[...] = jnp.where(allowed, 0.0, NEG_BIG)
        for out in outs[:2]:
            out.start()

    cols = tokens_ref.shape[1]
    found = dot(pick_ref[...], tokens_ref[...]).astype(jnp.bfloat16)
    source_ref[...] = found
    for i in range(2):

        @pl.when(step == i)
        def _(i=i):
            rows_ref[:, cols * i : cols * i + cols] = found

    @pl.when(step == pl.num_programs(0) - 1)
    def _():
        gain, shift = wide_row(gain_ref), wide_row(shift_ref)

        def some(i, carry):
            here = pl.ds(pl.multiple_of(i * 16, 16), 16)
            normal, _ = normed(rows_ref[here, :].astype(jnp.float32))
            normal_ref[here, :] = normal.astype(jnp.bfloat16)
            act_ref[here, :] = (normal * gain + shift).astype(jnp.bfloat16)
            return carry

        lax.fori_loop(0, LIVE // 16, some, 0, unroll=8)
        for out in outs[2:]:
            out.start()
        for copy in copies:
            copy.wait()
        width = q_ref.shape[1]
        product = dot(act_ref[...], w_ref[...])
        q_ref[...] = ((product[:, 0:width] + wide_row(bq_ref)) * 0.125).astype(jnp.bfloat16)
        k_ref[...] = product[:, width : 2 * width].astype(jnp.bfloat16)
        v_ref[...] = (product[:, 2 * width :] + wide_row(bv_ref)).astype(jnp.bfloat16)
        rows = LIVE
        lane = iota((1, 128), 1)
        for pair in range(q_ref.shape[1] // 128):
            at = slice(128 * pair, 128 * pair + 128)
            for part in range(LIVE // rows):
                here = slice(part * rows, part * rows + rows)
                bias = bias_ref[here, :]
                total = jnp.zeros((rows, 128), jnp.float32)
                logs = jnp.zeros((rows, 128), jnp.float32)
                for head in range(2):
                    inside = (lane // HEAD) == head
                    query = jnp.where(inside, q_ref[here, at], 0)
                    scores = back_dot(query, k_ref[:, at]) + bias
                    peak = jnp.max(scores, axis=-1, keepdims=True)
                    expo = jnp.exp(scores - peak)
                    total_expo = jnp.sum(expo, axis=-1, keepdims=True)
                    prob = (expo * (1.0 / total_expo)).astype(jnp.bfloat16)
                    total = jnp.where(inside, dot(prob, v_ref[:, at]), total)
                    logs = jnp.where(inside, peak + jnp.log(total_expo), logs)
                out_ref[here, at] = total.astype(jnp.bfloat16)
                lse_ref[here, at] = logs
        for out in outs:
            out.wait()


def wide_row(ref):
    return ref[...].astype(jnp.float32).reshape(1, -1)


def front(lengths, exits, tokens, gain, shift, weights, b_query, b_value):
    features, cols = weights[0].shape
    rows = tokens.shape[0]
    block = features // 2
    low = jax.ShapeDtypeStruct((LIVE, cols), jnp.bfloat16)
    row = whole((features,))
    heads = whole((LIVE, cols))
    return pl.pallas_call(
        front_kernel,
        grid=(2,),
        in_specs=[
            pl.BlockSpec(memory_space=pltpu.SMEM),
            whole((8, rows // 8)),
            pl.BlockSpec((rows, block), lambda i: (0, i)),
            row,
            row,
        ]
        + [ANYWHERE] * 3
        + [whole((cols,))] * 2,
        out_specs=[ANYWHERE] * 2
        + [pl.BlockSpec((LIVE, block), lambda i: (0, i))]
        + [ANYWHERE] * 2
        + [heads] * 5,
        out_shape=[
            in_hbm((LIVE, rows), jnp.bfloat16),
            in_hbm((LIVE, LIVE), jnp.float32),
        ]
        + [in_hbm((LIVE, features), jnp.bfloat16)] * 3
        + [in_hbm((LIVE, cols), jnp.bfloat16)] * 3
        + [low]
        + [in_hbm((LIVE, cols), jnp.float32)],
        scratch_shapes=[
            pltpu.VMEM((LIVE, features), jnp.bfloat16),
            pltpu.VMEM((features, 3 * cols), jnp.bfloat16),
            pltpu.VMEM((LIVE, rows), jnp.bfloat16),
            pltpu.VMEM((LIVE, LIVE), jnp.float32),
            pltpu.VMEM((LIVE, features), jnp.bfloat16),
            pltpu.VMEM((LIVE, features), jnp.bfloat16),
            pltpu.SemaphoreType.DMA((3,)),
            pltpu.SemaphoreType.DMA((4,)),
        ],
        compiler_params=grant(44),
        cost_estimate=cost(
            2 * LIVE * features * (rows + 3 * cols) + 16 * LIVE * LIVE * 128, 16, 4 * LIVE * LIVE
        ),
        name="front",
    )(
        *far_away(
            lengths, exits.reshape(8, rows // 8), tokens, gain, shift, *weights, b_query, b_value
        ),
    )


def pick_rows_kernel(pick_ref, full_ref, w_ref, *refs):
    rows_ref, product_ref, done_ref = refs[-3:]
    done_ref[...] = jnp.zeros_like(done_ref)
    rows = dot(pick_ref[...], full_ref[...]).astype(jnp.bfloat16)
    rows_ref[...] = rows
    product = back_dot(rows, w_ref[...])

    @pl.when(pl.program_id(0) == 0)
    def _():
        product_ref[...] = product

    @pl.when(pl.program_id(0) > 0)
    def _():
        product_ref[...] += product


def pick_rows(pick, full, weight, after):
    tokens, features = full.shape
    width = weight.shape[0]
    cols = 512
    return pl.pallas_call(
        pick_rows_kernel,
        grid=(features // cols,),
        in_specs=[
            whole((LIVE, tokens)),
            pl.BlockSpec((tokens, cols), lambda i: (0, i)),
            pl.BlockSpec((width, cols), lambda i: (0, i)),
        ]
        + [ANYWHERE] * len(after),
        out_specs=[pl.BlockSpec((LIVE, cols), lambda i: (0, i)), whole((LIVE, width)), whole((8, 128))],
        out_shape=[
            in_hbm((LIVE, features), jnp.bfloat16),
            in_hbm((LIVE, width), jnp.float32),
            DONE,
        ],
        compiler_params=grant(18),
        cost_estimate=cost(2 * LIVE * features * (tokens + width), 12),
        name="pick_rows",
    )(*far_away(pick, full, weight), *after)


def piece_specs(cols):
    return [pl.BlockSpec((128, cols), lambda i: (0, i))] * 4


def together(pieces):
    return jnp.concatenate([piece[...] for piece in pieces], axis=0)


def attend_back_kernel(
    p0, p1, p2, p3, w_ref, q_ref, k_ref, v_ref, bias_ref, lse_ref,
    low_ref, gq_ref, gk_ref, gv_ref, sum_ref, mixed, key_sum, value_sum,
):
    step = pl.program_id(0)
    low = together((p0, p1, p2, p3)).astype(jnp.bfloat16)
    low_ref[...] = low
    product = back_dot(low, w_ref[...])

    @pl.when(step == 0)
    def _():
        mixed[...] = product

    @pl.when(step > 0)
    def _():
        mixed[...] += product

    @pl.when(step == pl.num_programs(0) - 1)
    def _():
        rows = LIVE
        width = q_ref.shape[1]
        lane = lax.broadcasted_iota(jnp.int32, (1, 128), 1)
        sum_ref[...] = jnp.zeros_like(sum_ref)
        for pair in range(width // 128):
            cols = slice(128 * pair, 128 * pair + 128)
            key_sum[...] = jnp.zeros_like(key_sum)
            value_sum[...] = jnp.zeros_like(value_sum)
            for part in range(LIVE // rows):
                here = slice(part * rows, part * rows + rows)
                bias = bias_ref[here, :]
                total = jnp.zeros((rows, 128), jnp.float32)
                for head in range(2):
                    inside = (lane // HEAD) == head
                    query = jnp.where(inside, q_ref[here, cols], 0)
                    grad = jnp.where(inside, mixed[here, cols], 0.0).astype(jnp.bfloat16)
                    first = 128 * pair + head * HEAD
                    logs = lse_ref[here, first : first + 1]
                    prob = jnp.exp(back_dot(query, k_ref[:, cols]) + bias - logs)
                    grad_prob = back_dot(grad, v_ref[:, cols])
                    inner = jnp.sum(prob * grad_prob, axis=-1, keepdims=True)
                    grad_scores = (prob * (grad_prob - inner)).astype(jnp.bfloat16)
                    total = jnp.where(inside, dot(grad_scores, k_ref[:, cols]), total)
                    key_sum[...] += outer_sum(grad_scores, query)
                    value_sum[...] += outer_sum(prob.astype(jnp.bfloat16), grad)
                grad_query = total.astype(jnp.bfloat16) * jnp.bfloat16(0.125)
                gq_ref[here, cols] = grad_query
                sum_ref[0:1, cols] += jnp.sum(
                    grad_query.astype(jnp.float32), axis=0, keepdims=True
                )
            gk_ref[:, cols] = key_sum[...].astype(jnp.bfloat16)
            grad_value = value_sum[...].astype(jnp.bfloat16)
            gv_ref[:, cols] = grad_value
            sum_ref[1:2, cols] = jnp.sum(grad_value.astype(jnp.float32), axis=0, keepdims=True)


def attend_back(pieces, w_out, query, keys, values, bias, logs):
    cols, features = w_out.shape
    block = 1024
    wide = pl.BlockSpec((LIVE, block), lambda i: (0, i))
    heads = whole((LIVE, cols))
    return pl.pallas_call(
        attend_back_kernel,
        grid=(features // block,),
        in_specs=piece_specs(block)
        + [pl.BlockSpec((cols, block), lambda i: (0, i))]
        + [heads] * 3
        + [whole((LIVE, LIVE)), heads],
        out_specs=[wide] + [heads] * 3 + [whole((8, cols))],
        out_shape=[in_hbm((LIVE, features), jnp.bfloat16)]
        + [in_hbm((LIVE, cols), jnp.bfloat16)] * 3
        + [jax.ShapeDtypeStruct((8, cols), jnp.float32)],
        scratch_shapes=[pltpu.VMEM((LIVE, cols), jnp.float32)]
        + [pltpu.VMEM((LIVE, 128), jnp.float32)] * 2,
        compiler_params=grant(26),
        cost_estimate=cost(40 * LIVE * LIVE * 128, 11, 4 * LIVE * LIVE),
        name="attend_back",
    )(*pieces, *far_away(w_out, query, keys, values, bias, logs))


def ffn_kernel(places, *refs):
    count = len(places)
    gain_ref, shift_ref, up_ref, bias_ref, grad_hbm = refs[count : count + 5]
    act_hbm, inner_hbm, pre_hbm, sum_ref = refs[-10:-6]
    act_ref, inner_ref, pre_ref, grad_ref, in_sems, out_sems = refs[-6:]

    def rows_of(ref, i):
        return ref.at[pl.ds(128 * i, 128), :]

    grads = [
        pltpu.make_async_copy(rows_of(grad_hbm, place), rows_of(grad_ref, i), in_sems.at[i])
        for i, place in enumerate(places)
    ]
    outs = [
        [
            pltpu.make_async_copy(rows_of(here, i), rows_of(there, place), out_sems.at[k, i])
            for i, place in enumerate(places)
        ]
        for k, (here, there) in enumerate(
            ((act_ref, act_hbm), (inner_ref, inner_hbm), (pre_ref, pre_hbm))
        )
    ]
    for copy in grads:
        copy.start()
    sum_ref[...] = jnp.zeros_like(sum_ref)
    for i in range(count):
        here = slice(128 * i, 128 * i + 128)
        act = (refs[i][...] * gain_ref[...] + shift_ref[...]).astype(jnp.bfloat16)
        act_ref[here, :] = act
        outs[0][i].start()
        total = dot(act, up_ref[...]) + bias_ref[...]
        grads[i].wait()
        square = total * total
        bent = jnp.tanh(GELU_A * total * (1.0 + GELU_B * square))
        side = 0.5 * (1.0 + bent)
        inner_ref[here, :] = (total * side).astype(jnp.bfloat16)
        outs[1][i].start()
        slope = side + 0.5 * GELU_A * total * (1.0 - bent * bent) * (1.0 + 3.0 * GELU_B * square)
        grad = (slope * grad_ref[here, :]).astype(jnp.bfloat16)
        pre_ref[here, :] = grad
        outs[2][i].start()
        sum_ref[...] += jnp.sum(grad.astype(jnp.float32).reshape(16, 8, -1), axis=0)
    for copies in outs:
        for copy in copies:
            copy.wait()


def ffn(places, pieces, gain, shift, w_up, b_up, grad_inner, before=()):
    features, width = w_up.shape
    count = len(places)
    near = pl.BlockSpec(memory_space=pltpu.VMEM)
    shapes = [(LIVE, features), (LIVE, width), (LIVE, width)]
    return pl.pallas_call(
        functools.partial(ffn_kernel, places),
        in_specs=[near] * (count + 4) + [ANYWHERE] * (1 + len(before)),
        out_specs=[ANYWHERE] * 3 + [near],
        out_shape=[in_hbm(shape, jnp.bfloat16) for shape in shapes]
        + [jax.ShapeDtypeStruct((8, width), jnp.float32)],
        input_output_aliases={count + 5 + i: i for i in range(len(before))},
        scratch_shapes=[
            pltpu.VMEM((128 * count, features), jnp.bfloat16),
            pltpu.VMEM((128 * count, width), jnp.bfloat16),
            pltpu.VMEM((128 * count, width), jnp.bfloat16),
            pltpu.VMEM((128 * count, width), jnp.float32),
            pltpu.SemaphoreType.DMA((count,)),
            pltpu.SemaphoreType.DMA((3, count)),
        ],
        compiler_params=grant(20),
        cost_estimate=cost(256 * count * features * width, 4, 128 * count * width),
        name="ffn",
    )(*pieces, gain, shift, w_up, b_up, *far_away(grad_inner, *before))


def ffn_grads_kernel(out_grad_ref, inner_ref, act_ref, pre_ref, out_ref, done_ref):
    width = inner_ref.shape[1]
    done_ref[...] = jnp.zeros_like(done_ref)
    out_ref[:, 0:width] = outer_sum(out_grad_ref[...], inner_ref[...])
    out_ref[:, width:] = outer_sum(act_ref[...], pre_ref[...])


def ffn_grads(out_grad, inner, act, grad_pre):
    features, width = act.shape[1], inner.shape[1]
    half = grad_pre.shape[1] // 2
    rows = 512
    left = pl.BlockSpec((LIVE, rows), lambda i: (0, i))
    return pl.pallas_call(
        ffn_grads_kernel,
        grid=(features // rows,),
        in_specs=[left, whole((LIVE, width)), left, whole((LIVE, half))],
        out_specs=[pl.BlockSpec((rows, width + half), lambda i: (i, 0)), whole((8, 128))],
        out_shape=[in_hbm((features, width + half), jnp.float32), DONE],
        compiler_params=grant(18),
        cost_estimate=cost(3 * LIVE * features * width, 18),
        name="ffn_grads",
    )(*far_away(out_grad, inner, act, grad_pre))


def more_grads_kernel(act_two_ref, pre_ref, act_one_ref, gq, gk, gv, attn_ref, attended_ref, *refs):
    out_ref = refs[-1]
    half, cols = pre_ref.shape[1], gq.shape[1]
    out_ref[:, 0:half] = outer_sum(act_two_ref[...], pre_ref[...])
    act_one = act_one_ref[...]
    for i, grad_ref in enumerate((gq, gk, gv)):
        out_ref[:, half + cols * i : half + cols * i + cols] = outer_sum(act_one, grad_ref[...])
    out_ref[:, half + 3 * cols :] = outer_sum(attn_ref[...], attended_ref[...])


def more_grads(act_two, grad_pre, act_one, heads, grad_attn, attended, after):
    features, cols = act_two.shape[1], attended.shape[1]
    half = grad_pre.shape[1] // 2
    rows = 512
    left = pl.BlockSpec((LIVE, rows), lambda i: (0, i))
    head = whole((LIVE, cols))
    width = half + 4 * cols
    return pl.pallas_call(
        more_grads_kernel,
        grid=(features // rows,),
        in_specs=[left, pl.BlockSpec((LIVE, half), lambda i: (0, 1)), left]
        + [head] * 3
        + [left, head]
        + [ANYWHERE] * len(after),
        out_specs=pl.BlockSpec((rows, width), lambda i: (i, 0)),
        out_shape=in_hbm((features, width), jnp.float32),
        compiler_params=grant(18),
        cost_estimate=cost(2 * LIVE * features * width, 20),
        name="more_grads",
    )(*far_away(act_two, grad_pre, act_one, *heads, grad_attn, attended), *after)


def vectors_kernel(perm_ref, norm_one_ref, norm_two_ref, heads_ref, up_ref, out_ref):
    lane = iota((8, 128), 1)
    for place in range(16):
        share = perm_ref[place]
        here = pl.ds(pl.multiple_of(share * 128, 128), 128)
        heads = heads_ref[:, pl.ds(pl.multiple_of((share >> 3) * 128, 128), 128)]
        heads = pltpu.roll(heads, 128 - 16 * (share & 7), 1)
        up = up_ref[:, pl.ds(pl.multiple_of((share >> 1) * 128, 128), 128)]
        up = pltpu.roll(up, 64 * (1 - (share & 1)), 1)
        up = jnp.broadcast_to(jnp.sum(up, axis=0, keepdims=True), (8, 128))
        own = jnp.where(lane < 16, heads, jnp.where(lane < 64, 0.0, up))
        out_ref[8 * place : 8 * place + 2, :] = norm_one_ref[0:2, here]
        out_ref[8 * place + 2 : 8 * place + 6, :] = norm_two_ref[0:4, here]
        out_ref[8 * place + 6 : 8 * place + 8, :] = own[0:2, :]


def vectors_of(perm, norm_one, norm_two, heads, up):
    values = (norm_one, norm_two, heads, up)
    return pl.pallas_call(
        vectors_kernel,
        in_specs=[pl.BlockSpec(memory_space=pltpu.SMEM)]
        + [pl.BlockSpec(value.shape, lambda: (0, 0)) for value in values],
        out_specs=pl.BlockSpec((128, 128), lambda: (0, 0)),
        out_shape=jax.ShapeDtypeStruct((128, 128), jnp.float32),
        compiler_params=grant(6),
        cost_estimate=cost(0, 1),
        name="vectors_of",
    )(perm, *values)


def turn_kernel(share_ref, out_ref):
    out_ref[...] = share_ref[...].T


def turn(share, width):
    rows = share.shape[0]
    return pl.pallas_call(
        turn_kernel,
        grid=(1,),
        in_specs=[pl.BlockSpec((rows, width), lambda i: (0, 0))],
        out_specs=whole((width, rows)),
        out_shape=in_hbm((width, rows), jnp.float32),
        compiler_params=grant(6),
        cost_estimate=cost(0, 2),
        name="turn",
    )(*far_away(share))


def deal_kernel(left_ref, right_ref, up_ref, gq, gk, gv, out_ref):
    half, cols = left_ref.shape[1], gq.shape[1]
    up_ref[:, 0:half] = left_ref[...]
    up_ref[:, half:] = right_ref[:, 0:half]
    for i, ref in enumerate((gq, gk, gv)):
        ref[...] = right_ref[:, half + cols * i : half + cols * i + cols]
    out_ref[...] = right_ref[:, half + 3 * cols :].T


def deal(first, second, half, cols):
    rows = first.shape[0]
    shapes = [(rows, 2 * half)] + [(rows, cols)] * 3 + [(cols, rows)]
    return pl.pallas_call(
        deal_kernel,
        grid=(1,),
        in_specs=[
            pl.BlockSpec((rows, half), lambda i: (0, first.shape[1] // half - 1)),
            whole(second.shape),
        ],
        out_specs=[whole(shape) for shape in shapes],
        out_shape=[in_hbm(shape, jnp.float32) for shape in shapes],
        compiler_params=grant(8),
        cost_estimate=cost(0, 3),
        name="deal",
    )(*far_away(first, second))


def spread_kernel(place_ref, tokens_ref, grads_ref, live_ref, *refs):
    for i, (full_ref, out_ref) in enumerate(zip((tokens_ref, grads_ref), refs[-2:])):
        rows = jnp.concatenate(
            [
                ref[64 * part + 32 * i : 64 * part + 32 * i + 32, :]
                for ref in refs[:4]
                for part in range(4)
            ],
            axis=0,
        )
        wide = dot(place_ref[...], rows.astype(jnp.bfloat16)).astype(jnp.bfloat16)
        for first in range(0, wide.shape[1], 128):
            here = slice(first, first + 128)
            out_ref[:, here] = jnp.where(live_ref[...] > 0, wide[:, here], full_ref[:, here])


def spread(place, tokens, grads, live, pieces):
    count, features = tokens.shape
    cols = 512
    block = pl.BlockSpec((count, cols), lambda i: (0, i))
    return pl.pallas_call(
        spread_kernel,
        grid=(features // cols,),
        in_specs=[whole((count, LIVE)), block, block, whole((count, 128))]
        + [pl.BlockSpec((256, cols), lambda i: (0, i))] * 4,
        out_specs=[block] * 2,
        out_shape=[in_hbm(tokens.shape, jnp.bfloat16)] * 2,
        compiler_params=grant(32),
        cost_estimate=cost(4 * count * LIVE * features, 28),
        name="spread",
    )(place, *far_away(tokens, grads), live, *pieces)


def local(
    tokens,
    cotangent,
    lengths,
    exits,
    w_query,
    b_query,
    w_key,
    w_value,
    b_value,
    w_out,
    b_out,
    gain_one,
    shift_one,
    gain_two,
    shift_two,
    w_up,
    b_up,
    w_down,
    b_down,
):
    f32, bf16 = jnp.float32, jnp.bfloat16
    bits = own_bits()
    at_dp = lax.axis_index("dp")
    y_high, z_high = at_dp >> 3, (at_dp >> 1) & 1
    y_gray, z_gray = ((at_dp >> 2) & 1) ^ y_high, (at_dp & 1) ^ z_high
    dp_bits = (y_gray, y_high, z_gray, z_high)

    def direct_place(rank):
        side, one, two = (rank >> 6) & 1, (rank >> 7) & 1, (rank >> 5) & 1
        gray, high = jnp.where(side == 1, two, one), jnp.where(side == 1, one, two)
        distance = (x_place - (2 * high + (gray ^ high))) & 3
        return 256 * ((rank >> 8) ^ bits[0]) + 64 * distance + 32 * side + (rank & 31)

    def dp_blocks(order):
        own = jnp.arange(16, dtype=jnp.int32)
        bits = [None] * 4
        for place, (_, bit) in enumerate(order):
            bits[bit] = ((own >> (3 - place)) & 1) ^ dp_bits[bit]
        return 4 * (2 * bits[1] + (bits[0] ^ bits[1])) + 2 * bits[3] + (bits[2] ^ bits[3])

    perm = dp_blocks(HALVES)

    gain_one_f, gain_two_f = gain_one.astype(f32)[None], gain_two.astype(f32)[None]
    pick, bias, source_low, act_one, normal_low, query, keys, values, attended, logs = front(
        lengths,
        exits,
        tokens,
        gain_one,
        shift_one,
        (w_query, w_key, w_value),
        b_query,
        b_value,
    )

    source_mine = jnp.concatenate([source_low[0:32], source_low[64:96]], axis=0).astype(f32)
    normal_one, scale_one = normed(source_mine)
    scale_one = jnp.broadcast_to(scale_one, (64, 128))
    begun = scatter_begin(both_parts(attended, w_out, False))
    grad_out_low, grad_inner, picked = pick_rows(pick, cotangent, w_down, begun[4:])
    terms_a, terms_b, _ = scatter_end(begun, (picked,))
    hidden_mine, normal_two, normal_a, normal_b, scale_two = norm_two(
        terms_a + [(source_low, 0)], terms_b + [(source_low, 2)], b_out.astype(f32)[None]
    )
    place_all = jnp.arange(tokens.shape[0], dtype=jnp.int32)
    living = exits > LAYER
    below = (place_all[None, :] <= place_all[:, None]) & living[None, :]
    rank = jnp.sum(jnp.where(below, 1, 0), axis=1) - 1
    own_index = jnp.arange(LIVE, dtype=jnp.int32)
    living_column = jnp.broadcast_to(living.astype(bf16)[:, None], (tokens.shape[0], 128))
    row_of = jnp.where(living, own_place(rank, bits), -1)
    place = (row_of[:, None] == own_index[None, :]).astype(bf16)

    shift_two_f, b_up_f = shift_two.astype(f32)[None], b_up.astype(f32)[None]
    weights = (gain_two_f, shift_two_f, w_up, b_up_f, grad_inner)
    begun = []

    def first_piece(piece):
        begun.extend(ffn((0,), (piece,), *weights))
        return begun[3:]

    normal_pieces, _ = gather_rows(normal_a, normal_b, first_piece)
    *begun, sum_up = begun
    *begun, more_up = ffn((1, 2), normal_pieces[1:3], *weights, begun)
    act_two, inner, grad_pre, last_up = ffn((3,), normal_pieces[3:], *weights, begun)
    sum_up = sum_up + more_up + last_up
    first_grads, first_done = ffn_grads(grad_out_low, inner, act_two, grad_pre)
    begun = scatter_begin(both_parts(grad_pre, w_up, True, (first_done,)))
    first_share = lax.psum_scatter(first_grads, "dp", scatter_dimension=0, tiled=True)
    terms_a, terms_b, sent = scatter_end(begun)

    out_pieces = both_parts(inner, w_down, False, sent)
    hidden_a, hidden_b, grad_hidden_mine, sums_two = norm_back(
        terms_a,
        terms_b,
        ((normal_two, 0), (normal_two, 1)),
        ((grad_out_low, 0), (grad_out_low, 2)),
        scale_two,
        gain_two_f,
        out_pieces[0:1],
    )
    hidden_pieces, last_pieces = gather_rows(hidden_a, hidden_b)
    out_begun = scatter_begin(out_pieces, lambda: last_pieces)
    grad_attn_low, grad_query, grad_key, grad_value, sums_heads = attend_back(
        hidden_pieces, w_out, query, keys, values, bias, logs
    )
    heads = (grad_query, grad_key, grad_value)
    *pieces, sums_one = all_parts(heads, (w_query, w_key, w_value), normal_low)

    shares = [vectors_of(perm, sums_one, sums_two, sums_heads, sum_up)]
    for count, (pairs, _) in zip((64, 32, 16, 8), HALVES):
        last = shares[-1]
        shares.append(last[0:count] + over_dp(last[count : 2 * count], pairs))

    out_a, out_b, out_sent = scatter_end(out_begun, (sums_one,))
    second_grads = more_grads(
        act_two, grad_pre, act_one, heads, grad_attn_low, attended, (sums_one, *out_sent)
    )
    begun = scatter_begin(pieces, lambda: (*out_sent, shares[1]))
    second_share = lax.psum_scatter(second_grads, "dp", scatter_dimension=0, tiled=True)
    terms_a, terms_b, _ = scatter_end(begun, (shares[3],))

    _, _, input_mine, _ = norm_back(
        terms_a,
        terms_b,
        ((normal_one, 0), (normal_one, 1)),
        ((grad_hidden_mine, 0), (grad_hidden_mine, 1)),
        scale_one,
        gain_one_f,
        (shares[4],),
    )
    mine = last_rows(out_a, out_b, hidden_mine, b_down.astype(f32)[None], input_mine)
    output_full, input_full = spread(
        place, tokens, cotangent, living_column, gather_rows(*mine)[0]
    )
    share_down = turn(first_share, inner.shape[1])

    own_share = shares[4]
    share_up, *attn_shares = deal(first_share, second_share, inner.shape[1] // 2, attended.shape[1])
    common_share = own_share
    for pairs in (CORE, X_NEAR, X_FAR):
        common_share = common_share + over_tensor(common_share, pairs)
    return (
        output_full,
        input_full,
        attn_shares[0],
        own_share[6, 0:16],
        attn_shares[1],
        attn_shares[2],
        own_share[7, 0:16],
        attn_shares[3],
        common_share[4],
        common_share[0],
        common_share[1],
        common_share[2],
        common_share[3],
        share_up,
        own_share[6, 64:128],
        share_down,
        common_share[5],
    )


def solution(mesh):
    in_specs = (
        P("dp", None),
        P("dp", None),
        P("dp", None),
        P("dp"),
        P(None, "tensor"),
        P("tensor"),
        P(None, "tensor"),
        P(None, "tensor"),
        P("tensor"),
        P("tensor", None),
        P(),
        P(),
        P(),
        P(),
        P(),
        P(None, "tensor"),
        P("tensor"),
        P("tensor", None),
        P(),
    )
    out_specs = (
        P("dp", None),
        P("dp", None),
        P("dp", "tensor"),
        P(("tensor", "dp")),
        P("dp", "tensor"),
        P("dp", "tensor"),
        P(("tensor", "dp")),
        P("tensor", "dp"),
        P("dp"),
        P("dp"),
        P("dp"),
        P("dp"),
        P("dp"),
        P("dp", "tensor"),
        P(("tensor", "dp")),
        P("tensor", "dp"),
        P("dp"),
    )
    return jax.shard_map(local, mesh=mesh, in_specs=in_specs, out_specs=out_specs, check_vma=False)
```
